128 devices in a mesh: dp: 16 (over z_hi, y, core), fsdp: 8 (over z_lo, x).
Axes of the slice: x: 4, y: 4, z: 4 (z_hi: 2, z_lo: 2; z = z_hi * 2 + z_lo), core: 2. Of those that a mesh axis runs over, the one named last changes fastest.
Arguments:
- frames: bfloat16 [98304, 768], P(('dp', 'fsdp')), may hold values from -6 to 6
- upstream: bfloat16 [98304, 768], P(('dp', 'fsdp')), may hold values from -6 to 6
- clip_lengths: int32 [128, 2], P(('dp', 'fsdp')), may hold values from 0 to 768, as said below
- clip_skip: int32 [128, 2], P(('dp', 'fsdp')), may hold values 0 or 1
- query_weight: bfloat16 [768, 768], P(('dp', 'fsdp')), may hold values from -0.21875 to 0.21875
- key_weight: bfloat16 [768, 768], P(('dp', 'fsdp')), may hold values from -0.21875 to 0.21875
- value_weight: bfloat16 [768, 768], P(('dp', 'fsdp')), may hold values from -0.21875 to 0.21875
- output_weight: bfloat16 [768, 768], P(('dp', 'fsdp')), may hold values from -1.75 to 1.75
- query_bias: bfloat16 [768], P(('dp', 'fsdp')), may hold values from -3 to 3
- value_bias: bfloat16 [768], P(('dp', 'fsdp')), may hold values from -3 to 3
- output_bias: bfloat16 [768], P(('dp', 'fsdp')), may hold values from -3 to 3
- first_gain: bfloat16 [768], P(('dp', 'fsdp')), may hold values from 0.5 to 1.5
- first_shift: bfloat16 [768], P(('dp', 'fsdp')), may hold values from -3 to 3
- expand_weight: bfloat16 [768, 3072], P(('dp', 'fsdp')), may hold values from -0.21875 to 0.21875
- shrink_weight: bfloat16 [3072, 768], P(('dp', 'fsdp')), may hold values from -0.109375 to 0.109375
- expand_bias: bfloat16 [3072], P(('dp', 'fsdp')), may hold values from -3 to 3
- shrink_bias: bfloat16 [768], P(('dp', 'fsdp')), may hold values from -3 to 3
- second_gain: bfloat16 [768], P(('dp', 'fsdp')), may hold values from 0.5 to 1.5
- second_shift: bfloat16 [768], P(('dp', 'fsdp')), may hold values from -3 to 3
Outputs:
- encoded: bfloat16 [98304, 768], P(('dp', 'fsdp'))
- frames_gradient: bfloat16 [98304, 768], P(('dp', 'fsdp'))
- query_weight_gradient: float32 [768, 768], P(('dp', 'fsdp'))
- key_weight_gradient: float32 [768, 768], P(('dp', 'fsdp'))
- value_weight_gradient: float32 [768, 768], P(('dp', 'fsdp'))
- output_weight_gradient: float32 [768, 768], P(('dp', 'fsdp'))
- query_bias_gradient: float32 [768], P(('dp', 'fsdp'))
- value_bias_gradient: float32 [768], P(('dp', 'fsdp'))
- output_bias_gradient: float32 [768], P(('dp', 'fsdp'))
- first_gain_gradient: float32 [768], P(('dp', 'fsdp'))
- first_shift_gradient: float32 [768], P(('dp', 'fsdp'))
- expand_weight_gradient: float32 [768, 3072], P(('dp', 'fsdp'))
- shrink_weight_gradient: float32 [3072, 768], P(('dp', 'fsdp'))
- expand_bias_gradient: float32 [3072], P(('dp', 'fsdp'))
- shrink_bias_gradient: float32 [768], P(('dp', 'fsdp'))
- second_gain_gradient: float32 [768], P(('dp', 'fsdp'))
- second_shift_gradient: float32 [768], P(('dp', 'fsdp'))
The draws below stay inside these ranges and needn't reach their ends.
Inputs may be any that keep to these rules, and one draw needn't show every extreme that they name: `clip_lengths`: each row is either one clip of 768 frames followed by 0, or a first clip of 75 to 150 frames followed by a second of 0 to 618 frames. In every draw some device holds a clip of 768 frames and some device a first clip of exactly 150 frames.
All inputs are finite; a program needn't handle non-finite values. No bound on the sum of `clip_skip` on one device may be relied on, other than what follows from the above.
Results may differ from the reference program's by a relative error of at most 0.015.
Values may be sent and summed in bfloat16 or wider, within the bound.
A program may use at most 256 MiB of HBM per device.

```python
import math
import jax
import jax.numpy as jnp
from jax import lax

D = 768
HEADS = 12
HEAD = 64
FF = 3072
ROWS = 768
CLIP = 150
TOKENS = 98304
N_DP = 16
N_FSDP = 8


def draw_clip_lengths(key, part):
    devices = N_DP * N_FSDP
    keys = jax.random.split(jax.random.fold_in(key, 7), 5)
    places = jnp.arange(devices, dtype=jnp.int32)
    longs = jax.random.randint(keys[0], (devices,), 0, 4) == 0
    forced_long = jax.random.randint(keys[1], (), 0, devices)
    forced_short = (forced_long + 1 + jax.random.randint(keys[2], (), 0, devices - 1)) % devices
    longs = (longs | (places == forced_long)) & (places != forced_short)
    first_clip = jax.random.randint(keys[3], (devices,), CLIP // 2, CLIP + 1)
    first_clip = jnp.where(places == forced_short, CLIP, first_clip)
    second_clip = jax.random.randint(keys[4], (devices,), 0, ROWS - CLIP + 1)
    first_clip = jnp.where(longs, ROWS, first_clip)
    second_clip = jnp.where(longs, 0, second_clip)
    return jnp.stack([first_clip, second_clip], axis=1).astype(jnp.int32)


def touch_ends(values, key, least, high):
    shape = values.shape
    index_at = [jax.random.randint(jax.random.fold_in(key, axis), (), 0, shape[axis]) for axis in range(len(shape))]
    values = values.at[tuple(index_at)].set(least)
    longest = shape.index(max(shape))
    index_at[longest] = (index_at[longest] + 1) % shape[longest]
    return values.at[tuple(index_at)].set(high)


def shard_levels(rng, extent, cuts, smallest, high):
    gain = 1.0
    for position, blocks in cuts:
        draws = jax.random.uniform(jax.random.fold_in(jax.random.fold_in(rng, 6), position), (blocks,), jnp.float32, smallest / len(cuts), high / len(cuts))
        gain = gain * jnp.repeat(jnp.exp(draws), extent[position] // blocks).reshape((-1,) + (1,) * (len(extent) - 1 - position))
    return gain


def normal_values(key, shape, width, reach, pieces=(), kind=jnp.bfloat16):
    entries = jax.random.normal(key, shape, jnp.float32) * width
    if len(pieces) > 0:
        entries = shard_levels(key, shape, pieces, -0.22, 0.18) * entries
    return jnp.clip(entries, min=-reach, max=reach).astype(kind)


def setup_inputs(seed: int = 0) -> dict:
    splits = jax.random.split(jax.random.key(seed), 20)
    return {
        "frames": normal_values(splits[0], (TOKENS, D), 1.0, 6.0, ((0, 128),)),
        "upstream": normal_values(splits[1], (TOKENS, D), 1.0, 6.0, ((0, 128),)),
        "clip_lengths": draw_clip_lengths(jax.random.fold_in(splits[19], 71), 0),
        "clip_skip": touch_ends((jax.random.randint(splits[3], (N_DP * N_FSDP, 2), 0, 20) < 1).astype(jnp.int32), jax.random.fold_in(splits[3], 1), 0, 1),
        "query_weight": normal_values(splits[4], (D, D), D ** -0.5, 0.21875, ((0, 128),)),
        "key_weight": normal_values(splits[5], (D, D), D ** -0.5, 0.21875, ((0, 128),)),
        "value_weight": normal_values(splits[6], (D, D), D ** -0.5, 0.21875, ((0, 128),)),
        "output_weight": normal_values(splits[7], (D, D), (D // 64) ** -0.5, 1.75, ((0, 128),)),
        "query_bias": normal_values(splits[8], (D,), 0.5, 3.0, ((0, 128),)),
        "value_bias": normal_values(splits[9], (D,), 0.5, 3.0, ((0, 128),)),
        "output_bias": normal_values(splits[10], (D,), 0.5, 3.0, ((0, 128),)),
        "first_gain": jnp.clip(1.0 + 0.1 * jax.random.normal(splits[11], (D,), jnp.float32), 0.5, 1.5).astype(jnp.bfloat16),
        "first_shift": normal_values(splits[12], (D,), 0.5, 3.0, ((0, 128),)),
        "expand_weight": normal_values(splits[13], (D, FF), D ** -0.5, 0.21875, ((0, 128),)),
        "shrink_weight": normal_values(splits[14], (FF, D), FF ** -0.5, 0.109375, ((0, 128),)),
        "expand_bias": normal_values(splits[15], (FF,), 0.5, 3.0, ((0, 128),)),
        "shrink_bias": normal_values(splits[16], (D,), 0.5, 3.0, ((0, 128),)),
        "second_gain": jnp.clip(1.0 + 0.1 * jax.random.normal(splits[17], (D,), jnp.float32), 0.5, 1.5).astype(jnp.bfloat16),
        "second_shift": normal_values(splits[18], (D,), 0.5, 3.0, ((0, 128),)),
    }


epsilon = 1e-05
masked_score = -1e+30
highest = lax.Precision.HIGHEST

@jax.custom_vjp
def low(v):
    return lax.optimization_barrier(v.astype(jnp.bfloat16)).astype(jnp.float32)

@jax.custom_vjp
def low_back(v):
    return v

def low_keep(v):
    return (low(v), None)

def low_pass(kept, grad):
    return (grad,)

def back_keep(v):
    return (v, None)

def back_low(kept, grad):
    return (low(grad),)
low.defvjp(low_keep, low_pass)
low_back.defvjp(back_keep, back_low)

def live_rows(lengths, skipped, count):
    places = jnp.arange(count, dtype=jnp.int32)
    first_end = lengths[0]
    second_end = lengths[0] + lengths[1]
    segment = jnp.where(places < first_end, 0, jnp.where(places < second_end, 1, 2)).astype(jnp.int32)
    dropped = jnp.where(segment == 0, skipped[0], jnp.where(segment == 1, skipped[1], 1))
    return (segment, dropped == 0)

def layer_norm(values, factor, offset):
    average = lax.optimization_barrier(jnp.mean(values, axis=-1, keepdims=True))
    centered = values - average
    variance = lax.optimization_barrier(jnp.mean(centered * centered, axis=-1, keepdims=True))
    return centered * lax.rsqrt(variance + epsilon) * factor + offset

def matmul(left, right):
    return jnp.dot(left, right, precision=highest)

def attend(queries, keys, values, segment):
    count = queries.shape[0]
    block = count if count <= 1024 else 512
    blocks = count // block
    scale = 1.0 / math.sqrt(HEAD)

    def one_block(item):
        query_block, query_segment = item
        scores = jnp.einsum('qhd,khd->hqk', query_block, keys, precision=highest) * scale
        allowed = query_segment[:, None] == segment[None, :]
        scores = low_back(jnp.where(allowed[None], scores, masked_score))
        largest = lax.optimization_barrier(jnp.max(scores, axis=-1, keepdims=True))
        raised = jnp.exp(scores - largest)
        denominator = lax.optimization_barrier(jnp.sum(raised, axis=-1, keepdims=True))
        probs = low(raised / denominator)
        return jnp.einsum('hqk,khd->qhd', probs, values, precision=highest)
    outputs = lax.map(jax.checkpoint(one_block), (queries.reshape(blocks, block, HEADS, HEAD), segment.reshape(blocks, block)))
    return outputs.reshape(count, HEADS * HEAD)

def forward(params, frames, segment, live):
    query_weight, key_weight, value_weight, output_weight, query_bias, value_bias, output_bias, first_gain, first_shift, expand_weight, shrink_weight, expand_bias, shrink_bias, second_gain, second_shift = params
    count = frames.shape[0]
    head_shape = (count, HEADS, HEAD)
    inputs = low(frames)
    queries = low(low_back(matmul(inputs, query_weight) + query_bias))
    keys = low(low_back(matmul(inputs, key_weight)))
    values = low(low_back(matmul(inputs, value_weight) + value_bias))
    context = low(low_back(attend(queries.reshape(head_shape), keys.reshape(head_shape), values.reshape(head_shape), segment)))
    branch = low_back(matmul(context, output_weight) + output_bias)
    hidden = layer_norm(frames + branch, first_gain, first_shift)
    expanded = low_back(matmul(low(hidden), expand_weight) + expand_bias)
    activated = low(jax.nn.gelu(expanded, approximate=False))
    shrunk = low_back(matmul(activated, shrink_weight) + shrink_bias)
    result = layer_norm(hidden + shrunk, second_gain, second_shift)
    return jnp.where(live[:, None], result, frames)

def reference(frames, upstream, clip_lengths, clip_skip, query_weight, key_weight, value_weight, output_weight, query_bias, value_bias, output_bias, first_gain, first_shift, expand_weight, shrink_weight, expand_bias, shrink_bias, second_gain, second_shift):
    params = tuple((weight.astype(jnp.float32) for weight in (query_weight, key_weight, value_weight, output_weight, query_bias, value_bias, output_bias, first_gain, first_shift, expand_weight, shrink_weight, expand_bias, shrink_bias, second_gain, second_shift)))
    devices = N_DP * N_FSDP
    framed = frames.reshape(devices, ROWS, D)
    upper = upstream.reshape(devices, ROWS, D)

    def step(carry, item):
        block_frames, block_upstream, lengths, skipped = item
        segment, live = live_rows(lengths, skipped, ROWS)

        def local(weights, inputs):
            return forward(weights, inputs, segment, live)
        outputs, pullback = jax.vjp(local, params, block_frames.astype(jnp.float32))
        param_grads, input_grad = pullback(block_upstream.astype(jnp.float32))
        carry = jax.tree.map(jnp.add, carry, param_grads)
        return (carry, (outputs.astype(jnp.bfloat16), input_grad.astype(jnp.bfloat16)))
    zeros = tuple((jnp.zeros_like(weight) for weight in params))
    sums, (encoded, gradient) = lax.scan(step, zeros, (framed, upper, clip_lengths, clip_skip))
    return (encoded.reshape(TOKENS, D), gradient.reshape(TOKENS, D), sums[0], sums[1], sums[2], sums[3], sums[4], sums[5], sums[6], sums[7], sums[8], sums[9], sums[10], sums[11], sums[12], sums[13], sums[14])
```

```python
import functools
import math

import jax
import jax.numpy as jnp
import numpy as np
from jax import lax
from jax.experimental import pallas as pl
from jax.experimental.pallas import tpu as pltpu
from jax.sharding import PartitionSpec as P

epsilon = 1e-05

SCALE = 0.125
EXCLUDED = -1e30
F32 = jnp.float32
BF16 = jnp.bfloat16
WHOLE = pl.BlockSpec(memory_space=pltpu.VMEM)
SCALARS = pl.BlockSpec(memory_space=pltpu.SMEM)
ANYWHERE = pl.BlockSpec(memory_space=pl.ANY)
VEC_QUERY, VEC_VALUE, VEC_OUTPUT, VEC_GAIN1, VEC_SHIFT1, VEC_SHRINK, VEC_GAIN2, VEC_SHIFT2, VEC_EXPAND = range(9)


def dot(left, right, a=1, b=0):
    return lax.dot_general(left, right, (((a,), (b,)), ((), ())), preferred_element_type=F32)


def shape(*sizes, kind=jnp.bfloat16):
    return jax.ShapeDtypeStruct(sizes, kind)


def segments(lengths_ref, axis, extent, first=0):
    place = lax.broadcasted_iota(jnp.int32, extent, axis) + first
    first_end = lengths_ref[0, 0]
    second_end = first_end + lengths_ref[0, 1]
    return jnp.where(place < first_end, 0, jnp.where(place < second_end, 1, 2))


def live_mask(lengths_ref, skip_ref, extent, first):
    segment = segments(lengths_ref, 0, extent, first)
    dropped = jnp.where(segment == 0, skip_ref[0, 0], jnp.where(segment == 1, skip_ref[0, 1], 1))
    return dropped == 0


def vector(ref, number):
    return ref[0:1, 768 * number : 768 * (number + 1)]


def head_rows(head):
    return pl.ds(pl.multiple_of(head * 64, 64), 64)


def pair_lanes(pair):
    return pl.ds(pl.multiple_of(pair * 128, 128), 128)


def project(frames, attend, vectors, q_n, k_n, v_n, q_t, k_t, v_t):
    x = frames[...]
    q_n[...] = ((dot(x, attend[0]) + vector(vectors, VEC_QUERY)) * SCALE).astype(BF16)
    q_t[...] = q_n[...].T
    k_n[...] = dot(x, attend[1]).astype(BF16)
    k_t[...] = k_n[...].T
    v_n[...] = (dot(x, attend[2]) + vector(vectors, VEC_VALUE)).astype(BF16)
    v_t[...] = v_n[...].T


def mask_operands(lengths_ref, right, k_mask):
    lane = lax.broadcasted_iota(jnp.int32, (768, 128), 1)
    k_mask[...] = jnp.where(lane == segments(lengths_ref, 0, (768, 128)), 1.0, 0.0).astype(BF16)
    row = lax.broadcasted_iota(jnp.int32, (128, 768), 0)
    other = (row < 3) & (row != segments(lengths_ref, 1, (128, 768)))
    other = jnp.where(other, EXCLUDED, 0.0).astype(BF16)
    for side in range(2):
        right[side, 128:256] = other
        right[side, 64 * (1 - side) : 64 * (1 - side) + 64] = jnp.zeros((64, 768), BF16)


def score_stage(pair, side, q_t, k_n, k_mask, right, scores, tops):
    left = jnp.concatenate([k_n[:, pair_lanes(pair)], k_mask[...]], axis=1)
    right[side, 64 * side : 64 * side + 64] = q_t[head_rows(pair * 2 + side), :]
    values = dot(left, right[side])
    scores[side] = values
    tops[side] = jnp.broadcast_to(jnp.max(values, axis=0, keepdims=True), (8, 768))


def prob_stage(pair, side, v_t, scores, tops, probs, inverse, ctx_t):
    head = pair * 2 + side
    rows = head_rows(head)
    left = jnp.concatenate([v_t[rows, :], jnp.ones((16, 768), BF16)], axis=0)
    raised = jnp.exp(scores[side] - tops[side, 0:1]).astype(BF16)
    probs[head] = raised
    total = dot(left, raised)
    factor = 1.0 / total[64:65]
    inverse[pl.ds(pl.multiple_of(head * 8, 8), 8), :] = jnp.broadcast_to(factor, (8, 768))
    ctx_t[rows, :] = (total[:64] * factor).astype(BF16)


def attend_kernel(
    lengths_ref, frames, attend, vectors, q_n, k_t, v_n, ctx_t, inverse, probs,
    k_n, v_t, q_t, right, k_mask, scores, tops,
):
    project(frames, attend, vectors, q_n, k_n, v_n, q_t, k_t, v_t)
    mask_operands(lengths_ref, right, k_mask)
    score_stage(0, 0, q_t, k_n, k_mask, right, scores, tops)

    def body(pair, carry):
        score_stage(pair, 1, q_t, k_n, k_mask, right, scores, tops)
        prob_stage(pair, 0, v_t, scores, tops, probs, inverse, ctx_t)
        score_stage(jnp.minimum(pair + 1, 5), 0, q_t, k_n, k_mask, right, scores, tops)
        prob_stage(pair, 1, v_t, scores, tops, probs, inverse, ctx_t)
        return carry

    lax.fori_loop(0, 6, body, 0)


def attend_call(lengths, frames, attend, vectors):
    return pl.pallas_call(
        attend_kernel,
        out_shape=(
            shape(768, 768), shape(768, 768), shape(768, 768), shape(768, 768), shape(96, 768, kind=F32), shape(12, 768, 768),
        ),
        in_specs=[SCALARS] + [WHOLE] * 3,
        out_specs=[WHOLE] * 6,
        scratch_shapes=[pltpu.VMEM((768, 768), BF16)] * 3
        + [
            pltpu.VMEM((2, 256, 768), BF16), pltpu.VMEM((768, 128), BF16),
            pltpu.VMEM((2, 768, 768), F32), pltpu.VMEM((2, 8, 768), F32),
        ],
        compiler_params=pltpu.CompilerParams(vmem_limit_bytes=58 * 2**20),
        name="attend",
    )(lengths, frames, attend, vectors)


def gelu_pair(v):
    x = jnp.abs(v) * (1.0 / math.sqrt(2.0))
    t = 1.0 / (1.0 + 0.3275911 * x)
    e = jnp.exp(-(x * x))
    poly = t * (0.254829592 + t * (-0.284496736 + t * (1.421413741 + t * (-1.453152027 + t * 1.061405429))))
    tail = 0.5 * poly * e
    phi = jnp.where(v >= 0, 1.0 - tail, tail)
    return v * phi, phi + v * e * (1.0 / math.sqrt(2.0 * math.pi))


def normalise(values):
    centered = values - jnp.mean(values, axis=-1, keepdims=True)
    scale = lax.rsqrt(jnp.mean(centered * centered, axis=-1, keepdims=True) + epsilon)
    return centered * scale, scale


def norm_back(cotangent, gain, normed, scale):
    c = cotangent * gain
    return scale * (
        c - jnp.mean(c, axis=-1, keepdims=True) - normed * jnp.mean(c * normed, axis=-1, keepdims=True)
    )


def feed_kernel(
    lengths_ref, skip_ref, frames, upstream, ctx_t, output_weight, expand, shrink, vectors,
    encoded, residual_grad, branch_grad, output_out, expand_out, shrink_out, vector_out,
    normed, scales, hidden, act, slope, acc, raw, summed_grad,
):
    def rows_of(block):
        return slice(256 * block, 256 * (block + 1))

    def wide_columns(chunk):
        return slice(768 * chunk, 768 * (chunk + 1))

    for block in range(3):
        rows = rows_of(block)
        values = (
            dot(ctx_t[:, rows], output_weight[...], 0, 0) + frames[rows, :].astype(F32) + vector(vectors, VEC_OUTPUT)
        )
        unit, scale = normalise(values)
        normed[rows, :] = unit
        scales[rows, :] = jnp.broadcast_to(scale, (256, 128))
        hidden[rows, :] = (unit * vector(vectors, VEC_GAIN1) + vector(vectors, VEC_SHIFT1)).astype(BF16)

    def expand_stage(chunk):
        raw[chunk % 2] = dot(hidden[...], expand[:, wide_columns(chunk)])

    def gelu_stage(chunk):
        columns = wide_columns(chunk)
        value, derivative = gelu_pair(raw[chunk % 2] + vector(vectors, VEC_EXPAND + chunk))
        act[:, columns] = value.astype(BF16)
        slope[:, columns] = derivative.astype(BF16)

    def shrink_stage(chunk):
        columns = wide_columns(chunk)
        product = dot(act[:, columns], shrink[columns, :])
        if chunk == 0:
            acc[...] = product
        else:
            acc[...] = acc[...] + product

    expand_stage(0)
    for chunk in range(4):
        if chunk < 3:
            expand_stage(chunk + 1)
        gelu_stage(chunk)
        if chunk > 0:
            shrink_stage(chunk - 1)
    shrink_stage(3)

    sums = [jnp.zeros((1, 768), F32) for _ in range(3)]
    for block in range(3):
        rows = rows_of(block)
        first = normed[rows, :] * vector(vectors, VEC_GAIN1) + vector(vectors, VEC_SHIFT1)
        unit, scale = normalise(first + acc[rows, :] + vector(vectors, VEC_SHRINK))
        result = unit * vector(vectors, VEC_GAIN2) + vector(vectors, VEC_SHIFT2)
        live = live_mask(lengths_ref, skip_ref, (256, 1), 256 * block)
        encoded[rows, :] = jnp.where(live, result, frames[rows, :].astype(F32)).astype(BF16)
        cotangent = jnp.where(live, upstream[rows, :].astype(F32), 0.0)
        grad = norm_back(cotangent, vector(vectors, VEC_GAIN2), unit, scale)
        acc[rows, :] = grad
        summed_grad[rows, :] = grad.astype(BF16)
        sums[0] = sums[0] + jnp.sum(cotangent * unit, axis=0, keepdims=True)
        sums[1] = sums[1] + jnp.sum(cotangent, axis=0, keepdims=True)
        sums[2] = sums[2] + jnp.sum(grad, axis=0, keepdims=True)

    def put(number, value):
        vector_out[0:1, 768 * number : 768 * (number + 1)] = value

    put(VEC_QUERY, jnp.zeros((1, 768), F32))
    put(VEC_VALUE, jnp.zeros((1, 768), F32))
    put(VEC_GAIN2, sums[0])
    put(VEC_SHIFT2, sums[1])
    put(VEC_SHRINK, sums[2])

    for chunk in range(4):
        columns = wide_columns(chunk)
        grad = dot(summed_grad[...], shrink[columns, :], 1, 1) * slope[:, columns].astype(F32)
        put(VEC_EXPAND + chunk, jnp.sum(grad, axis=0, keepdims=True))
        slope[:, columns] = grad.astype(BF16)
        shrink_out[columns, :] = dot(act[:, columns], summed_grad[...], 0, 0).astype(BF16)
    for chunk in range(4):
        columns = wide_columns(chunk)
        acc[...] = acc[...] + dot(slope[:, columns], expand[:, columns], 1, 1)
        expand_out[:, columns] = dot(hidden[...], slope[:, columns], 0, 0).astype(BF16)
    sums = [jnp.zeros((1, 768), F32) for _ in range(3)]
    for block in range(3):
        rows = rows_of(block)
        grad = acc[rows, :]
        unit = normed[rows, :]
        back = norm_back(grad, vector(vectors, VEC_GAIN1), unit, scales[rows, 0:1])
        residual_grad[rows, :] = back
        branch_grad[rows, :] = back.astype(BF16)
        sums[0] = sums[0] + jnp.sum(grad * unit, axis=0, keepdims=True)
        sums[1] = sums[1] + jnp.sum(grad, axis=0, keepdims=True)
        sums[2] = sums[2] + jnp.sum(back, axis=0, keepdims=True)
    put(VEC_GAIN1, sums[0])
    put(VEC_SHIFT1, sums[1])
    put(VEC_OUTPUT, sums[2])
    output_out[...] = dot(ctx_t[...], branch_grad[...]).astype(BF16)


def feed_call(lengths, skip, frames, upstream, ctx_t, output_weight, expand, shrink, vectors):
    return pl.pallas_call(
        feed_kernel,
        out_shape=(
            shape(768, 768), shape(768, 768, kind=F32), shape(768, 768), shape(768, 768), shape(768, 3072), shape(3072, 768),
            shape(1, VECTORS * 768, kind=F32),
        ),
        in_specs=[SCALARS] * 2 + [WHOLE] * 7,
        out_specs=[WHOLE] * 7,
        scratch_shapes=[
            pltpu.VMEM((768, 768), F32), pltpu.VMEM((768, 128), F32), pltpu.VMEM((768, 768), BF16),
            pltpu.VMEM((768, 3072), BF16), pltpu.VMEM((768, 3072), BF16), pltpu.VMEM((768, 768), F32),
            pltpu.VMEM((2, 768, 768), F32), pltpu.VMEM((768, 768), BF16),
        ],
        compiler_params=pltpu.CompilerParams(vmem_limit_bytes=60 * 2**20),
        name="feed",
    )(lengths, skip, frames, upstream, ctx_t, output_weight, expand, shrink, vectors)


def back_kernel(
    lengths_ref, skip_ref, frames, upstream, q_n, k_t, v_n, ctx_t, inverse, probs, branch_grad, residual_grad, attend, output_weight,
    frames_grad, query_out, key_out, value_out, vector_out,
    ctx_grad, scaled_t, right, ones_mask, score_grad, dk_n, dq_t, dv_t,
):
    ctx_grad[...] = dot(output_weight[...], branch_grad[...], 1, 1)
    lane = lax.broadcasted_iota(jnp.int32, (768, 128), 1)
    ones_mask[...] = jnp.where(lane < 2, 1.0, 0.0).astype(BF16)
    for side in range(2):
        right[side] = jnp.zeros((256, 768), BF16)

    def score_stage(pair, side):
        head = pair * 2 + side
        rows = head_rows(head)
        factor = inverse[pl.ds(pl.multiple_of(head * 8, 8), 8), :][0:1]
        scaled = (ctx_grad[rows, :] * factor).astype(BF16)
        scaled_t[rows, :] = scaled
        right[side, 64 * side : 64 * side + 64] = scaled
        inner = jnp.sum(scaled.astype(F32) * ctx_t[rows, :].astype(F32), axis=0, keepdims=True)
        high = inner.astype(BF16).astype(F32)
        row = lax.broadcasted_iota(jnp.int32, (16, 768), 0)
        right[side, 128:144] = jnp.where(row == 0, -high, jnp.where(row == 1, high - inner, 0.0)).astype(BF16)
        left = jnp.concatenate([v_n[:, pair_lanes(pair)], ones_mask[...]], axis=1)
        score_grad[side] = (dot(left, right[side]) * probs[head].astype(F32)).astype(BF16)

    def use_stage(pair, side):
        head = pair * 2 + side
        rows = head_rows(head)
        lanes = pair_lanes(pair)
        dv_t[rows, :] = dot(scaled_t[rows, :], probs[head], 1, 1).astype(BF16)
        dq_t[rows, :] = (dot(k_t[rows, :], score_grad[side]) * SCALE).astype(BF16)
        keys = dot(score_grad[side], q_n[:, lanes]).astype(BF16)
        if side == 1:
            keys = jnp.where(lax.broadcasted_iota(jnp.int32, (768, 128), 1) < 64, dk_n[:, lanes], keys)
        dk_n[:, lanes] = keys

    score_stage(0, 0)

    def body(pair, carry):
        score_stage(pair, 1)
        use_stage(pair, 0)
        score_stage(jnp.minimum(pair + 1, 5), 0)
        use_stage(pair, 1)
        return carry

    lax.fori_loop(0, 6, body, 0)
    x = frames[...]
    queries, keys, values = dq_t[...].T, dk_n[...], dv_t[...].T
    query_out[...] = dot(x, queries, 0, 0).astype(BF16)
    key_out[...] = dot(x, keys, 0, 0).astype(BF16)
    value_out[...] = dot(x, values, 0, 0).astype(BF16)
    vector_out[0:1, 0:768] = jnp.sum(queries.astype(F32), axis=0, keepdims=True)
    vector_out[0:1, 768:1536] = jnp.sum(values.astype(F32), axis=0, keepdims=True)
    total = residual_grad[...] + dot(queries, attend[0], 1, 1) + dot(keys, attend[1], 1, 1) + dot(values, attend[2], 1, 1)
    live = live_mask(lengths_ref, skip_ref, (768, 1), 0)
    frames_grad[...] = jnp.where(live, total, upstream[...].astype(F32)).astype(BF16)


def back_call(*args):
    return pl.pallas_call(
        back_kernel,
        out_shape=(shape(768, 768),) * 4 + (shape(1, 2 * 768, kind=F32),),
        in_specs=[SCALARS] * 2 + [WHOLE] * 12,
        out_specs=[WHOLE] * 5,
        scratch_shapes=[
            pltpu.VMEM((768, 768), F32), pltpu.VMEM((768, 768), BF16), pltpu.VMEM((2, 256, 768), BF16),
            pltpu.VMEM((768, 128), BF16), pltpu.VMEM((2, 768, 768), BF16), pltpu.VMEM((768, 768), BF16),
            pltpu.VMEM((768, 768), BF16), pltpu.VMEM((768, 768), BF16),
        ],
        compiler_params=pltpu.CompilerParams(vmem_limit_bytes=60 * 2**20),
        name="back",
    )(*args)


MESH = pl.DeviceIdType.MESH
ROWS_A = 32
ROWS_F = 48
ROWS_ALL = ROWS_A + ROWS_F
LANES = 256
PARTS = 3
VECTORS = 12
BIAS_OUT = 208


def attention_rows():
    table = np.zeros((BIAS_OUT, 8 * ROWS_A), np.float32)
    for row in range(192):
        matrix, inner = divmod(row, 48)
        device, lane = divmod(inner, 6)
        table[row, device * ROWS_A + 6 * matrix + lane] = 1
    for device in range(8):
        table[192 + device, device * ROWS_A + 24] = 1
    return table


def feed_rows():
    table = np.zeros((384, 8 * ROWS_F), np.float32)
    for row in range(192):
        matrix, inner = divmod(row, 48)
        device, lane = divmod(inner, 6)
        table[row, device * ROWS_F + 6 * matrix + lane] = 1
    for row in range(192):
        device, lane = divmod(row, 24)
        table[192 + row, device * ROWS_F + 24 + lane] = 1
    return table


def vector_lanes():
    table = np.zeros((128, VECTORS * 768), np.float32)
    for column in range(8 * 768):
        vector, place = divmod(column, 768)
        table[6 * vector + place % 6, column] = 1
    for column in range(3072):
        table[48 + column % 24, 8 * 768 + column] = 1
    return table


def owner_mask(first, wide):
    device = lax.broadcasted_iota(jnp.int32, (128, 768), 0)
    column = lax.broadcasted_iota(jnp.int32, (128, 768), 1) + first
    low = device * wide
    return (column >= low) & (column < low + wide)


def position():
    dp = lax.axis_index("dp")
    fsdp = lax.axis_index("fsdp")
    core = lax.rem(dp, 2)
    y = lax.rem(dp // 2, 4)
    z = (dp // 8) * 2 + fsdp // 4
    x = lax.rem(fsdp, 4)
    return x, y, z, core


def device_of(x, y, z, core):
    return (((z // 2) * 4 + y) * 2 + core, lax.rem(z, 2) * 4 + x)


AXES = ((0, 1, 2), (1, 2, 0), (2, 0, 1))


class Place:
    def __init__(self):
        self.at = position()

    def along(self, part, stage):
        return self.at[AXES[part][stage]]

    def peer(self, part, stage, step):
        where = list(self.at)
        axis = AXES[part][stage]
        where[axis] = lax.rem(where[axis] + step, 4)
        return device_of(*where)

    def sibling(self):
        x, y, z, core = self.at
        return device_of(x, y, z, 1 - core)


def meet(place):
    barrier = pltpu.get_barrier_semaphore()
    targets = [place.sibling()]
    for axis in range(3):
        for step in (1, 2, 3):
            where = list(place.at)
            where[axis] = lax.rem(where[axis] + step, 4)
            targets.append(device_of(*where))
    for target in targets:
        pl.semaphore_signal(barrier, inc=1, device_id=target, device_id_type=MESH)
    pl.semaphore_wait(barrier, len(targets))


def remote(source, target, send, receive, device):
    return pltpu.make_async_remote_copy(
        src_ref=source,
        dst_ref=target,
        send_sem=send,
        recv_sem=receive,
        device_id=device,
        device_id_type=MESH,
    )


def chunk_blocks(held, part, dp):
    high, y, core = dp // 8, lax.rem(dp // 2, 4), lax.rem(dp, 2)
    blocks = []
    for low in range(2):
        for x in range(4):
            where = (x, y, high * 2 + low)
            first, second, third = (where[a] for a in AXES[part])
            blocks.append((part, core, third, second, first))
    return blocks


def gather_kernel(
    query_in, key_in, value_in, output_in, expand_in, shrink_in, lanes_in, rows_a_ref, rows_f_ref, lanes_ref,
    attend_ref, output_ref, expand_ref, shrink_ref, vector_ref, held, block_ref, spread, send, recv,
):
    place = Place()
    for number, source in enumerate((query_in, key_in, value_in, output_in)):
        block_ref[6 * number : 6 * number + 6, :] = source[...].astype(F32)
    block_ref[24:32, :] = jnp.zeros((8, 768), F32)
    block_ref[24:25, 0:128] = lanes_in[...]
    for number in range(4):
        block_ref[32 + 6 * number : 38 + 6 * number, :] = expand_in[:, 768 * number : 768 * (number + 1)].astype(F32)
    block_ref[56:80, :] = shrink_in[...].astype(F32)
    core = place.at[3]
    mine = [(place.along(p, 2), place.along(p, 1), place.along(p, 0)) for p in range(PARTS)]
    for part in range(PARTS):
        third, second, first = mine[part]
        held[part, core, third, second, first] = block_ref[:, LANES * part : LANES * (part + 1)].astype(BF16)
    meet(place)

    def copy(part, number, view, device):
        return remote(view, view, send.at[part, number], recv.at[part, number], device)

    pending = []

    def start(*args):
        item = copy(*args)
        item.start()
        pending.append(item)

    def arrived(part, number, view):
        copy(part, number, view, place.sibling()).wait_recv()

    for part in range(PARTS):
        third, second, first = mine[part]
        for step in (1, 3, 2):
            start(part, step - 1, held.at[part, core, third, second, first], place.peer(part, 0, step))
    for part in range(PARTS):
        third, second, first = mine[part]
        for step in (1, 3, 2):
            arrived(part, step - 1, held.at[part, core, third, second, lax.rem(first + 4 - step, 4)])
        for step in (1, 3, 2):
            start(part, 2 + step, held.at[part, core, third, second], place.peer(part, 1, step))
    for part in range(PARTS):
        third, second, first = mine[part]
        for step in (1, 3, 2):
            arrived(part, 2 + step, held.at[part, core, third, lax.rem(second + 4 - step, 4)])
        ahead, behind = place.peer(part, 2, 1), place.peer(part, 2, 3)
        for half in (0, 1):
            start(part, 6 + half, held.at[part, core, third, pl.ds(2 * half, 2)], ahead)
            start(part, 9 - half, held.at[part, core, third, pl.ds(2 * (1 - half), 2)], behind)
        start(part, 12, held.at[part, core, third], place.sibling())
    for half in (0, 1):
        for part in range(PARTS):
            third, second, first = mine[part]
            ahead, behind = place.peer(part, 2, 1), place.peer(part, 2, 3)
            from_behind = held.at[part, core, lax.rem(third + 3, 4), pl.ds(2 * half, 2)]
            from_ahead = held.at[part, core, lax.rem(third + 1, 4), pl.ds(2 * (1 - half), 2)]
            arrived(part, 6 + half, from_behind)
            if half == 0:
                start(part, 10, from_behind, ahead)
            start(part, 13 + half, from_behind, place.sibling())
            arrived(part, 9 - half, from_ahead)
            if half == 0:
                start(part, 11, from_ahead, behind)
            start(part, 15 + half, from_ahead, place.sibling())
    for part in range(PARTS):
        third, second, first = mine[part]
        opposite = lax.rem(third + 2, 4)
        arrived(part, 10, held.at[part, core, opposite, pl.ds(0, 2)])
        start(part, 17, held.at[part, core, opposite, pl.ds(0, 2)], place.sibling())
        arrived(part, 11, held.at[part, core, opposite, pl.ds(2, 2)])
        start(part, 18, held.at[part, core, opposite, pl.ds(2, 2)], place.sibling())
    for part in range(PARTS):
        third, second, first = mine[part]
        other = 1 - core
        opposite = lax.rem(third + 2, 4)
        arrived(part, 12, held.at[part, other, third])
        for half in (0, 1):
            arrived(part, 13 + half, held.at[part, other, lax.rem(third + 3, 4), pl.ds(2 * half, 2)])
            arrived(part, 15 + half, held.at[part, other, lax.rem(third + 1, 4), pl.ds(2 * (1 - half), 2)])
            arrived(part, 17 + half, held.at[part, other, opposite, pl.ds(2 * half, 2)])

    def unpack(dp, carry):
        for part in range(PARTS):
            columns = slice(LANES * part, LANES * (part + 1))
            blocks = [held[index] for index in chunk_blocks(held, part, dp)]
            first = jnp.concatenate([b[:ROWS_A] for b in blocks], axis=0)
            second = jnp.concatenate([b[ROWS_A:] for b in blocks], axis=0)
            first = dot(rows_a_ref[...], first).astype(jnp.bfloat16)
            second = dot(rows_f_ref[...], second).astype(jnp.bfloat16)
            rows = pl.ds(pl.multiple_of(dp * 48, 16), 48)
            for matrix in range(4):
                piece = first[48 * matrix : 48 * (matrix + 1)]
                if matrix < 3:
                    attend_ref[matrix, rows, columns] = piece
                else:
                    output_ref[rows, columns] = piece
                expand_ref[rows, 768 * matrix + LANES * part : 768 * matrix + LANES * (part + 1)] = second[
                    48 * matrix : 48 * (matrix + 1)
                ]
            shrink_ref[pl.ds(pl.multiple_of(dp * 192, 16), 192), columns] = second[192:]
            if part == 0:
                spread[pl.ds(pl.multiple_of(dp * 8, 8), 8), :] = first[192:200, :128].astype(jnp.float32)
        return carry

    lax.fori_loop(0, 16, unpack, 0)
    vectors = spread[...].astype(jnp.bfloat16)
    for vector in range(VECTORS):
        wide = 6 if vector < 8 else 24
        mask = owner_mask(0 if vector < 8 else 768 * (vector - 8), wide)
        columns = slice(768 * vector, 768 * (vector + 1))
        whole = dot(vectors, lanes_ref[:, columns])
        vector_ref[:, columns] = jnp.sum(jnp.where(mask, whole, 0.0), axis=0, keepdims=True)
    for item in pending:
        item.wait_send()


def gather(*shards):
    shapes = (
        jax.ShapeDtypeStruct((3, 768, 768), jnp.bfloat16),
        jax.ShapeDtypeStruct((768, 768), jnp.bfloat16),
        jax.ShapeDtypeStruct((768, 3072), jnp.bfloat16),
        jax.ShapeDtypeStruct((3072, 768), jnp.bfloat16),
        jax.ShapeDtypeStruct((1, VECTORS * 768), jnp.float32),
    )
    whole = pl.BlockSpec(memory_space=pltpu.VMEM)
    return pl.pallas_call(
        gather_kernel,
        out_shape=shapes,
        in_specs=[whole] * 10,
        out_specs=[whole] * 5,
        scratch_shapes=[
            pltpu.VMEM((PARTS, 2, 4, 4, 4, ROWS_ALL, LANES), jnp.bfloat16),
            pltpu.VMEM((ROWS_ALL, 768), F32),
            pltpu.VMEM((128, 128), jnp.float32),
            pltpu.SemaphoreType.DMA((PARTS, 19)),
            pltpu.SemaphoreType.DMA((PARTS, 19)),
        ],
        compiler_params=pltpu.CompilerParams(
            collective_id=0, has_side_effects=True, vmem_limit_bytes=56 * 2**20
        ),
        name="gather",
    )(
        *shards,
        jnp.asarray(attention_rows(), jnp.bfloat16),
        jnp.asarray(feed_rows(), jnp.bfloat16),
        jnp.asarray(vector_lanes(), jnp.bfloat16),
    )


def scatter_kernel(
    query_ref, key_ref, value_ref, output_ref, expand_ref, shrink_ref, first_vector_ref, vector_ref,
    rows_a_ref, rows_f_ref, lanes_ref,
    query_out, key_out, value_out, output_out, expand_out, shrink_out, lanes_out,
    out_ref, held, from_core, from_far, from_near, from_second, from_first, spread, send, recv,
):
    place = Place()
    core = place.at[3]
    other = 1 - core
    mine = [(place.along(p, 2), place.along(p, 1), place.along(p, 0)) for p in range(PARTS)]
    bf16 = jnp.bfloat16

    packed = jnp.zeros((128, 128), jnp.float32)
    for vector in range(VECTORS):
        wide = 6 if vector < 8 else 24
        mask = owner_mask(0 if vector < 8 else 768 * (vector - 8), wide)
        columns = slice(768 * vector, 768 * (vector + 1))
        source = first_vector_ref if vector < 2 else vector_ref
        whole = jnp.where(mask, source[:, columns], 0.0).astype(bf16)
        packed = packed + dot(whole, lanes_ref[:, columns], 1, 1)
    spread[...] = packed

    def pack(half, which):
        def body(number, carry):
            dp = number * 2 + which
            rows = pl.ds(pl.multiple_of(dp * 48, 16), 48)
            for part in range(PARTS):
                columns = slice(LANES * part, LANES * (part + 1))
                pieces = [ref[rows, columns] for ref in (query_ref, key_ref, value_ref, output_ref)]
                if part == 0:
                    tail = spread[pl.ds(pl.multiple_of(dp * 8, 8), 8), :]
                    tail = jnp.concatenate([tail, jnp.zeros((8, 128), jnp.float32)], axis=0)
                    tail = jnp.concatenate([tail, jnp.zeros((16, 128), jnp.float32)], axis=1)
                else:
                    tail = jnp.zeros((16, LANES), jnp.float32)
                first = jnp.concatenate(pieces + [tail.astype(bf16)], axis=0)
                first = dot(rows_a_ref[...], first, 0, 0).astype(bf16)
                pieces = [
                    expand_ref[rows, 768 * matrix + LANES * part : 768 * matrix + LANES * (part + 1)]
                    for matrix in range(4)
                ]
                pieces.append(shrink_ref[pl.ds(pl.multiple_of(dp * 192, 16), 192), columns])
                second = dot(rows_f_ref[...], jnp.concatenate(pieces, axis=0), 0, 0).astype(bf16)
                for device, index in enumerate(chunk_blocks(held, part, dp)):
                    held[index] = jnp.concatenate(
                        [
                            first[ROWS_A * device : ROWS_A * (device + 1)],
                            second[ROWS_F * device : ROWS_F * (device + 1)],
                        ],
                        axis=0,
                    )
            return carry

        lax.fori_loop(0, 8, body, 0)

    meet(place)
    pending = []

    def start(part, number, source, target, device):
        item = remote(source, target, send.at[part, number], recv.at[part, number], device)
        item.start()
        pending.append(item)

    def arrived(part, number, view):
        remote(view, view, send.at[part, number], recv.at[part, number], place.sibling()).wait_recv()

    def accumulate(target, sources, count):
        def body(number, carry):
            for inner in range(4):
                total = target[number, inner].astype(jnp.float32)
                for source in sources:
                    total = total + source[number, inner].astype(jnp.float32)
                target[number, inner] = total.astype(bf16)
            return carry

        lax.fori_loop(0, count, body, 0)

    pack(0, other)
    order = (2, 1, 3, 0)
    for slot, step in enumerate(order):
        for part in range(PARTS):
            third = lax.rem(mine[part][0] + step, 4)
            start(part, slot, held.at[part, other, third], from_core.at[part, third], place.sibling())
    pack(0, core)
    for slot, step in enumerate(order):
        for part in range(PARTS):
            third = lax.rem(mine[part][0] + step, 4)
            ahead, behind = place.peer(part, 2, 1), place.peer(part, 2, 3)
            arrived(part, slot, from_core.at[part, third])
            plane = held.at[part, core, third]
            accumulate(plane, [from_core.at[part, third]], 4)
            if step == 2:
                start(part, 4, plane.at[pl.ds(0, 2)], from_far.at[part, 0], ahead)
                start(part, 5, plane.at[pl.ds(2, 2)], from_far.at[part, 1], behind)
            if step == 1:
                arrived(part, 4, from_far.at[part, 0])
                accumulate(plane.at[pl.ds(0, 2)], [from_far.at[part, 0]], 2)
                start(part, 6, plane, from_near.at[part, 0], ahead)
            if step == 3:
                arrived(part, 5, from_far.at[part, 1])
                accumulate(plane.at[pl.ds(2, 2)], [from_far.at[part, 1]], 2)
                start(part, 7, plane, from_near.at[part, 1], behind)
    for part in range(PARTS):
        third, second, first = mine[part]
        arrived(part, 6, from_near.at[part, 0])
        arrived(part, 7, from_near.at[part, 1])
        accumulate(held.at[part, core, third], [from_near.at[part, 0], from_near.at[part, 1]], 4)
        for step in (1, 3, 2):
            start(
                part, 7 + step, held.at[part, core, third, lax.rem(second + step, 4)],
                from_second.at[part, step - 1], place.peer(part, 1, step),
            )
    for part in range(PARTS):
        third, second, first = mine[part]
        for step in (1, 3, 2):
            arrived(part, 7 + step, from_second.at[part, step - 1])
        plane = held.at[part, core, third]
        for inner in range(4):
            total = plane[second, inner].astype(jnp.float32)
            for step in range(3):
                total = total + from_second[part, step, inner].astype(jnp.float32)
            plane[second, inner] = total.astype(bf16)
        for step in (1, 3, 2):
            start(
                part, 10 + step, held.at[part, core, third, second, lax.rem(first + step, 4)],
                from_first.at[part, step - 1], place.peer(part, 0, step),
            )
    for part in range(PARTS):
        third, second, first = mine[part]
        for step in (1, 3, 2):
            arrived(part, 10 + step, from_first.at[part, step - 1])
        total = held[part, core, third, second, first].astype(jnp.float32)
        for step in range(3):
            total = total + from_first[part, step].astype(jnp.float32)
        out_ref[:, LANES * part : LANES * (part + 1)] = total
    for number, target in enumerate((query_out, key_out, value_out, output_out)):
        target[...] = out_ref[6 * number : 6 * number + 6, :]
    for number in range(4):
        expand_out[:, 768 * number : 768 * (number + 1)] = out_ref[32 + 6 * number : 38 + 6 * number, :]
    shrink_out[...] = out_ref[56:80, :]
    lanes_out[...] = out_ref[24:25, 0:128]
    for item in pending:
        item.wait_send()


def scatter(*grads):
    whole = pl.BlockSpec(memory_space=pltpu.VMEM)
    block = (ROWS_ALL, LANES)
    return pl.pallas_call(
        scatter_kernel,
        out_shape=tuple(shape(*s, kind=F32) for s in ((6, 768),) * 4 + ((6, 3072), (24, 768), (1, 128))),
        in_specs=[whole] * 11,
        out_specs=[whole] * 7,
        scratch_shapes=[
            pltpu.VMEM((ROWS_ALL, 768), F32),
            pltpu.VMEM((PARTS, 2, 4, 4, 4) + block, jnp.bfloat16),
            pltpu.VMEM((PARTS, 4, 4, 4) + block, jnp.bfloat16),
            pltpu.VMEM((PARTS, 2, 2, 4) + block, jnp.bfloat16),
            pltpu.VMEM((PARTS, 2, 4, 4) + block, jnp.bfloat16),
            pltpu.VMEM((PARTS, 3, 4) + block, jnp.bfloat16),
            pltpu.VMEM((PARTS, 3) + block, jnp.bfloat16),
            pltpu.VMEM((128, 128), jnp.float32),
            pltpu.SemaphoreType.DMA((PARTS, 14)),
            pltpu.SemaphoreType.DMA((PARTS, 14)),
        ],
        compiler_params=pltpu.CompilerParams(
            collective_id=1, has_side_effects=True, vmem_limit_bytes=60 * 2**20
        ),
        name="scatter",
    )(
        *grads,
        jnp.asarray(attention_rows(), jnp.bfloat16),
        jnp.asarray(feed_rows(), jnp.bfloat16),
        jnp.asarray(vector_lanes(), jnp.bfloat16),
    )


PLACES = (0, 6, 12, 18, 24, 30, 36, 42, 48)


def local(
    frames,
    upstream,
    clip_lengths,
    clip_skip,
    query_weight,
    key_weight,
    value_weight,
    output_weight,
    query_bias,
    value_bias,
    output_bias,
    first_gain,
    first_shift,
    expand_weight,
    shrink_weight,
    expand_bias,
    shrink_bias,
    second_gain,
    second_shift,
):
    vectors = (
        query_bias, value_bias, output_bias, first_gain, first_shift, shrink_bias, second_gain, second_shift, expand_bias,
    )
    lanes = sum(
        jnp.pad(v.astype(F32), (place, 128 - place - v.shape[0])) for place, v in zip(PLACES, vectors, strict=True)
    )
    attend, output, expand, shrink, whole = gather(
        query_weight, key_weight, value_weight, output_weight, expand_weight, shrink_weight, lanes[None]
    )
    q_n, k_t, v_n, ctx_t, inverse, probs = attend_call(clip_lengths, frames, attend, whole)
    encoded, residual_grad, branch_grad, output_grad, expand_grad, shrink_grad, vector_grad = feed_call(
        clip_lengths, clip_skip, frames, upstream, ctx_t, output, expand, shrink, whole
    )
    frames_grad, query_grad, key_grad, value_grad, first_vector_grad = back_call(
        clip_lengths, clip_skip, frames, upstream, q_n, k_t, v_n, ctx_t, inverse, probs, branch_grad, residual_grad, attend, output
    )
    query_sum, key_sum, value_sum, output_sum, expand_sum, shrink_sum, lanes = scatter(
        query_grad, key_grad, value_grad, output_grad, expand_grad, shrink_grad, first_vector_grad, vector_grad
    )
    sums = [lanes[0, place : place + v.shape[0]] for place, v in zip(PLACES, vectors, strict=True)]
    return (
        encoded, frames_grad, query_sum, key_sum, value_sum, output_sum, sums[0], sums[1], sums[2], sums[3], sums[4],
        expand_sum, shrink_sum, sums[8], sums[5], sums[6], sums[7],
    )


def solution(mesh):
    return jax.shard_map(
        local,
        mesh=mesh,
        in_specs=(
            P(("dp", "fsdp"), None),
            P(("dp", "fsdp"), None),
            P(("dp", "fsdp"), None),
            P(("dp", "fsdp"), None),
            P(("dp", "fsdp"), None),
            P(("dp", "fsdp"), None),
            P(("dp", "fsdp"), None),
            P(("dp", "fsdp"), None),
            P(("dp", "fsdp")),
            P(("dp", "fsdp")),
            P(("dp", "fsdp")),
            P(("dp", "fsdp")),
            P(("dp", "fsdp")),
            P(("dp", "fsdp"), None),
            P(("dp", "fsdp"), None),
            P(("dp", "fsdp")),
            P(("dp", "fsdp")),
            P(("dp", "fsdp")),
            P(("dp", "fsdp")),
        ),
        out_specs=(
            P(("dp", "fsdp"), None),
            P(("dp", "fsdp"), None),
            P(("dp", "fsdp"), None),
            P(("dp", "fsdp"), None),
            P(("dp", "fsdp"), None),
            P(("dp", "fsdp"), None),
            P(("dp", "fsdp")),
            P(("dp", "fsdp")),
            P(("dp", "fsdp")),
            P(("dp", "fsdp")),
            P(("dp", "fsdp")),
            P(("dp", "fsdp"), None),
            P(("dp", "fsdp"), None),
            P(("dp", "fsdp")),
            P(("dp", "fsdp")),
            P(("dp", "fsdp")),
            P(("dp", "fsdp")),
        ),
        check_vma=False,
    )
```

```python
import functools
import math

import jax
import jax.numpy as jnp
import numpy as np
from jax import lax
from jax.experimental import pallas as pl
from jax.experimental.pallas import tpu as pltpu
from jax.sharding import PartitionSpec as P

epsilon = 1e-05

SCALE = 0.125
EXCLUDED = -1e30
F32 = jnp.float32
BF16 = jnp.bfloat16
WHOLE = pl.BlockSpec(memory_space=pltpu.VMEM)
SCALARS = pl.BlockSpec(memory_space=pltpu.SMEM)
ANYWHERE = pl.BlockSpec(memory_space=pl.ANY)
VEC_QUERY, VEC_VALUE, VEC_OUTPUT, VEC_GAIN1, VEC_SHIFT1, VEC_SHRINK, VEC_GAIN2, VEC_SHIFT2, VEC_EXPAND = range(9)


def dot(left, right, a=1, b=0):
    return lax.dot_general(left, right, (((a,), (b,)), ((), ())), preferred_element_type=F32)


def shape(*sizes, kind=jnp.bfloat16):
    return jax.ShapeDtypeStruct(sizes, kind)


def segments(lengths_ref, axis, extent, first=0):
    place = lax.broadcasted_iota(jnp.int32, extent, axis) + first
    first_end = lengths_ref[0, 0]
    second_end = first_end + lengths_ref[0, 1]
    return jnp.where(place < first_end, 0, jnp.where(place < second_end, 1, 2))


def live_mask(lengths_ref, skip_ref, extent, first):
    segment = segments(lengths_ref, 0, extent, first)
    dropped = jnp.where(segment == 0, skip_ref[0, 0], jnp.where(segment == 1, skip_ref[0, 1], 1))
    return dropped == 0


def vector(ref, number):
    return ref[0:1, 768 * number : 768 * (number + 1)]


def head_rows(head):
    return pl.ds(pl.multiple_of(head * 64, 64), 64)


def pair_lanes(pair):
    return pl.ds(pl.multiple_of(pair * 128, 128), 128)


def project(frames, attend, vectors, q_n, k_n, v_n, q_t, k_t, v_t):
    x = frames[...]
    q_n[...] = ((dot(x, attend[0]) + vector(vectors, VEC_QUERY)) * SCALE).astype(BF16)
    q_t[...] = q_n[...].T
    k_n[...] = dot(x, attend[1]).astype(BF16)
    k_t[...] = k_n[...].T
    v_n[...] = (dot(x, attend[2]) + vector(vectors, VEC_VALUE)).astype(BF16)
    v_t[...] = v_n[...].T


def mask_operands(lengths_ref, right, k_mask):
    lane = lax.broadcasted_iota(jnp.int32, (768, 128), 1)
    k_mask[...] = jnp.where(lane == segments(lengths_ref, 0, (768, 128)), 1.0, 0.0).astype(BF16)
    row = lax.broadcasted_iota(jnp.int32, (128, 768), 0)
    other = (row < 3) & (row != segments(lengths_ref, 1, (128, 768)))
    other = jnp.where(other, EXCLUDED, 0.0).astype(BF16)
    for side in range(2):
        right[side, 128:256] = other
        right[side, 64 * (1 - side) : 64 * (1 - side) + 64] = jnp.zeros((64, 768), BF16)


def score_stage(pair, side, q_t, k_n, k_mask, right, scores, tops):
    left = jnp.concatenate([k_n[:, pair_lanes(pair)], k_mask[...]], axis=1)
    right[side, 64 * side : 64 * side + 64] = q_t[head_rows(pair * 2 + side), :]
    values = dot(left, right[side])
    scores[side] = values
    tops[side] = jnp.broadcast_to(jnp.max(values, axis=0, keepdims=True), (8, 768))


def prob_stage(pair, side, v_t, scores, tops, probs, inverse, ctx_t):
    head = pair * 2 + side
    rows = head_rows(head)
    left = jnp.concatenate([v_t[rows, :], jnp.ones((16, 768), BF16)], axis=0)
    raised = jnp.exp(scores[side] - tops[side, 0:1]).astype(BF16)
    probs[side][...] = raised
    total = dot(left, raised)
    factor = 1.0 / total[64:65]
    inverse[pl.ds(pl.multiple_of(head * 8, 8), 8), :] = jnp.broadcast_to(factor, (8, 768))
    ctx_t[rows, :] = (total[:64] * factor).astype(BF16)


def gelu_pair(v):
    x = jnp.abs(v) * (1.0 / math.sqrt(2.0))
    t = 1.0 / (1.0 + 0.3275911 * x)
    e = jnp.exp(-(x * x))
    poly = t * (0.254829592 + t * (-0.284496736 + t * (1.421413741 + t * (-1.453152027 + t * 1.061405429))))
    tail = 0.5 * poly * e
    phi = jnp.where(v >= 0, 1.0 - tail, tail)
    return v * phi, phi + v * e * (1.0 / math.sqrt(2.0 * math.pi))


def normalise(values):
    centered = values - jnp.mean(values, axis=-1, keepdims=True)
    scale = lax.rsqrt(jnp.mean(centered * centered, axis=-1, keepdims=True) + epsilon)
    return centered * scale, scale


def norm_back(cotangent, gain, normed, scale):
    c = cotangent * gain
    return scale * (
        c - jnp.mean(c, axis=-1, keepdims=True) - normed * jnp.mean(c * normed, axis=-1, keepdims=True)
    )


MESH = pl.DeviceIdType.MESH
ROWS_A = 32
ROWS_F = 48
ROWS_ALL = ROWS_A + ROWS_F
LANES = 256
PARTS = 3
HALF_F = PARTS * 64 * ROWS_F
VECTORS = 12
BIAS_OUT = 208


def attention_rows():
    table = np.zeros((BIAS_OUT, 8 * ROWS_A), np.float32)
    for row in range(192):
        matrix, inner = divmod(row, 48)
        device, lane = divmod(inner, 6)
        table[row, device * ROWS_A + 6 * matrix + lane] = 1
    for device in range(8):
        table[192 + device, device * ROWS_A + 24] = 1
    return table


def expand_rows():
    table = np.zeros((192, 256), np.float32)
    for row in range(192):
        matrix, inner = divmod(row, 48)
        device, lane = divmod(inner, 6)
        table[row, 32 * device + 6 * matrix + lane] = 1
    return table


def shrink_rows():
    table = np.zeros((192, 256), np.float32)
    for row in range(192):
        device, lane = divmod(row, 24)
        table[row, 32 * device + 8 + lane] = 1
    return table


def vector_lanes(number):
    lane = lax.broadcasted_iota(jnp.int32, (128, 768), 0)
    column = lax.broadcasted_iota(jnp.int32, (128, 768), 1)
    if number < 8:
        wanted = column - 6 * ((column * 10923) >> 16) + 6 * number
    else:
        wanted = column - 24 * ((column * 2731) >> 16) + 48
    return jnp.where(lane == wanted, 1.0, 0.0).astype(BF16)


def owner_mask(first, wide):
    device = lax.broadcasted_iota(jnp.int32, (128, 768), 0)
    column = lax.broadcasted_iota(jnp.int32, (128, 768), 1) + first
    low = device * wide
    return (column >= low) & (column < low + wide)


def position():
    dp = lax.axis_index("dp")
    fsdp = lax.axis_index("fsdp")
    core = lax.rem(dp, 2)
    y = lax.rem(dp // 2, 4)
    z = (dp // 8) * 2 + fsdp // 4
    x = lax.rem(fsdp, 4)
    return x, y, z, core


def device_of(x, y, z, core):
    return (((z // 2) * 4 + y) * 2 + core, lax.rem(z, 2) * 4 + x)


AXES = ((0, 1, 2), (1, 2, 0), (2, 0, 1))


class Place:
    def __init__(self):
        self.at = position()

    def along(self, part, stage):
        return self.at[AXES[part][stage]]

    def peer(self, part, stage, step):
        where = list(self.at)
        axis = AXES[part][stage]
        where[axis] = lax.rem(where[axis] + step, 4)
        return device_of(*where)

    def sibling(self):
        x, y, z, core = self.at
        return device_of(x, y, z, 1 - core)


def greet(place):
    targets = [place.sibling()]
    for axis in range(3):
        for step in (1, 2, 3):
            where = list(place.at)
            where[axis] = lax.rem(where[axis] + step, 4)
            targets.append(device_of(*where))
    for target in targets:
        pl.semaphore_signal(pltpu.get_barrier_semaphore(), inc=1, device_id=target, device_id_type=MESH)


def meet():
    pl.semaphore_wait(pltpu.get_barrier_semaphore(), 10)


def remote(source, target, send, receive, device):
    return pltpu.make_async_remote_copy(
        src_ref=source,
        dst_ref=target,
        send_sem=send,
        recv_sem=receive,
        device_id=device,
        device_id_type=MESH,
    )


def chunk_blocks(part, dp):
    high, y, core = dp // 8, lax.rem(dp // 2, 4), lax.rem(dp, 2)
    blocks = []
    for low in range(2):
        for x in range(4):
            where = (x, y, high * 2 + low)
            first, second, third = (where[a] for a in AXES[part])
            blocks.append((part, core, third, second, first))
    return blocks


class Gather:
    def __init__(self, place, held, rows, send, recv):
        self.place, self.held, self.rows, self.send, self.recv = place, held, rows, send, recv
        self.core = place.at[3]

    def view(self, part, core, third, second=0, first=0, count=1):
        start = (((core * PARTS + part) * 4 + third) * 4 + second) * 4 + first
        return self.held.at[pl.ds(pl.multiple_of(start * self.rows, 16), count * self.rows), :]

    def mine(self, part):
        return tuple(self.place.along(part, stage) for stage in (2, 1, 0))

    def copy(self, part, number, view, device):
        return remote(view, view, self.send.at[part, number], self.recv.at[part, number], device)

    def start(self, part, number, view, device):
        self.copy(part, number, view, device).start()

    def arrived(self, part, number, view):
        self.copy(part, number, view, self.place.sibling()).wait_recv()

    def block(self, part, third, second, first):
        return self.view(part, self.core, third, second, first)

    def two(self, part, third, second, half):
        return self.view(part, self.core, third, second, 2 * half, 2)

    def eight(self, part, core, third, half):
        return self.view(part, core, third, 2 * half, 0, 8)

    def first(self):
        for part in range(PARTS):
            view = self.block(part, *self.mine(part))
            for step in (1, 3, 2):
                self.start(part, step - 1, view, self.place.peer(part, 0, step))

    def second(self):
        for part in range(PARTS):
            third, second, first = self.mine(part)
            for step in (1, 3, 2):
                self.arrived(part, step - 1, self.block(part, third, second, lax.rem(first + 4 - step, 4)))
            ahead, behind = self.place.peer(part, 1, 1), self.place.peer(part, 1, 3)
            for half in (0, 1):
                self.start(part, 3 + half, self.two(part, third, second, half), ahead)
                self.start(part, 6 - half, self.two(part, third, second, 1 - half), behind)

    def second_on(self):
        for part in range(PARTS):
            third, second, first = self.mine(part)
            ahead, behind = self.place.peer(part, 1, 1), self.place.peer(part, 1, 3)
            view = self.two(part, third, lax.rem(second + 3, 4), 0)
            self.arrived(part, 3, view)
            self.start(part, 7, view, ahead)
            view = self.two(part, third, lax.rem(second + 1, 4), 1)
            self.arrived(part, 6, view)
            self.start(part, 8, view, behind)

    def third(self):
        for part in range(PARTS):
            third, second, first = self.mine(part)
            self.arrived(part, 4, self.two(part, third, lax.rem(second + 3, 4), 1))
            self.arrived(part, 5, self.two(part, third, lax.rem(second + 1, 4), 0))
            for half in (0, 1):
                self.arrived(part, 7 + half, self.two(part, third, lax.rem(second + 2, 4), half))
            ahead, behind = self.place.peer(part, 2, 1), self.place.peer(part, 2, 3)
            for half in (0, 1):
                self.start(part, 9 + half, self.eight(part, self.core, third, half), ahead)
                self.start(part, 12 - half, self.eight(part, self.core, third, 1 - half), behind)
            self.start(part, 15, self.view(part, self.core, third, count=16), self.place.sibling())

    def third_on(self):
        for part in range(PARTS):
            third, second, first = self.mine(part)
            ahead, behind = self.place.peer(part, 2, 1), self.place.peer(part, 2, 3)
            view = self.eight(part, self.core, lax.rem(third + 3, 4), 0)
            self.arrived(part, 9, view)
            self.start(part, 13, view, ahead)
            self.start(part, 16, view, self.place.sibling())
            view = self.eight(part, self.core, lax.rem(third + 1, 4), 1)
            self.arrived(part, 12, view)
            self.start(part, 14, view, behind)
            self.start(part, 17, view, self.place.sibling())

    def near_over(self):
        for part in range(PARTS):
            third, second, first = self.mine(part)
            view = self.eight(part, self.core, lax.rem(third + 3, 4), 1)
            self.arrived(part, 10, view)
            self.start(part, 18, view, self.place.sibling())
            view = self.eight(part, self.core, lax.rem(third + 1, 4), 0)
            self.arrived(part, 11, view)
            self.start(part, 19, view, self.place.sibling())

    def far_over(self):
        for part in range(PARTS):
            third, second, first = self.mine(part)
            for half in (0, 1):
                view = self.eight(part, self.core, lax.rem(third + 2, 4), half)
                self.arrived(part, 13 + half, view)
                self.start(part, 20 + half, view, self.place.sibling())

    def finish(self):
        other = 1 - self.core
        for part in range(PARTS):
            third, second, first = self.mine(part)
            self.arrived(part, 15, self.view(part, other, third, count=16))
            self.arrived(part, 16, self.eight(part, other, lax.rem(third + 3, 4), 0))
            self.arrived(part, 17, self.eight(part, other, lax.rem(third + 1, 4), 1))
            self.arrived(part, 18, self.eight(part, other, lax.rem(third + 3, 4), 1))
            self.arrived(part, 19, self.eight(part, other, lax.rem(third + 1, 4), 0))
            for half in (0, 1):
                self.arrived(part, 20 + half, self.eight(part, other, lax.rem(third + 2, 4), half))

    def sent(self):
        for part in range(PARTS):
            for number in range(22):
                if number < 3:
                    view = self.block(part, 0, 0, 0)
                elif number < 9:
                    view = self.two(part, 0, 0, 0)
                elif number == 15:
                    view = self.view(part, self.core, 0, count=16)
                else:
                    view = self.eight(part, self.core, 0, 0)
                self.copy(part, number, view, self.place.sibling()).wait_send()


def unpack_attention(held, rows_a_ref, attend, output, vectors, spread):
    def body(number, carry):
        for inner in range(2):
            dp = number * 2 + inner
            rows = pl.ds(pl.multiple_of(dp * 48, 16), 48)
            for part in range(PARTS):
                columns = slice(LANES * part, LANES * (part + 1))
                blocks = jnp.concatenate([held.view(*index)[...] for index in chunk_blocks(part, dp)], axis=0)
                blocks = dot(rows_a_ref[...], blocks)
                if part == 0:
                    spread[pl.ds(pl.multiple_of(dp * 8, 8), 8), :] = blocks[192:200, :128]
                blocks = blocks.astype(BF16)
                for matrix in range(3):
                    attend[matrix, rows, columns] = blocks[48 * matrix : 48 * (matrix + 1)]
                output[rows, columns] = blocks[144:192]
        return carry

    lax.fori_loop(0, 8, body, 0)
    packed = spread[...].astype(BF16)
    for number in range(VECTORS):
        wide = 6 if number < 8 else 24
        mask = owner_mask(0 if number < 8 else 768 * (number - 8), wide)
        columns = slice(768 * number, 768 * (number + 1))
        whole = dot(packed, vector_lanes(number))
        vectors[:, columns] = jnp.sum(jnp.where(mask, whole, 0.0), axis=0, keepdims=True)


def unpack_feed(held, rows_e_ref, rows_s_ref, expand, shrink):
    def body(number, carry):
        for inner in range(2):
            dp = number * 2 + inner
            rows = pl.ds(pl.multiple_of(dp * 48, 16), 48)
            for part in range(PARTS):
                columns = slice(LANES * part, LANES * (part + 1))
                blocks = [held.view(*index)[...] for index in chunk_blocks(part, dp)]
                first = dot(rows_e_ref[...], jnp.concatenate([b[:32] for b in blocks], axis=0)).astype(BF16)
                second = dot(rows_s_ref[...], jnp.concatenate([b[16:] for b in blocks], axis=0)).astype(BF16)
                for matrix in range(4):
                    expand[rows, 768 * matrix + LANES * part : 768 * matrix + LANES * (part + 1)] = first[
                        48 * matrix : 48 * (matrix + 1)
                    ]
                shrink[pl.ds(pl.multiple_of(dp * 192, 16), 192), columns] = second
        return carry

    lax.fori_loop(0, 8, body, 0)


def pack_feed(held, rows_e_ref, rows_s_ref, expand, shrink):
    def body(number, carry):
        for inner in range(2):
            dp = number * 2 + inner
            rows = pl.ds(pl.multiple_of(dp * 48, 16), 48)
            for part in range(PARTS):
                pieces = [
                    expand[rows, 768 * matrix + LANES * part : 768 * matrix + LANES * (part + 1)] for matrix in range(4)
                ]
                first = dot(rows_e_ref[...], jnp.concatenate(pieces, axis=0), 0, 0)
                values = shrink[pl.ds(pl.multiple_of(dp * 192, 16), 192), LANES * part : LANES * (part + 1)]
                second = dot(rows_s_ref[...], values, 0, 0)
                for device, index in enumerate(chunk_blocks(part, dp)):
                    start = 32 * device
                    block = held.view(*index)
                    block[0:16, :] = first[start : start + 16].astype(BF16)
                    block[16:32, :] = (first[start + 16 : start + 32] + second[start : start + 16]).astype(BF16)
                    block[32:48, :] = second[start + 16 : start + 32].astype(BF16)
        return carry

    lax.fori_loop(0, 8, body, 0)


def forward_kernel(
    lengths_ref, skip_ref, frames_in, upstream_in,
    query_in, key_in, value_in, output_in, expand_in, shrink_in, lanes_in, rows_a_ref, rows_e_ref, rows_s_ref,
    vector_out, encoded_out, residual_out, branch_out, ctx_out, inverse_out,
    attend_out, weight_out, output_out, q_out, k_out, v_out, probs_out, feed_out,
    held_a, held_f, block_ref, spread, attend, output_weight, expand, shrink, vectors,
    frames, upstream, encoded, residual_grad, branch_grad, ctx_t, inverse,
    send_a, recv_a, send_f, recv_f, local,
):
    place = Place()
    core = place.at[3]
    greet(place)
    frames_load = pltpu.make_async_copy(frames_in, frames, local.at[32])
    upstream_load = pltpu.make_async_copy(upstream_in, upstream, local.at[33])
    frames_load.start()
    upstream_load.start()
    for number, source in enumerate((query_in, key_in, value_in, output_in)):
        block_ref[6 * number : 6 * number + 6, :] = source[...].astype(F32)
    block_ref[24:32, :] = jnp.zeros((8, 768), F32)
    block_ref[24:25, 0:128] = lanes_in[...]
    for number in range(4):
        block_ref[32 + 6 * number : 38 + 6 * number, :] = expand_in[:, 768 * number : 768 * (number + 1)].astype(F32)
    block_ref[56:80, :] = shrink_in[...].astype(F32)
    early = Gather(place, held_a, ROWS_A, send_a, recv_a)
    late = Gather(place, held_f, ROWS_F, send_f, recv_f)
    for part in range(PARTS):
        third, second, first = early.mine(part)
        values = block_ref[:, LANES * part : LANES * (part + 1)].astype(BF16)
        early.block(part, third, second, first)[...] = values[:ROWS_A]
        late.block(part, third, second, first)[...] = values[ROWS_A:]
    meet()
    early.first()
    late.first()
    early.second()
    early.second_on()
    early.third()
    late.second()
    early.third_on()
    late.second_on()
    early.near_over()
    early.far_over()
    late.third()
    early.finish()
    unpack_attention(early, rows_a_ref, attend, output_weight, vectors, spread)
    keep = [
        pltpu.make_async_copy(attend, attend_out, local.at[0]),
        pltpu.make_async_copy(output_weight, weight_out, local.at[1]),
    ]
    for item in keep:
        item.start()
    late.third_on()

    def attention(right, k_mask, scores, tops):
        q_n, k_n, v_n, q_t = (expand.at[:, 768 * i : 768 * (i + 1)] for i in range(4))
        k_t, v_t, *probs = (shrink.at[768 * i : 768 * (i + 1), :] for i in range(4))
        frames_load.wait()
        project(frames, attend, vectors, q_n, k_n, v_n, q_t, k_t, v_t)
        hold = [
            pltpu.make_async_copy(q_n, q_out, local.at[2]),
            pltpu.make_async_copy(k_t, k_out, local.at[3]),
            pltpu.make_async_copy(v_n, v_out, local.at[4]),
        ]
        for item in hold:
            item.start()
        mask_operands(lengths_ref, right, k_mask)
        score_stage(0, 0, q_t, k_n, k_mask, right, scores, tops)

        def away(head, side):
            return pltpu.make_async_copy(probs[side], probs_out.at[head], local.at[5 + side])

        def body(pair, carry):
            @pl.when(pair > 0)
            def _():
                away(0, 0).wait()

            @pl.when(pair == 1)
            def _():
                late.near_over()

            @pl.when(pair == 3)
            def _():
                late.far_over()

            score_stage(pair, 1, q_t, k_n, k_mask, right, scores, tops)
            prob_stage(pair, 0, v_t, scores, tops, probs, inverse, ctx_t)
            away(pair * 2, 0).start()

            @pl.when(pair > 0)
            def _():
                away(0, 1).wait()

            score_stage(jnp.minimum(pair + 1, 5), 0, q_t, k_n, k_mask, right, scores, tops)
            prob_stage(pair, 1, v_t, scores, tops, probs, inverse, ctx_t)
            away(pair * 2 + 1, 1).start()
            return carry

        lax.fori_loop(0, 6, body, 0)
        for side in range(2):
            away(0, side).wait()
        for item in hold:
            item.wait()

    square = pltpu.VMEM((768, 768), BF16)
    pl.run_scoped(
        attention, pltpu.VMEM((2, 256, 768), BF16), pltpu.VMEM((768, 128), BF16),
        pltpu.VMEM((2, 768, 768), F32), pltpu.VMEM((2, 8, 768), F32),
    )
    saves = [
        pltpu.make_async_copy(ctx_t, ctx_out, local.at[34]),
        pltpu.make_async_copy(inverse, inverse_out, local.at[35]),
        pltpu.make_async_copy(encoded, encoded_out, local.at[36]),
        pltpu.make_async_copy(residual_grad, residual_out, local.at[37]),
        pltpu.make_async_copy(branch_grad, branch_out, local.at[38]),
    ]
    saves[0].start()
    saves[1].start()
    late.finish()
    late.sent()
    unpack_feed(late, rows_e_ref, rows_s_ref, expand, shrink)
    upstream_load.wait()

    def feed(normed, scales, hidden, raw):
        feed_forward(
            lengths_ref, skip_ref, frames, upstream, ctx_t, output_weight, expand, shrink, vectors,
            encoded, residual_grad, branch_grad, output_out, vector_out,
            normed, scales, hidden, held_f, raw, branch_grad, local, saves,
            lambda: pack_feed(late, rows_e_ref, rows_s_ref, expand, shrink),
            pltpu.make_async_copy(held_f, feed_out, local.at[7]),
        )

    pl.run_scoped(
        feed, pltpu.VMEM((768, 768), F32), pltpu.VMEM((768, 128), F32), square,
        pltpu.VMEM((2, 768, 512), F32),
    )
    for item in keep + saves:
        item.wait()
    early.sent()


def feed_forward(
    lengths_ref, skip_ref, frames, upstream, ctx_t, output_weight, expand, shrink, vectors,
    encoded, acc, branch_grad, output_out, vector_out,
    normed, scales, hidden, panels, raw, summed_grad, local, saves, pack, feed_move,
):
    def rows_of(block):
        return slice(256 * block, 256 * (block + 1))

    def wide_columns(chunk):
        return pl.ds(pl.multiple_of(768 * chunk, 768), 768)

    for block in range(3):
        rows = rows_of(block)
        values = (
            dot(ctx_t[:, rows], output_weight[...], 0, 0) + frames[rows, :].astype(F32) + vector(vectors, VEC_OUTPUT)
        )
        unit, scale = normalise(values)
        normed[rows, :] = unit
        scales[rows, :] = jnp.broadcast_to(scale, (256, 128))
        hidden[rows, :] = (unit * vector(vectors, VEC_GAIN1) + vector(vectors, VEC_SHIFT1)).astype(BF16)

    def panel(kind, number, block=None):
        start = (kind * 12 + number) * 768
        if block is None:
            return panels.at[pl.ds(pl.multiple_of(start, 256), 768), :]
        return panels.at[pl.ds(pl.multiple_of(start + 256 * block, 256), 256), :]

    def load(kind, first, count, block=None):
        return jnp.concatenate([panel(kind, first + i, block)[...] for i in range(count)], axis=1)

    def save(kind, first, count, block, values):
        for i in range(count):
            panel(kind, first + i, block)[...] = values[:, 256 * i : 256 * (i + 1)].astype(BF16)

    def narrow_columns(chunk):
        return pl.ds(pl.multiple_of(512 * chunk, 512), 512)

    def expand_stage(chunk, slot):
        raw[slot] = dot(hidden[...], expand[:, narrow_columns(chunk)])

    def gelu_stage(chunk, slot):
        bias = vectors[0:1, pl.ds(pl.multiple_of(768 * VEC_EXPAND + 512 * chunk, 512), 512)]
        for block in range(3):
            rows = rows_of(block)
            value, derivative = gelu_pair(raw[slot, rows] + bias)
            save(0, 2 * chunk, 2, block, value)
            save(1, 2 * chunk, 2, block, derivative)

    def shrink_stage(chunk, first=False):
        columns = narrow_columns(chunk)
        for block in range(3):
            rows = rows_of(block)
            product = dot(load(0, 2 * chunk, 2, block), shrink[columns, :])
            acc[rows, :] = product if first else acc[rows, :] + product

    expand_stage(0, 0)
    expand_stage(1, 1)
    gelu_stage(0, 0)
    acc[...] = jnp.zeros((768, 768), F32)

    def chunks(number, carry):
        for inner in (1, 2):
            chunk = 2 * number + inner
            expand_stage(chunk + 1, 1 - inner % 2)
            gelu_stage(chunk, inner % 2)
            shrink_stage(chunk - 1)
        return carry

    for number in range(2):
        chunks(number, 0)
    gelu_stage(5, 1)
    shrink_stage(4)
    shrink_stage(5)

    sums = [jnp.zeros((1, 768), F32) for _ in range(3)]
    for block in range(3):
        rows = rows_of(block)
        first = normed[rows, :] * vector(vectors, VEC_GAIN1) + vector(vectors, VEC_SHIFT1)
        unit, scale = normalise(first + acc[rows, :] + vector(vectors, VEC_SHRINK))
        result = unit * vector(vectors, VEC_GAIN2) + vector(vectors, VEC_SHIFT2)
        live = live_mask(lengths_ref, skip_ref, (256, 1), 256 * block)
        encoded[rows, :] = jnp.where(live, result, frames[rows, :].astype(F32)).astype(BF16)
        cotangent = jnp.where(live, upstream[rows, :].astype(F32), 0.0)
        grad = norm_back(cotangent, vector(vectors, VEC_GAIN2), unit, scale)
        acc[rows, :] = grad
        summed_grad[rows, :] = grad.astype(BF16)
        sums[0] = sums[0] + jnp.sum(cotangent * unit, axis=0, keepdims=True)
        sums[1] = sums[1] + jnp.sum(cotangent, axis=0, keepdims=True)
        sums[2] = sums[2] + jnp.sum(grad, axis=0, keepdims=True)

    saves[2].start()

    def put(number, value):
        vector_out[0:1, 768 * number : 768 * (number + 1)] = value

    put(VEC_QUERY, jnp.zeros((1, 768), F32))
    put(VEC_VALUE, jnp.zeros((1, 768), F32))
    put(VEC_GAIN2, sums[0])
    put(VEC_SHIFT2, sums[1])
    put(VEC_SHRINK, sums[2])

    def shrink_back(chunk, carry):
        columns = wide_columns(chunk)
        total = jnp.zeros((1, 768), F32)
        for block in range(3):
            rows = rows_of(block)
            grad = dot(summed_grad[rows, :], shrink[columns, :], 1, 1) * load(1, 3 * chunk, 3, block).astype(F32)
            total = total + jnp.sum(grad, axis=0, keepdims=True)
            save(1, 3 * chunk, 3, block, grad)
        vector_out[0:1, pl.ds(pl.multiple_of(768 * (VEC_EXPAND + chunk), 768), 768)] = total
        for block in range(3):
            part = pl.ds(pl.multiple_of(768 * chunk + 256 * block, 256), 256)
            shrink[part, :] = dot(panel(0, 3 * chunk + block)[...], summed_grad[...], 0, 0).astype(BF16)
        return carry

    for chunk in range(4):
        shrink_back(chunk, 0)

    def expand_back(chunk, carry):
        columns = wide_columns(chunk)
        for block in range(3):
            rows = rows_of(block)
            acc[rows, :] = acc[rows, :] + dot(load(1, 3 * chunk, 3, block), expand[:, columns], 1, 1)
        for block in range(3):
            part = pl.ds(pl.multiple_of(768 * chunk + 256 * block, 256), 256)
            expand[:, part] = dot(hidden[...], panel(1, 3 * chunk + block)[...], 0, 0).astype(BF16)
        return carry

    for chunk in range(4):
        expand_back(chunk, 0)
    pack()
    feed_move.start()
    sums = [jnp.zeros((1, 768), F32) for _ in range(3)]
    for block in range(3):
        rows = rows_of(block)
        grad = acc[rows, :]
        unit = normed[rows, :]
        back = norm_back(grad, vector(vectors, VEC_GAIN1), unit, scales[rows, 0:1])
        acc[rows, :] = back
        branch_grad[rows, :] = back.astype(BF16)
        sums[0] = sums[0] + jnp.sum(grad * unit, axis=0, keepdims=True)
        sums[1] = sums[1] + jnp.sum(grad, axis=0, keepdims=True)
        sums[2] = sums[2] + jnp.sum(back, axis=0, keepdims=True)
    saves[3].start()
    saves[4].start()
    put(VEC_GAIN1, sums[0])
    put(VEC_SHIFT1, sums[1])
    put(VEC_OUTPUT, sums[2])
    hidden[...] = dot(ctx_t[...], branch_grad[...]).astype(BF16)
    move = pltpu.make_async_copy(hidden, output_out, local.at[31])
    move.start()
    feed_move.wait()
    move.wait()


def forward_call(lengths, skip, frames, upstream, *shards):
    square = shape(768, 768)
    return pl.pallas_call(
        forward_kernel,
        out_shape=(
            shape(1, VECTORS * 768, kind=F32), square, shape(768, 768, kind=F32), square, square,
            shape(96, 768, kind=F32), shape(3, 768, 768), square, square, square, square, square, shape(12, 768, 768),
            shape(PARTS * 128 * ROWS_F, LANES),
        ),
        in_specs=[SCALARS] * 2 + [ANYWHERE] * 2 + [WHOLE] * 10,
        out_specs=[WHOLE] + [ANYWHERE] * 13,
        scratch_shapes=[
            pltpu.VMEM((PARTS * 128 * ROWS_A, LANES), BF16),
            pltpu.VMEM((PARTS * 128 * ROWS_F, LANES), BF16),
            pltpu.VMEM((ROWS_ALL, 768), F32),
            pltpu.VMEM((128, 128), F32),
            pltpu.VMEM((3, 768, 768), BF16),
            pltpu.VMEM((768, 768), BF16),
            pltpu.VMEM((768, 3072), BF16),
            pltpu.VMEM((3072, 768), BF16),
            pltpu.VMEM((1, VECTORS * 768), F32),
        ]
        + [pltpu.VMEM((768, 768), kind) for kind in (BF16, BF16, BF16, F32, BF16, BF16)]
        + [pltpu.VMEM((96, 768), F32)]
        + [pltpu.SemaphoreType.DMA((PARTS, 22))] * 4
        + [pltpu.SemaphoreType.DMA((39,))],
        compiler_params=pltpu.CompilerParams(collective_id=0, has_side_effects=True, vmem_limit_bytes=62 * 2**20),
        name="forward",
    )(
        lengths, skip, frames, upstream, *shards,
        jnp.asarray(attention_rows(), BF16), jnp.asarray(expand_rows(), BF16), jnp.asarray(shrink_rows(), BF16),
    )


class Scatter:
    def __init__(self, place, own, outgoing, other, far, near, second, first, rows, send, recv):
        self.place, self.own, self.outgoing, self.other = place, own, outgoing, other
        self.rows, self.send, self.recv = rows, send, recv
        self.buffers = (far, near, second, first)

    def mine(self, part):
        return tuple(self.place.along(part, stage) for stage in (2, 1, 0))

    def rows_of(self, ref, start, count):
        return ref.at[pl.ds(pl.multiple_of(start * self.rows, 16), count * self.rows), :]

    def view(self, part, third, second=0, first=0, count=1, ref=None):
        return self.rows_of(self.own if ref is None else ref, ((part * 4 + third) * 4 + second) * 4 + first, count)

    def across(self, part, third, second=0, count=16):
        return self.view(part, third, second, 0, count, self.other)

    def landing(self, kind, part, slot):
        slots, count = ((2, 8), (2, 16), (3, 4), (3, 1))[kind]
        return self.rows_of(self.buffers[kind], (part * slots + slot) * count, count)

    def start(self, part, number, source, target, device):
        remote(source, target, self.send.at[part, number], self.recv.at[part, number], device).start()

    def arrived(self, part, number, view):
        remote(view, view, self.send.at[part, number], self.recv.at[part, number], self.place.sibling()).wait_recv()

    def accumulate(self, target, sources, count):
        size = 4 * self.rows

        def body(number, carry):
            rows = pl.ds(pl.multiple_of(number * size, size), size)
            total = target[rows, :].astype(F32)
            for source in sources:
                total = total + source[rows, :].astype(F32)
            target[rows, :] = total.astype(BF16)
            return carry

        lax.fori_loop(0, count // 4, body, 0)

    def exchange(self):
        for slot, step in enumerate((2, 1, 3, 0)):
            for part in range(PARTS):
                third = lax.rem(self.mine(part)[0] + step, 4)
                source = self.view(part, third, count=16, ref=self.outgoing)
                self.start(part, slot, source, self.across(part, third), self.place.sibling())

    def far_out(self):
        for part in range(PARTS):
            third = lax.rem(self.mine(part)[0] + 2, 4)
            self.arrived(part, 0, self.across(part, third))
            self.accumulate(self.view(part, third, count=16), [self.across(part, third)], 16)
            for half, step in ((0, 1), (1, 3)):
                source = self.view(part, third, 2 * half, count=8)
                self.start(part, 4 + half, source, self.landing(0, part, half), self.place.peer(part, 2, step))

    def near_out(self):
        for part in range(PARTS):
            for half, step in ((0, 1), (1, 3)):
                third = lax.rem(self.mine(part)[0] + step, 4)
                self.arrived(part, 1 + half, self.across(part, third))
                self.arrived(part, 4 + half, self.landing(0, part, half))
                for side in (0, 1):
                    sources = [self.across(part, third, 2 * side, 8)]
                    if side == half:
                        sources.append(self.landing(0, part, half))
                    self.accumulate(self.view(part, third, 2 * side, count=8), sources, 8)
                source = self.view(part, third, count=16)
                self.start(part, 6 + half, source, self.landing(1, part, half), self.place.peer(part, 2, step))

    def second_out(self):
        for part in range(PARTS):
            third, second, first = self.mine(part)
            self.arrived(part, 3, self.across(part, third))
            for half in (0, 1):
                self.arrived(part, 6 + half, self.landing(1, part, half))
            sources = [self.across(part, third), self.landing(1, part, 0), self.landing(1, part, 1)]
            self.accumulate(self.view(part, third, count=16), sources, 16)
            for step in (1, 3, 2):
                source = self.view(part, third, lax.rem(second + step, 4), count=4)
                target = self.landing(2, part, step - 1)
                self.start(part, 7 + step, source, target, self.place.peer(part, 1, step))

    def first_out(self):
        for part in range(PARTS):
            third, second, first = self.mine(part)
            for step in (1, 3, 2):
                self.arrived(part, 7 + step, self.landing(2, part, step - 1))
            sources = [self.landing(2, part, slot) for slot in range(3)]
            self.accumulate(self.view(part, third, second, count=4), sources, 4)
            for step in (1, 3, 2):
                source = self.view(part, third, second, lax.rem(first + step, 4))
                target = self.landing(3, part, step - 1)
                self.start(part, 10 + step, source, target, self.place.peer(part, 0, step))

    def total(self, out, place):
        for part in range(PARTS):
            third, second, first = self.mine(part)
            for step in (1, 3, 2):
                self.arrived(part, 10 + step, self.landing(3, part, step - 1))
            value = self.view(part, third, second, first)[...].astype(F32)
            for slot in range(3):
                value = value + self.landing(3, part, slot)[...].astype(F32)
            out[place : place + self.rows, LANES * part : LANES * (part + 1)] = value

    def sent(self):
        for part in range(PARTS):
            for number in range(14):
                count = 16 if number < 4 else 8 if number < 6 else 16 if number < 8 else 4 if number < 11 else 1
                view = self.view(part, 0, count=count)
                remote(view, view, self.send.at[part, number], self.recv.at[part, number], self.place.sibling()).wait_send()


def pack_attention(early, grads, spread, rows_a_ref, core, ref):
    def body(number, carry):
        for inner in range(2):
            dp = (number * 2 + inner) * 2 + core
            rows = pl.ds(pl.multiple_of(dp * 48, 16), 48)
            for part in range(PARTS):
                columns = slice(LANES * part, LANES * (part + 1))
                pieces = [grad[rows, columns] for grad in grads]
                if part == 0:
                    tail = spread[pl.ds(pl.multiple_of(dp * 8, 8), 8), :]
                    tail = jnp.concatenate([tail, jnp.zeros((8, 128), F32)], axis=0)
                    tail = jnp.concatenate([tail, jnp.zeros((16, 128), F32)], axis=1)
                else:
                    tail = jnp.zeros((16, LANES), F32)
                blocks = dot(rows_a_ref[...], jnp.concatenate(pieces + [tail.astype(BF16)], axis=0), 0, 0).astype(BF16)
                for device, index in enumerate(chunk_blocks(part, dp)):
                    target = early.view(part, *index[2:], ref=ref)
                    target[...] = blocks[ROWS_A * device : ROWS_A * (device + 1)]
        return carry

    lax.fori_loop(0, 4, body, 0)


def pack_vectors(vectors, numbers):
    packed = jnp.zeros((128, 128), F32)
    for number in numbers:
        wide = 6 if number < 8 else 24
        mask = owner_mask(0 if number < 8 else 768 * (number - 8), wide)
        whole = jnp.where(mask, vectors[number], 0.0).astype(BF16)
        packed = packed + dot(whole, vector_lanes(number), 1, 1)
    return packed


def backward_kernel(
    lengths_ref, skip_ref, inverse, vector_in, rows_a_ref,
    frames_in, upstream_in, q_in, k_in, v_in, ctx_in, probs_in, branch_in, residual_in, attend_in, output_in, output_grad_in,
    feed_in,
    summed, frames_grad,
    own_f, own_a, outgoing_a, other_a, other_f, far_f, near_f, second_f, first_f, far_a, near_a, second_a, first_a,
    attend, output_weight, q_n, k_t, v_n, ctx_t, frames, branch, scaled_t, dk_n, dq_t, dv_t, score_grad, probs,
    ctx_grad, right, ones_mask, spread,
    send_a, recv_a, send_f, recv_f, local,
):
    place = Place()
    core = place.at[3]
    greet(place)
    pairs = (
        (output_in, output_weight), (branch_in, branch), (feed_in.at[pl.ds(pl.multiple_of(core * HALF_F, 16), HALF_F), :], own_f), (v_in, v_n), (ctx_in, ctx_t), (k_in, k_t), (q_in, q_n),
        (frames_in, frames), (attend_in, attend),
    )
    loads = [pltpu.make_async_copy(source, target, local.at[i]) for i, (source, target) in enumerate(pairs)]
    later = [
        pltpu.make_async_copy(output_grad_in, output_weight, local.at[9]),
        pltpu.make_async_copy(upstream_in, branch, local.at[10]),
        pltpu.make_async_copy(residual_in, ctx_grad, local.at[11]),
        pltpu.make_async_copy(scaled_t, frames_grad, local.at[12]),
    ]

    def prob_load(head, slot):
        return pltpu.make_async_copy(probs_in.at[head], probs.at[slot], local.at[13 + slot])

    for item in loads[:3]:
        item.start()
    for slot in range(3):
        prob_load(slot, slot).start()
    for item in loads[3:]:
        item.start()
    outgoing = feed_in.at[pl.ds(pl.multiple_of((1 - core) * HALF_F, 16), HALF_F), :]
    late = Scatter(place, own_f, outgoing, other_f, far_f, near_f, second_f, first_f, ROWS_F, send_f, recv_f)
    early = Scatter(
        place, own_a, outgoing_a, other_a,
        far_a, near_a, second_a, first_a, ROWS_A, send_a, recv_a,
    )
    lane = lax.broadcasted_iota(jnp.int32, (768, 128), 1)
    ones_mask[...] = jnp.where(lane < 2, 1.0, 0.0).astype(BF16)
    for side in range(2):
        right[side] = jnp.zeros((256, 768), BF16)
    meet()
    late.exchange()
    spread[...] = pack_vectors([vector(vector_in, i) for i in range(VECTORS)], range(2, VECTORS))
    loads[0].wait()
    loads[1].wait()
    ctx_grad[...] = dot(output_weight[...], branch[...], 1, 1)
    later[0].start()
    later[1].start()
    for item in loads[2:7]:
        item.wait()
    prob_load(0, 0).wait()
    prob_load(1, 1).wait()

    def score_stage(pair, side):
        head = pair * 2 + side
        rows = head_rows(head)
        factor = inverse[pl.ds(pl.multiple_of(head * 8, 8), 8), :][0:1]
        scaled = (ctx_grad[rows, :] * factor).astype(BF16)
        scaled_t[rows, :] = scaled
        right[side, 64 * side : 64 * side + 64] = scaled
        inner = jnp.sum(scaled.astype(F32) * ctx_t[rows, :].astype(F32), axis=0, keepdims=True)
        high = inner.astype(BF16).astype(F32)
        row = lax.broadcasted_iota(jnp.int32, (16, 768), 0)
        right[side, 128:144] = jnp.where(row == 0, -high, jnp.where(row == 1, high - inner, 0.0)).astype(BF16)
        left = jnp.concatenate([v_n[:, pair_lanes(pair)], ones_mask[...]], axis=1)
        score_grad[side] = (dot(left, right[side]) * probs[lax.rem(head, 3)].astype(F32)).astype(BF16)

    def use_stage(pair, side):
        head = pair * 2 + side
        rows = head_rows(head)
        lanes = pair_lanes(pair)
        dv_t[rows, :] = dot(scaled_t[rows, :], probs[lax.rem(head, 3)], 1, 1).astype(BF16)
        dq_t[rows, :] = (dot(k_t[rows, :], score_grad[side]) * SCALE).astype(BF16)
        keys = dot(score_grad[side], q_n[:, lanes]).astype(BF16)
        if side == 1:
            keys = jnp.where(lax.broadcasted_iota(jnp.int32, (768, 128), 1) < 64, dk_n[:, lanes], keys)
        dk_n[:, lanes] = keys

    def refill(head):
        @pl.when(head + 3 < 12)
        def _():
            prob_load(head + 3, lax.rem(head, 3)).start()

        @pl.when(head + 2 < 12)
        def _():
            prob_load(head + 2, lax.rem(head + 2, 3)).wait()

    score_stage(0, 0)
    steps = (None, late.far_out, late.near_out, None, late.second_out, late.first_out)

    def body(pair, carry):
        for number, step in enumerate(steps):
            if step is not None:
                pl.when(pair == number)(step)
        score_stage(pair, 1)
        use_stage(pair, 0)
        refill(pair * 2)
        score_stage(jnp.minimum(pair + 1, 5), 0)
        use_stage(pair, 1)
        refill(pair * 2 + 1)
        return carry

    lax.fori_loop(0, 6, body, 0)
    later[2].start()
    loads[7].wait()
    loads[8].wait()
    x = frames[...]
    queries, values = score_grad.at[0], score_grad.at[1]
    queries[...] = dq_t[...].T
    values[...] = dv_t[...].T
    grads = (k_t, q_n, v_n, output_weight)
    k_t[...] = dot(x, queries[...], 0, 0).astype(BF16)
    q_n[...] = dot(x, dk_n[...], 0, 0).astype(BF16)
    v_n[...] = dot(x, values[...], 0, 0).astype(BF16)
    sums = [jnp.sum(ref[...].astype(F32), axis=0, keepdims=True) for ref in (queries, values)]
    spread[...] = spread[...] + pack_vectors(sums, range(2))
    later[0].wait()
    pack_attention(early, grads, spread, rows_a_ref, 1 - core, outgoing_a)
    early.exchange()
    pack_attention(early, grads, spread, rows_a_ref, core, own_a)
    later[1].wait()
    later[2].wait()

    def finish_rows(block):
        rows = slice(256 * block, 256 * (block + 1))
        live = live_mask(lengths_ref, skip_ref, (256, 1), 256 * block)
        total = ctx_grad[rows, :] + dot(queries[rows, :], attend[0], 1, 1) + dot(dk_n[rows, :], attend[1], 1, 1)
        total = total + dot(values[rows, :], attend[2], 1, 1)
        scaled_t[rows, :] = jnp.where(live, total, branch[rows, :].astype(F32)).astype(BF16)

    early.far_out()
    finish_rows(0)
    early.near_out()
    finish_rows(1)
    finish_rows(2)
    later[3].start()
    late.total(summed, ROWS_A)
    early.second_out()
    early.first_out()
    early.total(summed, 0)
    later[3].wait()
    early.sent()
    late.sent()


def backward_call(*args):
    square = pltpu.VMEM((768, 768), BF16)

    def blocks(count, rows):
        return pltpu.VMEM((PARTS * count * rows, LANES), BF16)

    return pl.pallas_call(
        backward_kernel,
        out_shape=(shape(ROWS_ALL, 768, kind=F32), shape(768, 768)),
        in_specs=[SCALARS] * 2 + [WHOLE] * 3 + [ANYWHERE] * 13,
        out_specs=[WHOLE, ANYWHERE],
        scratch_shapes=[blocks(64, ROWS_F)] + [blocks(64, ROWS_A)] * 3 + [blocks(64, ROWS_F)]
        + [blocks(count, ROWS_F) for count in (16, 32, 12, 3)]
        + [blocks(count, ROWS_A) for count in (16, 32, 12, 3)]
        + [pltpu.VMEM((3, 768, 768), BF16)]
        + [square] * 11
        + [
            pltpu.VMEM((2, 768, 768), BF16), pltpu.VMEM((3, 768, 768), BF16), pltpu.VMEM((768, 768), F32),
            pltpu.VMEM((2, 256, 768), BF16), pltpu.VMEM((768, 128), BF16), pltpu.VMEM((128, 128), F32),
        ]
        + [pltpu.SemaphoreType.DMA((PARTS, 14))] * 4
        + [pltpu.SemaphoreType.DMA((16,))],
        compiler_params=pltpu.CompilerParams(collective_id=1, has_side_effects=True, vmem_limit_bytes=62 * 2**20),
        name="backward",
    )(*args)


def deliver_kernel(summed, query_out, key_out, value_out, output_out, expand_out, shrink_out, lanes_out):
    for number, target in enumerate((query_out, key_out, value_out, output_out)):
        target[...] = summed[6 * number : 6 * number + 6, :]
    for number in range(4):
        expand_out[:, 768 * number : 768 * (number + 1)] = summed[32 + 6 * number : 38 + 6 * number, :]
    shrink_out[...] = summed[56:80, :]
    lanes_out[...] = summed[24:25, 0:128]


def deliver(summed):
    return pl.pallas_call(
        deliver_kernel,
        out_shape=tuple(shape(*s, kind=F32) for s in ((6, 768),) * 4 + ((6, 3072), (24, 768), (1, 128))),
        in_specs=[WHOLE],
        out_specs=[WHOLE] * 7,
        name="deliver",
    )(summed)


PLACES = (0, 6, 12, 18, 24, 30, 36, 42, 48)


def local(
    frames,
    upstream,
    clip_lengths,
    clip_skip,
    query_weight,
    key_weight,
    value_weight,
    output_weight,
    query_bias,
    value_bias,
    output_bias,
    first_gain,
    first_shift,
    expand_weight,
    shrink_weight,
    expand_bias,
    shrink_bias,
    second_gain,
    second_shift,
):
    vectors = (
        query_bias, value_bias, output_bias, first_gain, first_shift, shrink_bias, second_gain, second_shift, expand_bias,
    )
    lanes = sum(
        jnp.pad(v.astype(F32), (place, 128 - place - v.shape[0])) for place, v in zip(PLACES, vectors, strict=True)
    )
    (
        vector_grad, encoded, residual_grad, branch_grad, ctx_t, inverse,
        attend, output, output_grad, q_n, k_t, v_n, probs, feed_grad,
    ) = forward_call(
        clip_lengths, clip_skip, frames, upstream,
        query_weight, key_weight, value_weight, output_weight, expand_weight, shrink_weight, lanes[None],
    )
    summed, frames_grad = backward_call(
        clip_lengths, clip_skip, inverse, vector_grad,
        jnp.asarray(attention_rows(), BF16),
        frames, upstream, q_n, k_t, v_n, ctx_t, probs, branch_grad, residual_grad, attend, output, output_grad, feed_grad,
    )
    query_sum, key_sum, value_sum, output_sum, expand_sum, shrink_sum, lanes = deliver(summed)
    sums = [lanes[0, place : place + v.shape[0]] for place, v in zip(PLACES, vectors, strict=True)]
    return (
        encoded, frames_grad, query_sum, key_sum, value_sum, output_sum, sums[0], sums[1], sums[2], sums[3], sums[4],
        expand_sum, shrink_sum, sums[8], sums[5], sums[6], sums[7],
    )


def solution(mesh):
    return jax.shard_map(
        local,
        mesh=mesh,
        in_specs=(
            P(("dp", "fsdp"), None),
            P(("dp", "fsdp"), None),
            P(("dp", "fsdp"), None),
            P(("dp", "fsdp"), None),
            P(("dp", "fsdp"), None),
            P(("dp", "fsdp"), None),
            P(("dp", "fsdp"), None),
            P(("dp", "fsdp"), None),
            P(("dp", "fsdp")),
            P(("dp", "fsdp")),
            P(("dp", "fsdp")),
            P(("dp", "fsdp")),
            P(("dp", "fsdp")),
            P(("dp", "fsdp"), None),
            P(("dp", "fsdp"), None),
            P(("dp", "fsdp")),
            P(("dp", "fsdp")),
            P(("dp", "fsdp")),
            P(("dp", "fsdp")),
        ),
        out_specs=(
            P(("dp", "fsdp"), None),
            P(("dp", "fsdp"), None),
            P(("dp", "fsdp"), None),
            P(("dp", "fsdp"), None),
            P(("dp", "fsdp"), None),
            P(("dp", "fsdp"), None),
            P(("dp", "fsdp")),
            P(("dp", "fsdp")),
            P(("dp", "fsdp")),
            P(("dp", "fsdp")),
            P(("dp", "fsdp")),
            P(("dp", "fsdp"), None),
            P(("dp", "fsdp"), None),
            P(("dp", "fsdp")),
            P(("dp", "fsdp")),
            P(("dp", "fsdp")),
            P(("dp", "fsdp")),
        ),
        check_vma=False,
    )
```

```python
import functools
import math

import jax
import jax.numpy as jnp
import numpy as np
from jax import lax
from jax.experimental import pallas as pl
from jax.experimental.pallas import tpu as pltpu
from jax.sharding import PartitionSpec as P

epsilon = 1e-05

SCALE = 0.125
EXCLUDED = -1e30
F32 = jnp.float32
BF16 = jnp.bfloat16
WHOLE = pl.BlockSpec(memory_space=pltpu.VMEM)
SCALARS = pl.BlockSpec(memory_space=pltpu.SMEM)
ANYWHERE = pl.BlockSpec(memory_space=pl.ANY)
VEC_QUERY, VEC_VALUE, VEC_OUTPUT, VEC_GAIN1, VEC_SHIFT1, VEC_SHRINK, VEC_GAIN2, VEC_SHIFT2, VEC_EXPAND = range(9)


def dot(left, right, a=1, b=0):
    return lax.dot_general(left, right, (((a,), (b,)), ((), ())), preferred_element_type=F32)


def shape(*sizes, kind=jnp.bfloat16):
    return jax.ShapeDtypeStruct(sizes, kind)


def segments(lengths_ref, axis, extent, first=0):
    place = lax.broadcasted_iota(jnp.int32, extent, axis) + first
    first_end = lengths_ref[0, 0]
    second_end = first_end + lengths_ref[0, 1]
    return jnp.where(place < first_end, 0, jnp.where(place < second_end, 1, 2))


def live_mask(lengths_ref, skip_ref, extent, first):
    segment = segments(lengths_ref, 0, extent, first)
    dropped = jnp.where(segment == 0, skip_ref[0, 0], jnp.where(segment == 1, skip_ref[0, 1], 1))
    return dropped == 0


def vector(ref, number):
    return ref[0:1, 768 * number : 768 * (number + 1)]


def head_rows(head):
    return pl.ds(pl.multiple_of(head * 64, 64), 64)


def pair_lanes(pair):
    return pl.ds(pl.multiple_of(pair * 128, 128), 128)


def project(frames, attend, vectors, q_n, k_n, v_n, q_t, k_t, v_t):
    x = frames[...]
    q_n[...] = ((dot(x, attend[0]) + vector(vectors, VEC_QUERY)) * SCALE).astype(BF16)
    q_t[...] = q_n[...].T
    k_n[...] = dot(x, attend[1]).astype(BF16)
    k_t[...] = k_n[...].T
    v_n[...] = (dot(x, attend[2]) + vector(vectors, VEC_VALUE)).astype(BF16)
    v_t[...] = v_n[...].T


def mask_operands(lengths_ref, right, k_mask):
    lane = lax.broadcasted_iota(jnp.int32, (768, 128), 1)
    k_mask[...] = jnp.where(lane == segments(lengths_ref, 0, (768, 128)), 1.0, 0.0).astype(BF16)
    row = lax.broadcasted_iota(jnp.int32, (128, 768), 0)
    other = (row < 3) & (row != segments(lengths_ref, 1, (128, 768)))
    other = jnp.where(other, EXCLUDED, 0.0).astype(BF16)
    for side in range(2):
        right[side, 128:256] = other
        right[side, 64 * (1 - side) : 64 * (1 - side) + 64] = jnp.zeros((64, 768), BF16)


def score_stage(pair, side, q_t, k_n, k_mask, right, scores, tops):
    left = jnp.concatenate([k_n[:, pair_lanes(pair)], k_mask[...]], axis=1)
    right[side, 64 * side : 64 * side + 64] = q_t[head_rows(pair * 2 + side), :]
    values = dot(left, right[side])
    scores[side] = values
    tops[side] = jnp.broadcast_to(jnp.max(values, axis=0, keepdims=True), (8, 768))


def prob_stage(pair, side, v_t, scores, tops, probs, inverse, ctx_t):
    head = pair * 2 + side
    rows = head_rows(head)
    left = jnp.concatenate([v_t[rows, :], jnp.ones((16, 768), BF16)], axis=0)
    raised = jnp.exp(scores[side] - tops[side, 0:1]).astype(BF16)
    probs[side][...] = raised
    total = dot(left, raised)
    factor = 1.0 / total[64:65]
    inverse[pl.ds(pl.multiple_of(head * 8, 8), 8), :] = jnp.broadcast_to(factor, (8, 768))
    ctx_t[rows, :] = (total[:64] * factor).astype(BF16)


def gelu_pair(v):
    base = 1.0 + (0.3275911 / math.sqrt(2.0)) * jnp.abs(v)
    t = pl.reciprocal(base, approx=True)
    t = t * (2.0 - base * t)
    e = jnp.exp2((v * v) * (-0.5 / math.log(2.0)))
    poly = t * (0.127414796 + t * (-0.142248368 + t * (0.7107068705 + t * (-0.7265760135 + t * 0.5307027145))))
    tail = poly * e
    phi = jnp.where(v >= 0, 1.0 - tail, tail)
    return v * phi, phi + v * e * (1.0 / math.sqrt(2.0 * math.pi))


def normalise(values):
    centered = values - jnp.mean(values, axis=-1, keepdims=True)
    scale = lax.rsqrt(jnp.mean(centered * centered, axis=-1, keepdims=True) + epsilon)
    return centered * scale, scale


def norm_back(cotangent, gain, normed, scale):
    c = cotangent * gain
    return scale * (
        c - jnp.mean(c, axis=-1, keepdims=True) - normed * jnp.mean(c * normed, axis=-1, keepdims=True)
    )


MESH = pl.DeviceIdType.MESH
ROWS_A = 32
ROWS_F = 48
ROWS_ALL = ROWS_A + ROWS_F
LANES = 256
PARTS = 3
HALF_F = PARTS * 64 * ROWS_F
VECTORS = 12
BIAS_OUT = 208


def attention_rows():
    table = np.zeros((BIAS_OUT, 8 * ROWS_A), np.float32)
    for row in range(192):
        matrix, inner = divmod(row, 48)
        device, lane = divmod(inner, 6)
        table[row, device * ROWS_A + 6 * matrix + lane] = 1
    for device in range(8):
        table[192 + device, device * ROWS_A + 24] = 1
    return table


def expand_rows():
    table = np.zeros((192, 256), np.float32)
    for row in range(192):
        matrix, inner = divmod(row, 48)
        device, lane = divmod(inner, 6)
        table[row, 32 * device + 6 * matrix + lane] = 1
    return table


def shrink_rows():
    table = np.zeros((192, 256), np.float32)
    for row in range(192):
        device, lane = divmod(row, 24)
        table[row, 32 * device + 8 + lane] = 1
    return table


def vector_lanes(number):
    lane = lax.broadcasted_iota(jnp.int32, (128, 768), 0)
    column = lax.broadcasted_iota(jnp.int32, (128, 768), 1)
    if number < 8:
        wanted = column - 6 * ((column * 10923) >> 16) + 6 * number
    else:
        wanted = column - 24 * ((column * 2731) >> 16) + 48
    return jnp.where(lane == wanted, 1.0, 0.0).astype(BF16)


def owner_mask(first, wide):
    device = lax.broadcasted_iota(jnp.int32, (128, 768), 0)
    column = lax.broadcasted_iota(jnp.int32, (128, 768), 1) + first
    low = device * wide
    return (column >= low) & (column < low + wide)


def position():
    dp = lax.axis_index("dp")
    fsdp = lax.axis_index("fsdp")
    core = lax.rem(dp, 2)
    y = lax.rem(dp // 2, 4)
    z = (dp // 8) * 2 + fsdp // 4
    x = lax.rem(fsdp, 4)
    return x, y, z, core


def device_of(x, y, z, core):
    return (((z // 2) * 4 + y) * 2 + core, lax.rem(z, 2) * 4 + x)


AXES = ((0, 1, 2), (1, 2, 0), (2, 0, 1))


class Place:
    def __init__(self):
        self.at = position()

    def along(self, part, stage):
        return self.at[AXES[part][stage]]

    def peer(self, part, stage, step):
        where = list(self.at)
        axis = AXES[part][stage]
        where[axis] = lax.rem(where[axis] + step, 4)
        return device_of(*where)

    def sibling(self):
        x, y, z, core = self.at
        return device_of(x, y, z, 1 - core)


def greet(place):
    targets = [place.sibling()]
    for axis in range(3):
        for step in (1, 2, 3):
            where = list(place.at)
            where[axis] = lax.rem(where[axis] + step, 4)
            targets.append(device_of(*where))
    for target in targets:
        pl.semaphore_signal(pltpu.get_barrier_semaphore(), inc=1, device_id=target, device_id_type=MESH)


def meet():
    pl.semaphore_wait(pltpu.get_barrier_semaphore(), 10)


def remote(source, target, send, receive, device):
    return pltpu.make_async_remote_copy(
        src_ref=source,
        dst_ref=target,
        send_sem=send,
        recv_sem=receive,
        device_id=device,
        device_id_type=MESH,
    )


def chunk_blocks(part, high, y, core):
    blocks = []
    for low in range(2):
        for x in range(4):
            where = (x, y, high * 2 + low)
            first, second, third = (where[a] for a in AXES[part])
            blocks.append((part, core, third, second, first))
    return blocks


def rows_at(ref, start, count):
    if isinstance(start, int):
        return ref.at[start : start + count, :]
    return ref.at[pl.ds(pl.multiple_of(start, 16), count), :]


class Gather:
    def __init__(self, place, held, rows, send, recv):
        self.place, self.held, self.rows, self.send, self.recv = place, held, rows, send, recv
        self.core = place.at[3]

    def view(self, part, core, third, second=0, first=0, count=1):
        start = (((core * PARTS + part) * 4 + third) * 4 + second) * 4 + first
        return rows_at(self.held, start * self.rows, count * self.rows)

    def mine(self, part):
        return tuple(self.place.along(part, stage) for stage in (2, 1, 0))

    def copy(self, part, number, view, device):
        return remote(view, view, self.send.at[part, number], self.recv.at[part, number], device)

    def start(self, part, number, view, device):
        self.copy(part, number, view, device).start()

    def arrived(self, part, number, view):
        self.copy(part, number, view, self.place.sibling()).wait_recv()

    def block(self, part, third, second, first):
        return self.view(part, self.core, third, second, first)

    def two(self, part, third, second, half):
        return self.view(part, self.core, third, second, 2 * half, 2)

    def eight(self, part, core, third, half):
        return self.view(part, core, third, 2 * half, 0, 8)

    def first(self):
        for part in range(PARTS):
            view = self.block(part, *self.mine(part))
            for step in (1, 3, 2):
                self.start(part, step - 1, view, self.place.peer(part, 0, step))

    def second(self):
        for part in range(PARTS):
            third, second, first = self.mine(part)
            for step in (1, 3, 2):
                self.arrived(part, step - 1, self.block(part, third, second, lax.rem(first + 4 - step, 4)))
            ahead, behind = self.place.peer(part, 1, 1), self.place.peer(part, 1, 3)
            for half in (0, 1):
                self.start(part, 3 + half, self.two(part, third, second, half), ahead)
                self.start(part, 6 - half, self.two(part, third, second, 1 - half), behind)

    def second_on(self):
        for part in range(PARTS):
            third, second, first = self.mine(part)
            ahead, behind = self.place.peer(part, 1, 1), self.place.peer(part, 1, 3)
            view = self.two(part, third, lax.rem(second + 3, 4), 0)
            self.arrived(part, 3, view)
            self.start(part, 7, view, ahead)
            view = self.two(part, third, lax.rem(second + 1, 4), 1)
            self.arrived(part, 6, view)
            self.start(part, 8, view, behind)

    def third(self):
        for part in range(PARTS):
            third, second, first = self.mine(part)
            self.arrived(part, 4, self.two(part, third, lax.rem(second + 3, 4), 1))
            self.arrived(part, 5, self.two(part, third, lax.rem(second + 1, 4), 0))
            for half in (0, 1):
                self.arrived(part, 7 + half, self.two(part, third, lax.rem(second + 2, 4), half))
            ahead, behind = self.place.peer(part, 2, 1), self.place.peer(part, 2, 3)
            for half in (0, 1):
                self.start(part, 9 + half, self.eight(part, self.core, third, half), ahead)
                self.start(part, 12 - half, self.eight(part, self.core, third, 1 - half), behind)
            self.start(part, 15, self.view(part, self.core, third, count=16), self.place.sibling())

    def third_on(self):
        for part in range(PARTS):
            third, second, first = self.mine(part)
            ahead, behind = self.place.peer(part, 2, 1), self.place.peer(part, 2, 3)
            view = self.eight(part, self.core, lax.rem(third + 3, 4), 0)
            self.arrived(part, 9, view)
            self.start(part, 13, view, ahead)
            self.start(part, 16, view, self.place.sibling())
            view = self.eight(part, self.core, lax.rem(third + 1, 4), 1)
            self.arrived(part, 12, view)
            self.start(part, 14, view, behind)
            self.start(part, 17, view, self.place.sibling())

    def near_over(self):
        for part in range(PARTS):
            third, second, first = self.mine(part)
            view = self.eight(part, self.core, lax.rem(third + 3, 4), 1)
            self.arrived(part, 10, view)
            self.start(part, 18, view, self.place.sibling())
            view = self.eight(part, self.core, lax.rem(third + 1, 4), 0)
            self.arrived(part, 11, view)
            self.start(part, 19, view, self.place.sibling())

    def far_over(self):
        for part in range(PARTS):
            third, second, first = self.mine(part)
            for half in (0, 1):
                view = self.eight(part, self.core, lax.rem(third + 2, 4), half)
                self.arrived(part, 13 + half, view)
                self.start(part, 20 + half, view, self.place.sibling())

    def finish(self):
        other = 1 - self.core
        for part in range(PARTS):
            third, second, first = self.mine(part)
            self.arrived(part, 15, self.view(part, other, third, count=16))
            self.arrived(part, 16, self.eight(part, other, lax.rem(third + 3, 4), 0))
            self.arrived(part, 17, self.eight(part, other, lax.rem(third + 1, 4), 1))
            self.arrived(part, 18, self.eight(part, other, lax.rem(third + 3, 4), 1))
            self.arrived(part, 19, self.eight(part, other, lax.rem(third + 1, 4), 0))
            for half in (0, 1):
                self.arrived(part, 20 + half, self.eight(part, other, lax.rem(third + 2, 4), half))

    def sent(self):
        for part in range(PARTS):
            for number in range(22):
                if number < 3:
                    view = self.block(part, 0, 0, 0)
                elif number < 9:
                    view = self.two(part, 0, 0, 0)
                elif number == 15:
                    view = self.view(part, self.core, 0, count=16)
                else:
                    view = self.eight(part, self.core, 0, 0)
                self.copy(part, number, view, self.place.sibling()).wait_send()


def unpack_attention(held, rows_a_ref, attend, output, vectors, spread):
    def body(y, carry):
        for high, core in ((0, 0), (0, 1), (1, 0), (1, 1)):
            start = 8 * high + core
            rows = pl.ds(pl.multiple_of(48 * start + 96 * y, 16), 48)
            for part in range(PARTS):
                columns = slice(LANES * part, LANES * (part + 1))
                blocks = jnp.concatenate([held.view(*index)[...] for index in chunk_blocks(part, high, y, core)], axis=0)
                blocks = dot(rows_a_ref[...], blocks)
                if part == 0:
                    spread[pl.ds(pl.multiple_of(8 * start + 16 * y, 8), 8), :] = blocks[192:200, :128]
                blocks = blocks.astype(BF16)
                for matrix in range(3):
                    attend[matrix, rows, columns] = blocks[48 * matrix : 48 * (matrix + 1)]
                output[rows, columns] = blocks[144:192]
        return carry

    lax.fori_loop(0, 4, body, 0)

    packed = spread[...].astype(BF16)
    for number in range(VECTORS):
        wide = 6 if number < 8 else 24
        mask = owner_mask(0 if number < 8 else 768 * (number - 8), wide)
        columns = slice(768 * number, 768 * (number + 1))
        whole = dot(packed, vector_lanes(number))
        vectors[:, columns] = jnp.sum(jnp.where(mask, whole, 0.0), axis=0, keepdims=True)


def unpack_feed(held, rows_e_ref, rows_s_ref, expand, shrink):
    def body(y, carry):
        for high, core in ((0, 0), (0, 1), (1, 0), (1, 1)):
            start = 8 * high + core
            rows = pl.ds(pl.multiple_of(48 * start + 96 * y, 16), 48)
            for part in range(PARTS):
                columns = slice(LANES * part, LANES * (part + 1))
                blocks = [held.view(*index)[...] for index in chunk_blocks(part, high, y, core)]
                first = dot(rows_e_ref[...], jnp.concatenate([b[:32] for b in blocks], axis=0)).astype(BF16)
                second = dot(rows_s_ref[...], jnp.concatenate([b[16:] for b in blocks], axis=0)).astype(BF16)
                for matrix in range(4):
                    expand[rows, 768 * matrix + LANES * part : 768 * matrix + LANES * (part + 1)] = first[
                        48 * matrix : 48 * (matrix + 1)
                    ]
                shrink[pl.ds(pl.multiple_of(192 * start + 384 * y, 16), 192), columns] = second
        return carry

    lax.fori_loop(0, 4, body, 0)


def pack_feed(held, back_e_ref, back_s_ref, expand, shrink):
    def body(y, carry):
        for high, core in ((0, 0), (0, 1), (1, 0), (1, 1)):
            start = 8 * high + core
            rows = pl.ds(pl.multiple_of(48 * start + 96 * y, 16), 48)
            for part in range(PARTS):
                pieces = [
                    expand[rows, 768 * matrix + LANES * part : 768 * matrix + LANES * (part + 1)] for matrix in range(4)
                ]
                first = dot(back_e_ref[...], jnp.concatenate(pieces, axis=0))
                values = shrink[pl.ds(pl.multiple_of(192 * start + 384 * y, 16), 192), LANES * part : LANES * (part + 1)]
                second = dot(back_s_ref[...], values)
                for device, index in enumerate(chunk_blocks(part, high, y, core)):
                    at = 32 * device
                    block = held.view(*index)
                    block[0:16, :] = first[at : at + 16].astype(BF16)
                    block[16:32, :] = (first[at + 16 : at + 32] + second[at : at + 16]).astype(BF16)
                    block[32:48, :] = second[at + 16 : at + 32].astype(BF16)
        return carry

    lax.fori_loop(0, 4, body, 0)


def forward_kernel(
    lengths_ref, skip_ref, frames_in, upstream_in,
    query_in, key_in, value_in, output_in, expand_in, shrink_in,
    *rest,
):
    forward_body(
        lengths_ref, skip_ref, frames_in, upstream_in, query_in, key_in, value_in, output_in, expand_in, shrink_in,
        rest[:9], *rest[9:],
    )


def forward_body(
    lengths_ref, skip_ref, frames_in, upstream_in, query_in, key_in, value_in, output_in, expand_in, shrink_in,
    vectors_in, rows_a_ref, rows_e_ref, rows_s_ref, back_e_ref, back_s_ref,
    vector_out, encoded_out, residual_out, branch_out, ctx_out, inverse_out,
    attend_out, weight_out, output_out, q_out, k_out, v_out, probs_out, feed_out,
    held_a, held_f, block_ref, spread, attend, output_weight, expand, shrink, vectors,
    frames, upstream, residual_grad, branch_grad, ctx_t, inverse,
    send_a, recv_a, send_f, recv_f, local,
):
    place = Place()
    core = place.at[3]
    greet(place)
    frames_load = pltpu.make_async_copy(frames_in, frames, local.at[32])
    upstream_load = pltpu.make_async_copy(upstream_in, upstream, local.at[33])
    frames_load.start()
    upstream_load.start()
    for number, source in enumerate((query_in, key_in, value_in, output_in)):
        block_ref[6 * number : 6 * number + 6, :] = source[...].astype(F32)
    block_ref[24:32, :] = jnp.zeros((8, 768), F32)
    for at, ref in zip(PLACES, vectors_in, strict=True):
        size = ref.shape[0]
        block_ref[24:25, at : at + size] = ref[...].astype(F32).reshape(1, size)
    for number in range(4):
        block_ref[32 + 6 * number : 38 + 6 * number, :] = expand_in[:, 768 * number : 768 * (number + 1)].astype(F32)
    block_ref[56:80, :] = shrink_in[...].astype(F32)
    early = Gather(place, held_a, ROWS_A, send_a, recv_a)
    late = Gather(place, held_f, ROWS_F, send_f, recv_f)
    for part in range(PARTS):
        third, second, first = early.mine(part)
        values = block_ref[:, LANES * part : LANES * (part + 1)].astype(BF16)
        early.block(part, third, second, first)[...] = values[:ROWS_A]
        late.block(part, third, second, first)[...] = values[ROWS_A:]
    meet()
    early.first()
    late.first()
    early.second()
    early.second_on()
    early.third()
    late.second()
    early.third_on()
    late.second_on()
    early.near_over()
    early.far_over()
    late.third()
    early.finish()
    unpack_attention(early, rows_a_ref, attend, output_weight, vectors, spread)
    keep = [
        pltpu.make_async_copy(attend, attend_out, local.at[0]),
        pltpu.make_async_copy(output_weight, weight_out, local.at[1]),
    ]
    for item in keep:
        item.start()
    late.third_on()

    def attention(right, k_mask, scores, tops):
        q_n, k_n, v_n, q_t = (expand.at[:, 768 * i : 768 * (i + 1)] for i in range(4))
        k_t, v_t, *probs = (shrink.at[768 * i : 768 * (i + 1), :] for i in range(4))
        frames_load.wait()
        project(frames, attend, vectors, q_n, k_n, v_n, q_t, k_t, v_t)
        hold = [
            pltpu.make_async_copy(q_n, q_out, local.at[2]),
            pltpu.make_async_copy(k_t, k_out, local.at[3]),
            pltpu.make_async_copy(v_n, v_out, local.at[4]),
        ]
        for item in hold:
            item.start()
        mask_operands(lengths_ref, right, k_mask)
        score_stage(0, 0, q_t, k_n, k_mask, right, scores, tops)

        def away(head, side):
            return pltpu.make_async_copy(probs[side], probs_out.at[head], local.at[5 + side])

        def body(pair, carry):
            @pl.when(pair > 0)
            def _():
                away(0, 0).wait()

            @pl.when(pair == 1)
            def _():
                late.near_over()

            @pl.when(pair == 3)
            def _():
                late.far_over()

            score_stage(pair, 1, q_t, k_n, k_mask, right, scores, tops)
            prob_stage(pair, 0, v_t, scores, tops, probs, inverse, ctx_t)
            away(pair * 2, 0).start()

            @pl.when(pair > 0)
            def _():
                away(0, 1).wait()

            score_stage(jnp.minimum(pair + 1, 5), 0, q_t, k_n, k_mask, right, scores, tops)
            prob_stage(pair, 1, v_t, scores, tops, probs, inverse, ctx_t)
            away(pair * 2 + 1, 1).start()
            return carry

        lax.fori_loop(0, 6, body, 0)
        for side in range(2):
            away(0, side).wait()
        for item in hold:
            item.wait()

    square = pltpu.VMEM((768, 768), BF16)
    pl.run_scoped(
        attention, pltpu.VMEM((2, 256, 768), BF16), pltpu.VMEM((768, 128), BF16),
        pltpu.VMEM((2, 768, 768), F32), pltpu.VMEM((2, 8, 768), F32),
    )
    saves = [
        pltpu.make_async_copy(ctx_t, ctx_out, local.at[34]),
        pltpu.make_async_copy(inverse, inverse_out, local.at[35]),
        pltpu.make_async_copy(frames, encoded_out, local.at[36]),
        pltpu.make_async_copy(residual_grad, residual_out, local.at[37]),
        pltpu.make_async_copy(branch_grad, branch_out, local.at[38]),
    ]
    saves[0].start()
    saves[1].start()
    late.finish()
    late.sent()
    unpack_feed(late, rows_e_ref, rows_s_ref, expand, shrink)
    upstream_load.wait()

    def feed(normed, scales, hidden, raw):
        feed_forward(
            lengths_ref, skip_ref, frames, upstream, ctx_t, output_weight, expand, shrink, vectors,
            residual_grad, branch_grad, output_out, vector_out,
            normed, scales, hidden, held_f, raw, branch_grad, local, saves,
            lambda: pack_feed(late, back_e_ref, back_s_ref, expand, shrink),
            pltpu.make_async_copy(held_f, feed_out, local.at[7]),
        )

    pl.run_scoped(
        feed, pltpu.VMEM((768, 768), F32), pltpu.VMEM((768, 128), F32), square,
        pltpu.VMEM((2, 768, 512), F32),
    )
    for item in keep + saves:
        item.wait()
    early.sent()


def feed_forward(
    lengths_ref, skip_ref, frames, upstream, ctx_t, output_weight, expand, shrink, vectors,
    acc, branch_grad, output_out, vector_out,
    normed, scales, hidden, panels, raw, summed_grad, local, saves, pack, feed_move,
):
    def rows_of(block):
        return slice(256 * block, 256 * (block + 1))

    def wide_columns(chunk):
        return pl.ds(pl.multiple_of(768 * chunk, 768), 768)

    for block in range(3):
        rows = rows_of(block)
        values = (
            dot(ctx_t[:, rows], output_weight[...], 0, 0) + frames[rows, :].astype(F32) + vector(vectors, VEC_OUTPUT)
        )
        unit, scale = normalise(values)
        normed[rows, :] = unit
        scales[rows, :] = jnp.broadcast_to(scale, (256, 128))
        hidden[rows, :] = (unit * vector(vectors, VEC_GAIN1) + vector(vectors, VEC_SHIFT1)).astype(BF16)

    def panel(kind, number, block=None):
        start = (kind * 12 + number) * 768
        if block is None:
            return panels.at[pl.ds(pl.multiple_of(start, 256), 768), :]
        return panels.at[pl.ds(pl.multiple_of(start + 256 * block, 256), 256), :]

    def load(kind, first, count, block=None):
        return jnp.concatenate([panel(kind, first + i, block)[...] for i in range(count)], axis=1)

    def save(kind, first, count, block, values):
        for i in range(count):
            panel(kind, first + i, block)[...] = values[:, 256 * i : 256 * (i + 1)].astype(BF16)

    def narrow_columns(chunk):
        return pl.ds(pl.multiple_of(512 * chunk, 512), 512)

    def expand_stage(chunk, slot):
        raw[slot] = dot(hidden[...], expand[:, narrow_columns(chunk)])

    def gelu_stage(chunk, slot):
        bias = vectors[0:1, pl.ds(pl.multiple_of(768 * VEC_EXPAND + 512 * chunk, 512), 512)]
        for block in range(3):
            rows = rows_of(block)
            value, derivative = gelu_pair(raw[slot, rows] + bias)
            save(0, 2 * chunk, 2, block, value)
            save(1, 2 * chunk, 2, block, derivative)

    def shrink_stage(chunk, first=False):
        columns = narrow_columns(chunk)
        for block in range(3):
            rows = rows_of(block)
            product = dot(load(0, 2 * chunk, 2, block), shrink[columns, :])
            acc[rows, :] = product if first else acc[rows, :] + product

    expand_stage(0, 0)
    expand_stage(1, 1)
    gelu_stage(0, 0)
    acc[...] = jnp.zeros((768, 768), F32)

    def chunks(number, carry):
        for inner in (1, 2):
            chunk = 2 * number + inner
            expand_stage(chunk + 1, 1 - inner % 2)
            gelu_stage(chunk, inner % 2)
            shrink_stage(chunk - 1)
        return carry

    for number in range(2):
        chunks(number, 0)
    gelu_stage(5, 1)
    shrink_stage(4)
    shrink_stage(5)

    sums = [jnp.zeros((1, 768), F32) for _ in range(3)]
    for block in range(3):
        rows = rows_of(block)
        first = normed[rows, :] * vector(vectors, VEC_GAIN1) + vector(vectors, VEC_SHIFT1)
        unit, scale = normalise(first + acc[rows, :] + vector(vectors, VEC_SHRINK))
        result = unit * vector(vectors, VEC_GAIN2) + vector(vectors, VEC_SHIFT2)
        live = live_mask(lengths_ref, skip_ref, (256, 1), 256 * block)
        frames[rows, :] = jnp.where(live, result, frames[rows, :].astype(F32)).astype(BF16)
        cotangent = jnp.where(live, upstream[rows, :].astype(F32), 0.0)
        grad = norm_back(cotangent, vector(vectors, VEC_GAIN2), unit, scale)
        acc[rows, :] = grad
        summed_grad[rows, :] = grad.astype(BF16)
        sums[0] = sums[0] + jnp.sum(cotangent * unit, axis=0, keepdims=True)
        sums[1] = sums[1] + jnp.sum(cotangent, axis=0, keepdims=True)
        sums[2] = sums[2] + jnp.sum(grad, axis=0, keepdims=True)

    saves[2].start()

    def put(number, value):
        vector_out[0:1, 768 * number : 768 * (number + 1)] = value

    put(VEC_QUERY, jnp.zeros((1, 768), F32))
    put(VEC_VALUE, jnp.zeros((1, 768), F32))
    put(VEC_GAIN2, sums[0])
    put(VEC_SHIFT2, sums[1])
    put(VEC_SHRINK, sums[2])

    def shrink_back(chunk, carry):
        columns = wide_columns(chunk)
        total = jnp.zeros((1, 768), F32)
        for block in range(3):
            rows = rows_of(block)
            grad = dot(summed_grad[rows, :], shrink[columns, :], 1, 1) * load(1, 3 * chunk, 3, block).astype(F32)
            total = total + jnp.sum(grad, axis=0, keepdims=True)
            save(1, 3 * chunk, 3, block, grad)
        vector_out[0:1, pl.ds(pl.multiple_of(768 * (VEC_EXPAND + chunk), 768), 768)] = total
        for block in range(3):
            part = pl.ds(pl.multiple_of(768 * chunk + 256 * block, 256), 256)
            shrink[part, :] = dot(panel(0, 3 * chunk + block)[...], summed_grad[...], 0, 0).astype(BF16)
        return carry

    for chunk in range(4):
        shrink_back(chunk, 0)

    def expand_back(chunk, carry):
        columns = wide_columns(chunk)
        for block in range(3):
            rows = rows_of(block)
            acc[rows, :] = acc[rows, :] + dot(load(1, 3 * chunk, 3, block), expand[:, columns], 1, 1)
        for block in range(3):
            part = pl.ds(pl.multiple_of(768 * chunk + 256 * block, 256), 256)
            expand[:, part] = dot(hidden[...], panel(1, 3 * chunk + block)[...], 0, 0).astype(BF16)
        return carry

    for chunk in range(4):
        expand_back(chunk, 0)
    pack()
    feed_move.start()
    sums = [jnp.zeros((1, 768), F32) for _ in range(3)]
    for block in range(3):
        rows = rows_of(block)
        grad = acc[rows, :]
        unit = normed[rows, :]
        back = norm_back(grad, vector(vectors, VEC_GAIN1), unit, scales[rows, 0:1])
        acc[rows, :] = back
        branch_grad[rows, :] = back.astype(BF16)
        sums[0] = sums[0] + jnp.sum(grad * unit, axis=0, keepdims=True)
        sums[1] = sums[1] + jnp.sum(grad, axis=0, keepdims=True)
        sums[2] = sums[2] + jnp.sum(back, axis=0, keepdims=True)
    saves[3].start()
    saves[4].start()
    put(VEC_GAIN1, sums[0])
    put(VEC_SHIFT1, sums[1])
    put(VEC_OUTPUT, sums[2])
    hidden[...] = dot(ctx_t[...], branch_grad[...]).astype(BF16)
    move = pltpu.make_async_copy(hidden, output_out, local.at[31])
    move.start()
    feed_move.wait()
    move.wait()


def forward_call(lengths, skip, frames, upstream, *shards):
    square = shape(768, 768)
    return pl.pallas_call(
        forward_kernel,
        out_shape=(
            shape(1, VECTORS * 768, kind=F32), square, shape(768, 768, kind=F32), square, square,
            shape(96, 768, kind=F32), shape(3, 768, 768), square, square, square, square, square, shape(12, 768, 768),
            shape(PARTS * 128 * ROWS_F, LANES),
        ),
        in_specs=[SCALARS] * 2 + [ANYWHERE] * 2 + [WHOLE] * 20,
        out_specs=[WHOLE] + [ANYWHERE] * 13,
        scratch_shapes=[
            pltpu.VMEM((PARTS * 128 * ROWS_A, LANES), BF16),
            pltpu.VMEM((PARTS * 128 * ROWS_F, LANES), BF16),
            pltpu.VMEM((ROWS_ALL, 768), F32),
            pltpu.VMEM((128, 128), F32),
            pltpu.VMEM((3, 768, 768), BF16),
            pltpu.VMEM((768, 768), BF16),
            pltpu.VMEM((768, 3072), BF16),
            pltpu.VMEM((3072, 768), BF16),
            pltpu.VMEM((1, VECTORS * 768), F32),
        ]
        + [pltpu.VMEM((768, 768), kind) for kind in (BF16, BF16, F32, BF16, BF16)]
        + [pltpu.VMEM((96, 768), F32)]
        + [pltpu.SemaphoreType.DMA((PARTS, 22))] * 4
        + [pltpu.SemaphoreType.DMA((39,))],
        compiler_params=pltpu.CompilerParams(collective_id=0, has_side_effects=True, vmem_limit_bytes=62 * 2**20),
        name="forward",
    )(
        lengths, skip, frames, upstream, *shards,
        jnp.asarray(attention_rows(), BF16), jnp.asarray(expand_rows(), BF16), jnp.asarray(shrink_rows(), BF16),
        jnp.asarray(expand_rows().T, BF16), jnp.asarray(shrink_rows().T, BF16),
    )


class Scatter:
    def __init__(self, place, own, outgoing, other, far, near, second, first, rows, send, recv):
        self.place, self.own, self.outgoing, self.other = place, own, outgoing, other
        self.rows, self.send, self.recv = rows, send, recv
        self.buffers = (far, near, second, first)

    def mine(self, part):
        return tuple(self.place.along(part, stage) for stage in (2, 1, 0))

    def rows_of(self, ref, start, count):
        return rows_at(ref, start * self.rows, count * self.rows)

    def view(self, part, third, second=0, first=0, count=1, ref=None):
        return self.rows_of(self.own if ref is None else ref, ((part * 4 + third) * 4 + second) * 4 + first, count)

    def across(self, part, third, second=0, count=16):
        return self.view(part, third, second, 0, count, self.other)

    def landing(self, kind, part, slot):
        slots, count = ((2, 8), (2, 16), (3, 4), (3, 1))[kind]
        return self.rows_of(self.buffers[kind], (part * slots + slot) * count, count)

    def start(self, part, number, source, target, device):
        remote(source, target, self.send.at[part, number], self.recv.at[part, number], device).start()

    def arrived(self, part, number, view):
        remote(view, view, self.send.at[part, number], self.recv.at[part, number], self.place.sibling()).wait_recv()

    def accumulate(self, target, sources, count):
        group = min(count, 8)
        size = group * self.rows

        def body(number, carry):
            rows = pl.ds(pl.multiple_of(number * size, size), size)
            total = target[rows, :].astype(F32)
            for source in sources:
                total = total + source[rows, :].astype(F32)
            target[rows, :] = total.astype(BF16)
            return carry

        lax.fori_loop(0, count // group, body, 0)

    def exchange(self):
        for slot, step in enumerate((2, 1, 3, 0)):
            for part in range(PARTS):
                third = lax.rem(self.mine(part)[0] + step, 4)
                source = self.view(part, third, count=16, ref=self.outgoing)
                self.start(part, slot, source, self.across(part, third), self.place.sibling())

    def far_out(self):
        for part in range(PARTS):
            third = lax.rem(self.mine(part)[0] + 2, 4)
            self.arrived(part, 0, self.across(part, third))
            self.accumulate(self.view(part, third, count=16), [self.across(part, third)], 16)
            for half, step in ((0, 1), (1, 3)):
                source = self.view(part, third, 2 * half, count=8)
                self.start(part, 4 + half, source, self.landing(0, part, half), self.place.peer(part, 2, step))

    def near_out(self):
        for part in range(PARTS):
            for half, step in ((0, 1), (1, 3)):
                third = lax.rem(self.mine(part)[0] + step, 4)
                self.arrived(part, 1 + half, self.across(part, third))
                self.arrived(part, 4 + half, self.landing(0, part, half))
                for side in (0, 1):
                    sources = [self.across(part, third, 2 * side, 8)]
                    if side == half:
                        sources.append(self.landing(0, part, half))
                    self.accumulate(self.view(part, third, 2 * side, count=8), sources, 8)
                source = self.view(part, third, count=16)
                self.start(part, 6 + half, source, self.landing(1, part, half), self.place.peer(part, 2, step))

    def second_out(self):
        for part in range(PARTS):
            third, second, first = self.mine(part)
            self.arrived(part, 3, self.across(part, third))
            for half in (0, 1):
                self.arrived(part, 6 + half, self.landing(1, part, half))
            sources = [self.across(part, third), self.landing(1, part, 0), self.landing(1, part, 1)]
            self.accumulate(self.view(part, third, count=16), sources, 16)
            for step in (1, 3, 2):
                source = self.view(part, third, lax.rem(second + step, 4), count=4)
                target = self.landing(2, part, step - 1)
                self.start(part, 7 + step, source, target, self.place.peer(part, 1, step))

    def first_out(self):
        for part in range(PARTS):
            third, second, first = self.mine(part)
            for step in (1, 3, 2):
                self.arrived(part, 7 + step, self.landing(2, part, step - 1))
            sources = [self.landing(2, part, slot) for slot in range(3)]
            self.accumulate(self.view(part, third, second, count=4), sources, 4)
            for step in (1, 3, 2):
                source = self.view(part, third, second, lax.rem(first + step, 4))
                target = self.landing(3, part, step - 1)
                self.start(part, 10 + step, source, target, self.place.peer(part, 0, step))

    def total(self, out, place):
        for part in range(PARTS):
            third, second, first = self.mine(part)
            for step in (1, 3, 2):
                self.arrived(part, 10 + step, self.landing(3, part, step - 1))
            value = self.view(part, third, second, first)[...].astype(F32)
            for slot in range(3):
                value = value + self.landing(3, part, slot)[...].astype(F32)
            out[place : place + self.rows, LANES * part : LANES * (part + 1)] = value

    def sent(self):
        for part in range(PARTS):
            for number in range(14):
                count = 16 if number < 4 else 8 if number < 6 else 16 if number < 8 else 4 if number < 11 else 1
                view = self.view(part, 0, count=count)
                remote(view, view, self.send.at[part, number], self.recv.at[part, number], self.place.sibling()).wait_send()


def pack_attention(early, grads, spread, back_a_ref, core, ref):
    for number in range(8):
        dp = number * 2 + core
        rows = pl.ds(pl.multiple_of(dp * 48, 16), 48)
        for part in range(PARTS):
            columns = slice(LANES * part, LANES * (part + 1))
            pieces = [grad[rows, columns] for grad in grads]
            if part == 0:
                tail = spread[pl.ds(pl.multiple_of(dp * 8, 8), 8), :]
                tail = jnp.concatenate([tail, jnp.zeros((8, 128), F32)], axis=0)
                tail = jnp.concatenate([tail, jnp.zeros((16, 128), F32)], axis=1)
            else:
                tail = jnp.zeros((16, LANES), F32)
            blocks = dot(back_a_ref[...], jnp.concatenate(pieces + [tail.astype(BF16)], axis=0)).astype(BF16)
            for device, index in enumerate(chunk_blocks(part, number // 4, number % 4, 0)):
                target = early.view(part, *index[2:], ref=ref)
                target[...] = blocks[ROWS_A * device : ROWS_A * (device + 1)]


def pack_vectors(vectors, numbers):
    packed = jnp.zeros((128, 128), F32)
    for number in numbers:
        wide = 6 if number < 8 else 24
        mask = owner_mask(0 if number < 8 else 768 * (number - 8), wide)
        whole = jnp.where(mask, vectors[number], 0.0).astype(BF16)
        packed = packed + dot(whole, vector_lanes(number), 1, 1)
    return packed


def backward_kernel(
    lengths_ref, skip_ref, inverse, vector_in, back_a_ref,
    frames_in, upstream_in, q_in, k_in, v_in, ctx_in, probs_in, branch_in, residual_in, attend_in, output_in, output_grad_in,
    feed_in,
    summed, frames_grad,
    own_f, own_a, outgoing_a, other_a, other_f, far_f, near_f, second_f, first_f, far_a, near_a, second_a, first_a,
    attend, output_weight, q_n, k_t, v_n, ctx_t, frames, branch, scaled_t, dk_n, dq_t, dv_t, score_grad, probs,
    ctx_grad, right, ones_mask, spread,
    send_a, recv_a, send_f, recv_f, local,
):
    place = Place()
    core = place.at[3]
    greet(place)
    pairs = (
        (output_in, output_weight), (branch_in, branch), (v_in, v_n), (ctx_in, ctx_t), (k_in, k_t), (q_in, q_n),
        (feed_in.at[pl.ds(pl.multiple_of(core * HALF_F, 16), HALF_F), :], own_f), (frames_in, frames), (attend_in, attend),
    )
    loads = [pltpu.make_async_copy(source, target, local.at[i]) for i, (source, target) in enumerate(pairs)]
    later = [
        pltpu.make_async_copy(output_grad_in, output_weight, local.at[9]),
        pltpu.make_async_copy(upstream_in, branch, local.at[10]),
        pltpu.make_async_copy(residual_in, ctx_grad, local.at[11]),
        pltpu.make_async_copy(scaled_t, frames_grad, local.at[12]),
    ]

    def prob_load(head, slot):
        return pltpu.make_async_copy(probs_in.at[head], probs.at[slot], local.at[13 + slot])

    for item in loads[:4]:
        item.start()
    prob_load(0, 0).start()
    for item in loads[4:6]:
        item.start()
    prob_load(1, 1).start()
    prob_load(2, 2).start()
    for item in loads[6:]:
        item.start()
    outgoing = feed_in.at[pl.ds(pl.multiple_of((1 - core) * HALF_F, 16), HALF_F), :]
    late = Scatter(place, own_f, outgoing, other_f, far_f, near_f, second_f, first_f, ROWS_F, send_f, recv_f)
    early = Scatter(
        place, own_a, outgoing_a, other_a,
        far_a, near_a, second_a, first_a, ROWS_A, send_a, recv_a,
    )
    lane = lax.broadcasted_iota(jnp.int32, (768, 128), 1)
    ones_mask[...] = jnp.where(lane < 2, 1.0, 0.0).astype(BF16)
    for side in range(2):
        right[side] = jnp.zeros((256, 768), BF16)
    meet()
    late.exchange()
    spread[...] = pack_vectors([vector(vector_in, i) for i in range(VECTORS)], range(2, VECTORS))
    loads[0].wait()
    loads[1].wait()
    ctx_grad[...] = dot(output_weight[...], branch[...], 1, 1)
    later[0].start()
    later[1].start()
    for item in loads[2:4]:
        item.wait()
    prob_load(0, 0).wait()

    def score_stage(pair, side):
        head = pair * 2 + side
        rows = head_rows(head)
        factor = inverse[pl.ds(pl.multiple_of(head * 8, 8), 8), :][0:1]
        scaled = (ctx_grad[rows, :] * factor).astype(BF16)
        scaled_t[rows, :] = scaled
        right[side, 64 * side : 64 * side + 64] = scaled
        inner = jnp.sum(scaled.astype(F32) * ctx_t[rows, :].astype(F32), axis=0, keepdims=True)
        high = inner.astype(BF16).astype(F32)
        row = lax.broadcasted_iota(jnp.int32, (16, 768), 0)
        right[side, 128:144] = jnp.where(row == 0, -high, jnp.where(row == 1, high - inner, 0.0)).astype(BF16)
        left = jnp.concatenate([v_n[:, pair_lanes(pair)], ones_mask[...]], axis=1)
        score_grad[side] = (dot(left, right[side]) * probs[lax.rem(head, 3)].astype(F32)).astype(BF16)

    def use_stage(pair, side):
        head = pair * 2 + side
        rows = head_rows(head)
        lanes = pair_lanes(pair)
        dv_t[rows, :] = dot(scaled_t[rows, :], probs[lax.rem(head, 3)], 1, 1).astype(BF16)
        dq_t[rows, :] = (dot(k_t[rows, :], score_grad[side]) * SCALE).astype(BF16)
        keys = dot(score_grad[side], q_n[:, lanes]).astype(BF16)
        if side == 1:
            keys = jnp.where(lax.broadcasted_iota(jnp.int32, (768, 128), 1) < 64, dk_n[:, lanes], keys)
        dk_n[:, lanes] = keys

    def refill(head):
        @pl.when(head + 3 < 12)
        def _():
            prob_load(head + 3, lax.rem(head, 3)).start()

        @pl.when(head + 2 < 12)
        def _():
            prob_load(head + 2, lax.rem(head + 2, 3)).wait()

    score_stage(0, 0)
    for item in loads[4:6]:
        item.wait()
    prob_load(1, 1).wait()
    loads[6].wait()
    steps = (None, late.far_out, late.near_out, None, None, late.second_out)

    def body(pair, carry):
        for number, step in enumerate(steps):
            if step is not None:
                pl.when(pair == number)(step)
        score_stage(pair, 1)
        use_stage(pair, 0)
        refill(pair * 2)
        score_stage(jnp.minimum(pair + 1, 5), 0)
        use_stage(pair, 1)
        refill(pair * 2 + 1)
        return carry

    lax.fori_loop(0, 6, body, 0)
    later[2].start()
    loads[7].wait()
    loads[8].wait()
    x = frames[...]
    queries, values = score_grad.at[0], score_grad.at[1]
    queries[...] = dq_t[...].T
    values[...] = dv_t[...].T
    grads = (k_t, q_n, v_n, output_weight)
    k_t[...] = dot(x, queries[...], 0, 0).astype(BF16)
    q_n[...] = dot(x, dk_n[...], 0, 0).astype(BF16)
    v_n[...] = dot(x, values[...], 0, 0).astype(BF16)
    sums = [jnp.sum(ref[...].astype(F32), axis=0, keepdims=True) for ref in (queries, values)]
    spread[...] = spread[...] + pack_vectors(sums, range(2))
    later[0].wait()
    late.first_out()
    pack_attention(early, grads, spread, back_a_ref, 1 - core, outgoing_a)
    early.exchange()
    pack_attention(early, grads, spread, back_a_ref, core, own_a)
    later[1].wait()
    later[2].wait()

    def finish_rows(block):
        rows = slice(256 * block, 256 * (block + 1))
        live = live_mask(lengths_ref, skip_ref, (256, 1), 256 * block)
        total = ctx_grad[rows, :] + dot(queries[rows, :], attend[0], 1, 1) + dot(dk_n[rows, :], attend[1], 1, 1)
        total = total + dot(values[rows, :], attend[2], 1, 1)
        scaled_t[rows, :] = jnp.where(live, total, branch[rows, :].astype(F32)).astype(BF16)

    early.far_out()
    finish_rows(0)
    early.near_out()
    finish_rows(1)
    finish_rows(2)
    later[3].start()
    late.total(summed, ROWS_A)
    early.second_out()
    early.first_out()
    early.total(summed, 0)
    later[3].wait()
    early.sent()
    late.sent()


def backward_call(*args):
    square = pltpu.VMEM((768, 768), BF16)

    def blocks(count, rows):
        return pltpu.VMEM((PARTS * count * rows, LANES), BF16)

    return pl.pallas_call(
        backward_kernel,
        out_shape=(shape(ROWS_ALL, 768, kind=F32), shape(768, 768)),
        in_specs=[SCALARS] * 2 + [WHOLE] * 3 + [ANYWHERE] * 13,
        out_specs=[WHOLE, ANYWHERE],
        scratch_shapes=[blocks(64, ROWS_F)] + [blocks(64, ROWS_A)] * 3 + [blocks(64, ROWS_F)]
        + [blocks(count, ROWS_F) for count in (16, 32, 12, 3)]
        + [blocks(count, ROWS_A) for count in (16, 32, 12, 3)]
        + [pltpu.VMEM((3, 768, 768), BF16)]
        + [square] * 11
        + [
            pltpu.VMEM((2, 768, 768), BF16), pltpu.VMEM((3, 768, 768), BF16), pltpu.VMEM((768, 768), F32),
            pltpu.VMEM((2, 256, 768), BF16), pltpu.VMEM((768, 128), BF16), pltpu.VMEM((128, 128), F32),
        ]
        + [pltpu.SemaphoreType.DMA((PARTS, 14))] * 4
        + [pltpu.SemaphoreType.DMA((16,))],
        compiler_params=pltpu.CompilerParams(collective_id=1, has_side_effects=True, vmem_limit_bytes=62 * 2**20),
        name="backward",
    )(*args)


def deliver_kernel(summed, encoded_in, frames_in, encoded_out, frames_out, *rest):
    query_out, key_out, value_out, output_out, expand_out, shrink_out, *vectors, hold, sems = rest
    moves = [
        (pltpu.make_async_copy(source, hold.at[i], sems.at[i]), pltpu.make_async_copy(hold.at[i], target, sems.at[2 + i]))
        for i, (source, target) in enumerate(((encoded_in, encoded_out), (frames_in, frames_out)))
    ]
    for inward, outward in moves:
        inward.start()
    for number, target in enumerate((query_out, key_out, value_out, output_out)):
        target[...] = summed[6 * number : 6 * number + 6, :]
    for number in range(4):
        expand_out[:, 768 * number : 768 * (number + 1)] = summed[32 + 6 * number : 38 + 6 * number, :]
    shrink_out[...] = summed[56:80, :]
    for at, target in zip(PLACES, vectors, strict=True):
        target[...] = summed[24, at : at + target.shape[0]]
    for inward, outward in moves:
        inward.wait()
        outward.start()
    for inward, outward in moves:
        outward.wait()


def deliver(summed, encoded, frames_grad):
    sizes = ((6, 768),) * 4 + ((6, 3072), (24, 768)) + ((6,),) * 8 + ((24,),)
    return pl.pallas_call(
        deliver_kernel,
        out_shape=(shape(768, 768), shape(768, 768)) + tuple(shape(*s, kind=F32) for s in sizes),
        in_specs=[WHOLE] + [ANYWHERE] * 2,
        out_specs=[ANYWHERE] * 2 + [WHOLE] * 15,
        scratch_shapes=[pltpu.VMEM((2, 768, 768), BF16), pltpu.SemaphoreType.DMA((4,))],
        name="deliver",
    )(summed, encoded, frames_grad)


PLACES = (0, 6, 12, 18, 24, 30, 36, 42, 48)


def local(
    frames,
    upstream,
    clip_lengths,
    clip_skip,
    query_weight,
    key_weight,
    value_weight,
    output_weight,
    query_bias,
    value_bias,
    output_bias,
    first_gain,
    first_shift,
    expand_weight,
    shrink_weight,
    expand_bias,
    shrink_bias,
    second_gain,
    second_shift,
):
    vectors = (
        query_bias, value_bias, output_bias, first_gain, first_shift, shrink_bias, second_gain, second_shift, expand_bias,
    )
    (
        vector_grad, encoded, residual_grad, branch_grad, ctx_t, inverse,
        attend, output, output_grad, q_n, k_t, v_n, probs, feed_grad,
    ) = forward_call(
        clip_lengths, clip_skip, frames, upstream,
        query_weight, key_weight, value_weight, output_weight, expand_weight, shrink_weight, *vectors,
    )
    summed, frames_grad = backward_call(
        clip_lengths, clip_skip, inverse, vector_grad,
        jnp.asarray(attention_rows().T, BF16),
        frames, upstream, q_n, k_t, v_n, ctx_t, probs, branch_grad, residual_grad, attend, output, output_grad, feed_grad,
    )
    encoded, frames_grad, query_sum, key_sum, value_sum, output_sum, expand_sum, shrink_sum, *sums = deliver(
        summed, encoded, frames_grad
    )
    return (
        encoded, frames_grad, query_sum, key_sum, value_sum, output_sum, sums[0], sums[1], sums[2], sums[3], sums[4],
        expand_sum, shrink_sum, sums[8], sums[5], sums[6], sums[7],
    )


def solution(mesh):
    return jax.shard_map(
        local,
        mesh=mesh,
        in_specs=(
            P(("dp", "fsdp"), None),
            P(("dp", "fsdp"), None),
            P(("dp", "fsdp"), None),
            P(("dp", "fsdp"), None),
            P(("dp", "fsdp"), None),
            P(("dp", "fsdp"), None),
            P(("dp", "fsdp"), None),
            P(("dp", "fsdp"), None),
            P(("dp", "fsdp")),
            P(("dp", "fsdp")),
            P(("dp", "fsdp")),
            P(("dp", "fsdp")),
            P(("dp", "fsdp")),
            P(("dp", "fsdp"), None),
            P(("dp", "fsdp"), None),
            P(("dp", "fsdp")),
            P(("dp", "fsdp")),
            P(("dp", "fsdp")),
            P(("dp", "fsdp")),
        ),
        out_specs=(
            P(("dp", "fsdp"), None),
            P(("dp", "fsdp"), None),
            P(("dp", "fsdp"), None),
            P(("dp", "fsdp"), None),
            P(("dp", "fsdp"), None),
            P(("dp", "fsdp"), None),
            P(("dp", "fsdp")),
            P(("dp", "fsdp")),
            P(("dp", "fsdp")),
            P(("dp", "fsdp")),
            P(("dp", "fsdp")),
            P(("dp", "fsdp"), None),
            P(("dp", "fsdp"), None),
            P(("dp", "fsdp")),
            P(("dp", "fsdp")),
            P(("dp", "fsdp")),
            P(("dp", "fsdp")),
        ),
        check_vma=False,
    )
```

```python
import functools
import math

import jax
import jax.numpy as jnp
import numpy as np
from jax import lax
from jax.experimental import pallas as pl
from jax.experimental.pallas import tpu as pltpu
from jax.sharding import PartitionSpec as P

epsilon = 1e-05

SCALE = 0.125
EXCLUDED = -1e30
F32 = jnp.float32
BF16 = jnp.bfloat16
WHOLE = pl.BlockSpec(memory_space=pltpu.VMEM)
SCALARS = pl.BlockSpec(memory_space=pltpu.SMEM)
ANYWHERE = pl.BlockSpec(memory_space=pl.ANY)
VEC_QUERY, VEC_VALUE, VEC_OUTPUT, VEC_GAIN1, VEC_SHIFT1, VEC_SHRINK, VEC_GAIN2, VEC_SHIFT2, VEC_EXPAND = range(9)


def dot(left, right, a=1, b=0):
    return lax.dot_general(left, right, (((a,), (b,)), ((), ())), preferred_element_type=F32)


def shape(*sizes, kind=jnp.bfloat16):
    return jax.ShapeDtypeStruct(sizes, kind)


def segments(lengths_ref, axis, extent, first=0):
    place = lax.broadcasted_iota(jnp.int32, extent, axis) + first
    first_end = lengths_ref[0, 0]
    second_end = first_end + lengths_ref[0, 1]
    return jnp.where(place < first_end, 0, jnp.where(place < second_end, 1, 2))


def live_mask(lengths_ref, skip_ref, extent, first):
    segment = segments(lengths_ref, 0, extent, first)
    dropped = jnp.where(segment == 0, skip_ref[0, 0], jnp.where(segment == 1, skip_ref[0, 1], 1))
    return dropped == 0


def vector(ref, number):
    return ref[0:1, 768 * number : 768 * (number + 1)]


def head_rows(head):
    return pl.ds(pl.multiple_of(head * 64, 64), 64)


def pair_lanes(pair):
    return pl.ds(pl.multiple_of(pair * 128, 128), 128)


def project(frames, attend, vectors, q_n, k_n, v_n, q_t, k_t, v_t):
    x = frames[...]
    q_n[...] = ((dot(x, attend[0]) + vector(vectors, VEC_QUERY)) * SCALE).astype(BF16)
    q_t[...] = q_n[...].T
    k_n[...] = dot(x, attend[1]).astype(BF16)
    k_t[...] = k_n[...].T
    v_n[...] = (dot(x, attend[2]) + vector(vectors, VEC_VALUE)).astype(BF16)
    v_t[...] = v_n[...].T


def mask_operands(lengths_ref, right, k_mask):
    lane = lax.broadcasted_iota(jnp.int32, (768, 128), 1)
    k_mask[...] = jnp.where(lane == segments(lengths_ref, 0, (768, 128)), 1.0, 0.0).astype(BF16)
    row = lax.broadcasted_iota(jnp.int32, (128, 768), 0)
    other = (row < 3) & (row != segments(lengths_ref, 1, (128, 768)))
    other = jnp.where(other, EXCLUDED, 0.0).astype(BF16)
    for side in range(2):
        right[side, 128:256] = other
        right[side, 64 * (1 - side) : 64 * (1 - side) + 64] = jnp.zeros((64, 768), BF16)


def score_stage(pair, side, q_t, k_n, k_mask, right, scores, tops):
    left = jnp.concatenate([k_n[:, pair_lanes(pair)], k_mask[...]], axis=1)
    right[side, 64 * side : 64 * side + 64] = q_t[head_rows(pair * 2 + side), :]
    values = dot(left, right[side])
    scores[side] = values
    tops[side] = jnp.broadcast_to(jnp.max(values, axis=0, keepdims=True), (8, 768))


def prob_stage(pair, side, v_t, scores, tops, probs, inverse, ctx_t):
    head = pair * 2 + side
    rows = head_rows(head)
    left = jnp.concatenate([v_t[rows, :], jnp.ones((16, 768), BF16)], axis=0)
    raised = jnp.exp(scores[side] - tops[side, 0:1]).astype(BF16)
    probs[side][...] = raised
    total = dot(left, raised)
    factor = 1.0 / total[64:65]
    inverse[pl.ds(pl.multiple_of(head * 8, 8), 8), :] = jnp.broadcast_to(factor, (8, 768))
    ctx_t[rows, :] = (total[:64] * factor).astype(BF16)


def gelu_pair(v):
    base = 1.0 + (0.3275911 / math.sqrt(2.0)) * jnp.abs(v)
    t = pl.reciprocal(base, approx=True)
    t = t * (2.0 - base * t)
    e = jnp.exp2((v * v) * (-0.5 / math.log(2.0)))
    poly = t * (0.127414796 + t * (-0.142248368 + t * (0.7107068705 + t * (-0.7265760135 + t * 0.5307027145))))
    tail = poly * e
    phi = jnp.where(v >= 0, 1.0 - tail, tail)
    return v * phi, phi + v * e * (1.0 / math.sqrt(2.0 * math.pi))


def normalise(values):
    centered = values - jnp.mean(values, axis=-1, keepdims=True)
    scale = lax.rsqrt(jnp.mean(centered * centered, axis=-1, keepdims=True) + epsilon)
    return centered * scale, scale


def norm_back(cotangent, gain, normed, scale):
    c = cotangent * gain
    return scale * (
        c - jnp.mean(c, axis=-1, keepdims=True) - normed * jnp.mean(c * normed, axis=-1, keepdims=True)
    )


MESH = pl.DeviceIdType.MESH
ROWS_A = 32
ROWS_F = 48
ROWS_ALL = ROWS_A + ROWS_F
LANES = 256
PARTS = 3
HALF_F = PARTS * 64 * ROWS_F
VECTORS = 12
BIAS_OUT = 208


def attention_rows():
    table = np.zeros((BIAS_OUT, 8 * ROWS_A), np.float32)
    for row in range(192):
        matrix, inner = divmod(row, 48)
        device, lane = divmod(inner, 6)
        table[row, device * ROWS_A + 6 * matrix + lane] = 1
    for device in range(8):
        table[192 + device, device * ROWS_A + 24] = 1
    return table


def expand_rows():
    table = np.zeros((192, 256), np.float32)
    for row in range(192):
        matrix, inner = divmod(row, 48)
        device, lane = divmod(inner, 6)
        table[row, 32 * device + 6 * matrix + lane] = 1
    return table


def shrink_rows():
    table = np.zeros((192, 256), np.float32)
    for row in range(192):
        device, lane = divmod(row, 24)
        table[row, 32 * device + 8 + lane] = 1
    return table


def vector_lanes(number):
    lane = lax.broadcasted_iota(jnp.int32, (128, 768), 0)
    column = lax.broadcasted_iota(jnp.int32, (128, 768), 1)
    if number < 8:
        wanted = column - 6 * ((column * 10923) >> 16) + 6 * number
    else:
        wanted = column - 24 * ((column * 2731) >> 16) + 48
    return jnp.where(lane == wanted, 1.0, 0.0).astype(BF16)


def owner_mask(first, wide):
    device = lax.broadcasted_iota(jnp.int32, (128, 768), 0)
    column = lax.broadcasted_iota(jnp.int32, (128, 768), 1) + first
    low = device * wide
    return (column >= low) & (column < low + wide)


def position():
    dp = lax.axis_index("dp")
    fsdp = lax.axis_index("fsdp")
    core = lax.rem(dp, 2)
    y = lax.rem(lax.div(dp, 2), 4)
    z = lax.div(dp, 8) * 2 + lax.div(fsdp, 4)
    x = lax.rem(fsdp, 4)
    return x, y, z, core


def device_of(x, y, z, core):
    return ((lax.div(z, 2) * 4 + y) * 2 + core, lax.rem(z, 2) * 4 + x)


AXES = ((0, 1, 2), (1, 2, 0), (2, 0, 1))


class Place:
    def __init__(self):
        self.at = position()
        x, y, z, core = self.at
        self.turns = [[at] + [lax.rem(at + step, 4) for step in (1, 2, 3)] for at in (x, y, z)]
        self.twin = device_of(x, y, z, 1 - core)
        self.devices = {}
        for axis in range(3):
            for step in (1, 2, 3):
                where = list(self.at)
                where[axis] = self.turns[axis][step]
                self.devices[axis, step] = device_of(*where)

    def along(self, part, stage, step=0):
        return self.turns[AXES[part][stage]][step]

    def peer(self, part, stage, step):
        return self.devices[AXES[part][stage], step]

    def sibling(self):
        return self.twin


def greet(place):
    for target in (place.twin, *place.devices.values()):
        pl.semaphore_signal(pltpu.get_barrier_semaphore(), inc=1, device_id=target, device_id_type=MESH)


def meet():
    pl.semaphore_wait(pltpu.get_barrier_semaphore(), 10)


def remote(source, target, send, receive, device):
    return pltpu.make_async_remote_copy(
        src_ref=source,
        dst_ref=target,
        send_sem=send,
        recv_sem=receive,
        device_id=device,
        device_id_type=MESH,
    )


def chunk_blocks(part, high, y, core):
    blocks = []
    for low in range(2):
        for x in range(4):
            where = (x, y, high * 2 + low)
            first, second, third = (where[a] for a in AXES[part])
            blocks.append((part, core, third, second, first))
    return blocks


def rows_at(ref, start, count):
    if isinstance(start, int):
        return ref.at[start : start + count, :]
    return ref.at[pl.ds(pl.multiple_of(start, 16), count), :]


class Gather:
    def __init__(self, place, held, rows, send, recv):
        self.place, self.held, self.rows, self.send, self.recv = place, held, rows, send, recv
        self.core = place.at[3]

    def view(self, part, core, third, second=0, first=0, count=1):
        start = (((core * PARTS + part) * 4 + third) * 4 + second) * 4 + first
        return rows_at(self.held, start * self.rows, count * self.rows)

    def mine(self, part):
        return tuple(self.place.along(part, stage) for stage in (2, 1, 0))

    def copy(self, part, number, view, device):
        return remote(view, view, self.send.at[part, number], self.recv.at[part, number], device)

    def start(self, part, number, view, device):
        self.copy(part, number, view, device).start()

    def arrived(self, part, number, view):
        self.copy(part, number, view, self.place.sibling()).wait_recv()

    def block(self, part, third, second, first):
        return self.view(part, self.core, third, second, first)

    def two(self, part, third, second, half):
        return self.view(part, self.core, third, second, 2 * half, 2)

    def eight(self, part, core, third, half):
        return self.view(part, core, third, 2 * half, 0, 8)

    def first(self):
        for part in range(PARTS):
            view = self.block(part, *self.mine(part))
            for step in (1, 3, 2):
                self.start(part, step - 1, view, self.place.peer(part, 0, step))

    def second(self):
        for part in range(PARTS):
            third, second, first = self.mine(part)
            for step in (1, 3, 2):
                self.arrived(part, step - 1, self.block(part, third, second, self.place.along(part, 0, 4 - step)))
            ahead, behind = self.place.peer(part, 1, 1), self.place.peer(part, 1, 3)
            for half in (0, 1):
                self.start(part, 3 + half, self.two(part, third, second, half), ahead)
                self.start(part, 6 - half, self.two(part, third, second, 1 - half), behind)

    def second_on(self):
        for part in range(PARTS):
            third, second, first = self.mine(part)
            ahead, behind = self.place.peer(part, 1, 1), self.place.peer(part, 1, 3)
            view = self.two(part, third, self.place.along(part, 1, 3), 0)
            self.arrived(part, 3, view)
            self.start(part, 7, view, ahead)
            view = self.two(part, third, self.place.along(part, 1, 1), 1)
            self.arrived(part, 6, view)
            self.start(part, 8, view, behind)

    def third(self):
        for part in range(PARTS):
            third, second, first = self.mine(part)
            self.arrived(part, 4, self.two(part, third, self.place.along(part, 1, 3), 1))
            self.arrived(part, 5, self.two(part, third, self.place.along(part, 1, 1), 0))
            for half in (0, 1):
                self.arrived(part, 7 + half, self.two(part, third, self.place.along(part, 1, 2), half))
            ahead, behind = self.place.peer(part, 2, 1), self.place.peer(part, 2, 3)
            for half in (0, 1):
                self.start(part, 9 + half, self.eight(part, self.core, third, half), ahead)
                self.start(part, 12 - half, self.eight(part, self.core, third, 1 - half), behind)
            self.start(part, 15, self.view(part, self.core, third, count=16), self.place.sibling())

    def third_on(self):
        for part in range(PARTS):
            third, second, first = self.mine(part)
            ahead, behind = self.place.peer(part, 2, 1), self.place.peer(part, 2, 3)
            view = self.eight(part, self.core, self.place.along(part, 2, 3), 0)
            self.arrived(part, 9, view)
            self.start(part, 13, view, ahead)
            self.start(part, 16, view, self.place.sibling())
            view = self.eight(part, self.core, self.place.along(part, 2, 1), 1)
            self.arrived(part, 12, view)
            self.start(part, 14, view, behind)
            self.start(part, 17, view, self.place.sibling())

    def near_over(self):
        for part in range(PARTS):
            third, second, first = self.mine(part)
            view = self.eight(part, self.core, self.place.along(part, 2, 3), 1)
            self.arrived(part, 10, view)
            self.start(part, 18, view, self.place.sibling())
            view = self.eight(part, self.core, self.place.along(part, 2, 1), 0)
            self.arrived(part, 11, view)
            self.start(part, 19, view, self.place.sibling())

    def far_over(self):
        for part in range(PARTS):
            third, second, first = self.mine(part)
            for half in (0, 1):
                view = self.eight(part, self.core, self.place.along(part, 2, 2), half)
                self.arrived(part, 13 + half, view)
                self.start(part, 20 + half, view, self.place.sibling())

    def finish(self):
        other = 1 - self.core
        for part in range(PARTS):
            third, second, first = self.mine(part)
            self.arrived(part, 15, self.view(part, other, third, count=16))
            self.arrived(part, 16, self.eight(part, other, self.place.along(part, 2, 3), 0))
            self.arrived(part, 17, self.eight(part, other, self.place.along(part, 2, 1), 1))
            self.arrived(part, 18, self.eight(part, other, self.place.along(part, 2, 3), 1))
            self.arrived(part, 19, self.eight(part, other, self.place.along(part, 2, 1), 0))
            for half in (0, 1):
                self.arrived(part, 20 + half, self.eight(part, other, self.place.along(part, 2, 2), half))

    def sent(self):
        for part in range(PARTS):
            for number in range(22):
                if number < 3:
                    view = self.block(part, 0, 0, 0)
                elif number < 9:
                    view = self.two(part, 0, 0, 0)
                elif number == 15:
                    view = self.view(part, self.core, 0, count=16)
                else:
                    view = self.eight(part, self.core, 0, 0)
                self.copy(part, number, view, self.place.sibling()).wait_send()


def unpack_attention(held, rows_a_ref, attend, output, vectors, spread):
    def body(y, carry):
        for high, core in ((0, 0), (0, 1), (1, 0), (1, 1)):
            start = 8 * high + core
            rows = pl.ds(pl.multiple_of(48 * start + 96 * y, 16), 48)
            for part in range(PARTS):
                columns = slice(LANES * part, LANES * (part + 1))
                blocks = jnp.concatenate([held.view(*index)[...] for index in chunk_blocks(part, high, y, core)], axis=0)
                blocks = dot(rows_a_ref[...], blocks)
                if part == 0:
                    spread[pl.ds(pl.multiple_of(8 * start + 16 * y, 8), 8), :] = blocks[192:200, :128]
                blocks = blocks.astype(BF16)
                for matrix in range(3):
                    attend[matrix, rows, columns] = blocks[48 * matrix : 48 * (matrix + 1)]
                output[rows, columns] = blocks[144:192]
        return carry

    lax.fori_loop(0, 4, body, 0)

    packed = spread[...].astype(BF16)
    for number in range(VECTORS):
        wide = 6 if number < 8 else 24
        mask = owner_mask(0 if number < 8 else 768 * (number - 8), wide)
        columns = slice(768 * number, 768 * (number + 1))
        whole = dot(packed, vector_lanes(number))
        vectors[:, columns] = jnp.sum(jnp.where(mask, whole, 0.0), axis=0, keepdims=True)


def unpack_feed(held, rows_e_ref, rows_s_ref, expand, shrink, beside):
    def body(y, carry):
        beside(y)
        for high, core in ((0, 0), (0, 1), (1, 0), (1, 1)):
            start = 8 * high + core
            rows = pl.ds(pl.multiple_of(48 * start + 96 * y, 16), 48)
            for part in range(PARTS):
                columns = slice(LANES * part, LANES * (part + 1))
                blocks = [held.view(*index)[...] for index in chunk_blocks(part, high, y, core)]
                first = dot(rows_e_ref[...], jnp.concatenate([b[:32] for b in blocks], axis=0)).astype(BF16)
                second = dot(rows_s_ref[...], jnp.concatenate([b[16:] for b in blocks], axis=0)).astype(BF16)
                for matrix in range(4):
                    expand[rows, 768 * matrix + LANES * part : 768 * matrix + LANES * (part + 1)] = first[
                        48 * matrix : 48 * (matrix + 1)
                    ]
                shrink[pl.ds(pl.multiple_of(192 * start + 384 * y, 16), 192), columns] = second
        return carry

    lax.fori_loop(0, 4, body, 0)


def pack_feed(held, back_e_ref, back_s_ref, expand, shrink):
    def body(y, carry):
        for high, core in ((0, 0), (0, 1), (1, 0), (1, 1)):
            start = 8 * high + core
            rows = pl.ds(pl.multiple_of(48 * start + 96 * y, 16), 48)
            for part in range(PARTS):
                pieces = [
                    expand[rows, 768 * matrix + LANES * part : 768 * matrix + LANES * (part + 1)] for matrix in range(4)
                ]
                first = dot(back_e_ref[...], jnp.concatenate(pieces, axis=0))
                values = shrink[pl.ds(pl.multiple_of(192 * start + 384 * y, 16), 192), LANES * part : LANES * (part + 1)]
                second = dot(back_s_ref[...], values)
                for device, index in enumerate(chunk_blocks(part, high, y, core)):
                    at = 32 * device
                    block = held.view(*index)
                    block[0:16, :] = first[at : at + 16].astype(BF16)
                    block[16:32, :] = (first[at + 16 : at + 32] + second[at : at + 16]).astype(BF16)
                    block[32:48, :] = second[at + 16 : at + 32].astype(BF16)
        return carry

    lax.fori_loop(0, 4, body, 0)


def forward_kernel(
    lengths_ref, skip_ref, frames_in, upstream_in,
    query_in, key_in, value_in, output_in, expand_in, shrink_in,
    *rest,
):
    forward_body(
        lengths_ref, skip_ref, frames_in, upstream_in, query_in, key_in, value_in, output_in, expand_in, shrink_in,
        rest[:9], *rest[9:],
    )


def forward_body(
    lengths_ref, skip_ref, frames_in, upstream_in, query_in, key_in, value_in, output_in, expand_in, shrink_in,
    vectors_in, rows_a_ref, rows_e_ref, rows_s_ref, back_e_ref, back_s_ref,
    vector_out, encoded_out, residual_out, branch_out, ctx_out, inverse_out,
    attend_out, weight_out, output_out, q_out, k_out, v_out, probs_out, feed_out,
    held_a, held_f, block_ref, spread, attend, output_weight, expand, shrink, vectors,
    frames, upstream, residual_grad, branch_grad, ctx_t, inverse, right, k_mask,
    send_a, recv_a, send_f, recv_f, local,
):
    place = Place()
    core = place.at[3]
    greet(place)
    frames_load = pltpu.make_async_copy(frames_in, frames, local.at[32])
    upstream_load = pltpu.make_async_copy(upstream_in, upstream, local.at[33])
    frames_load.start()
    upstream_load.start()
    for number, source in enumerate((query_in, key_in, value_in, output_in)):
        block_ref[6 * number : 6 * number + 6, :] = source[...].astype(F32)
    block_ref[24:32, :] = jnp.zeros((8, 768), F32)
    for at, ref in zip(PLACES, vectors_in, strict=True):
        size = ref.shape[0]
        block_ref[24:25, at : at + size] = ref[...].astype(F32).reshape(1, size)
    for number in range(4):
        block_ref[32 + 6 * number : 38 + 6 * number, :] = expand_in[:, 768 * number : 768 * (number + 1)].astype(F32)
    block_ref[56:80, :] = shrink_in[...].astype(F32)
    early = Gather(place, held_a, ROWS_A, send_a, recv_a)
    late = Gather(place, held_f, ROWS_F, send_f, recv_f)
    for part in range(PARTS):
        third, second, first = early.mine(part)
        values = block_ref[:, LANES * part : LANES * (part + 1)].astype(BF16)
        early.block(part, third, second, first)[...] = values[:ROWS_A]
        late.block(part, third, second, first)[...] = values[ROWS_A:]
    mask_operands(lengths_ref, right, k_mask)
    meet()
    early.first()
    late.first()
    early.second()
    early.second_on()
    early.third()
    late.second()
    early.third_on()
    late.second_on()
    early.near_over()
    early.far_over()
    late.third()
    early.finish()
    unpack_attention(early, rows_a_ref, attend, output_weight, vectors, spread)
    keep = [
        pltpu.make_async_copy(attend, attend_out, local.at[0]),
        pltpu.make_async_copy(output_weight, weight_out, local.at[1]),
    ]
    for item in keep:
        item.start()
    late.third_on()

    def attention(scores, tops):
        q_n, k_n, v_n, q_t = (expand.at[:, 768 * i : 768 * (i + 1)] for i in range(4))
        k_t, v_t, *probs = (shrink.at[768 * i : 768 * (i + 1), :] for i in range(4))
        frames_load.wait()
        project(frames, attend, vectors, q_n, k_n, v_n, q_t, k_t, v_t)
        hold = [
            pltpu.make_async_copy(q_n, q_out, local.at[2]),
            pltpu.make_async_copy(k_t, k_out, local.at[3]),
            pltpu.make_async_copy(v_n, v_out, local.at[4]),
        ]
        for item in hold:
            item.start()
        score_stage(0, 0, q_t, k_n, k_mask, right, scores, tops)

        def away(head, side):
            return pltpu.make_async_copy(probs[side], probs_out.at[head], local.at[5 + side])

        def body(pair, carry):
            @pl.when(pair > 0)
            def _():
                away(0, 0).wait()

            @pl.when(pair == 1)
            def _():
                late.near_over()

            @pl.when(pair == 3)
            def _():
                late.far_over()

            score_stage(pair, 1, q_t, k_n, k_mask, right, scores, tops)
            prob_stage(pair, 0, v_t, scores, tops, probs, inverse, ctx_t)
            away(pair * 2, 0).start()

            @pl.when(pair > 0)
            def _():
                away(0, 1).wait()

            score_stage(jnp.minimum(pair + 1, 5), 0, q_t, k_n, k_mask, right, scores, tops)
            prob_stage(pair, 1, v_t, scores, tops, probs, inverse, ctx_t)
            away(pair * 2 + 1, 1).start()
            return carry

        lax.fori_loop(0, 6, body, 0)
        for side in range(2):
            away(0, side).wait()
        for item in hold:
            item.wait()

    square = pltpu.VMEM((768, 768), BF16)
    pl.run_scoped(
        attention, pltpu.VMEM((2, 768, 768), F32), pltpu.VMEM((2, 8, 768), F32),
    )
    saves = [
        pltpu.make_async_copy(ctx_t, ctx_out, local.at[34]),
        pltpu.make_async_copy(inverse, inverse_out, local.at[35]),
        pltpu.make_async_copy(frames, encoded_out, local.at[36]),
        pltpu.make_async_copy(residual_grad, residual_out, local.at[37]),
        pltpu.make_async_copy(branch_grad, branch_out, local.at[38]),
    ]
    saves[0].start()
    saves[1].start()
    late.finish()
    late.sent()
    upstream_load.wait()

    def feed(normed, scales, hidden, raw):
        feed_forward(
            lengths_ref, skip_ref, frames, upstream, ctx_t, output_weight, expand, shrink, vectors,
            residual_grad, branch_grad, output_out, vector_out,
            normed, scales, hidden, held_f, raw, branch_grad, local, saves,
            lambda beside: unpack_feed(late, rows_e_ref, rows_s_ref, expand, shrink, beside),
            lambda: pack_feed(late, back_e_ref, back_s_ref, expand, shrink),
            pltpu.make_async_copy(held_f, feed_out, local.at[7]),
        )

    pl.run_scoped(
        feed, pltpu.VMEM((768, 768), F32), pltpu.VMEM((768, 128), F32), square,
        pltpu.VMEM((2, 768, 512), F32),
    )
    for item in keep + saves:
        item.wait()
    early.sent()


def feed_forward(
    lengths_ref, skip_ref, frames, upstream, ctx_t, output_weight, expand, shrink, vectors,
    acc, branch_grad, output_out, vector_out,
    normed, scales, hidden, panels, raw, summed_grad, local, saves, unpack, pack, feed_move,
):
    def rows_of(block):
        return slice(256 * block, 256 * (block + 1))

    def wide_columns(chunk):
        return pl.ds(pl.multiple_of(768 * chunk, 768), 768)

    hidden[...] = ctx_t[...].T

    def first_norm(y):
        rows = pl.ds(pl.multiple_of(192 * y, 64), 192)
        values = dot(hidden[rows, :], output_weight[...]) + frames[rows, :].astype(F32) + vector(vectors, VEC_OUTPUT)
        unit, scale = normalise(values)
        normed[rows, :] = unit
        scales[rows, :] = jnp.broadcast_to(scale, (192, 128))
        hidden[rows, :] = (unit * vector(vectors, VEC_GAIN1) + vector(vectors, VEC_SHIFT1)).astype(BF16)

    unpack(first_norm)

    def panel(kind, number, block=None):
        start = (kind * 12 + number) * 768
        if block is None:
            return panels.at[pl.ds(pl.multiple_of(start, 256), 768), :]
        return panels.at[pl.ds(pl.multiple_of(start + 256 * block, 256), 256), :]

    def load(kind, first, count, block=None):
        return jnp.concatenate([panel(kind, first + i, block)[...] for i in range(count)], axis=1)

    def save(kind, first, count, block, values):
        for i in range(count):
            panel(kind, first + i, block)[...] = values[:, 256 * i : 256 * (i + 1)].astype(BF16)

    def narrow_columns(chunk):
        return pl.ds(pl.multiple_of(512 * chunk, 512), 512)

    def expand_stage(chunk, slot):
        raw[slot] = dot(hidden[...], expand[:, narrow_columns(chunk)])

    def gelu_stage(chunk, slot):
        bias = vectors[0:1, pl.ds(pl.multiple_of(768 * VEC_EXPAND + 512 * chunk, 512), 512)]
        for block in range(3):
            rows = rows_of(block)
            value, derivative = gelu_pair(raw[slot, rows] + bias)
            save(0, 2 * chunk, 2, block, value)
            save(1, 2 * chunk, 2, block, derivative)

    def shrink_stage(chunk, first=False):
        columns = narrow_columns(chunk)
        for block in range(3):
            rows = rows_of(block)
            product = dot(load(0, 2 * chunk, 2, block), shrink[columns, :])
            acc[rows, :] = product if first else acc[rows, :] + product

    expand_stage(0, 0)
    expand_stage(1, 1)
    gelu_stage(0, 0)
    acc[...] = jnp.zeros((768, 768), F32)

    def chunks(number, carry):
        for inner in (1, 2):
            chunk = 2 * number + inner
            expand_stage(chunk + 1, 1 - inner % 2)
            gelu_stage(chunk, inner % 2)
            shrink_stage(chunk - 1)
        return carry

    for number in range(2):
        chunks(number, 0)
    gelu_stage(5, 1)
    shrink_stage(4)
    shrink_stage(5)

    sums = [jnp.zeros((1, 768), F32) for _ in range(3)]
    for block in range(3):
        rows = rows_of(block)
        first = normed[rows, :] * vector(vectors, VEC_GAIN1) + vector(vectors, VEC_SHIFT1)
        unit, scale = normalise(first + acc[rows, :] + vector(vectors, VEC_SHRINK))
        result = unit * vector(vectors, VEC_GAIN2) + vector(vectors, VEC_SHIFT2)
        live = live_mask(lengths_ref, skip_ref, (256, 1), 256 * block)
        frames[rows, :] = jnp.where(live, result, frames[rows, :].astype(F32)).astype(BF16)
        cotangent = jnp.where(live, upstream[rows, :].astype(F32), 0.0)
        grad = norm_back(cotangent, vector(vectors, VEC_GAIN2), unit, scale)
        acc[rows, :] = grad
        summed_grad[rows, :] = grad.astype(BF16)
        sums[0] = sums[0] + jnp.sum(cotangent * unit, axis=0, keepdims=True)
        sums[1] = sums[1] + jnp.sum(cotangent, axis=0, keepdims=True)
        sums[2] = sums[2] + jnp.sum(grad, axis=0, keepdims=True)

    saves[2].start()

    def put(number, value):
        vector_out[0:1, 768 * number : 768 * (number + 1)] = value

    put(VEC_QUERY, jnp.zeros((1, 768), F32))
    put(VEC_VALUE, jnp.zeros((1, 768), F32))
    put(VEC_GAIN2, sums[0])
    put(VEC_SHIFT2, sums[1])
    put(VEC_SHRINK, sums[2])

    def shrink_back(chunk, carry):
        columns = wide_columns(chunk)
        total = jnp.zeros((1, 768), F32)
        for block in range(3):
            rows = rows_of(block)
            grad = dot(summed_grad[rows, :], shrink[columns, :], 1, 1) * load(1, 3 * chunk, 3, block).astype(F32)
            total = total + jnp.sum(grad, axis=0, keepdims=True)
            save(1, 3 * chunk, 3, block, grad)
        vector_out[0:1, pl.ds(pl.multiple_of(768 * (VEC_EXPAND + chunk), 768), 768)] = total
        for block in range(3):
            part = pl.ds(pl.multiple_of(768 * chunk + 256 * block, 256), 256)
            shrink[part, :] = dot(panel(0, 3 * chunk + block)[...], summed_grad[...], 0, 0).astype(BF16)
        return carry

    for chunk in range(4):
        shrink_back(chunk, 0)

    def expand_back(chunk, carry):
        columns = wide_columns(chunk)
        for block in range(3):
            rows = rows_of(block)
            acc[rows, :] = acc[rows, :] + dot(load(1, 3 * chunk, 3, block), expand[:, columns], 1, 1)
        for block in range(3):
            part = pl.ds(pl.multiple_of(768 * chunk + 256 * block, 256), 256)
            expand[:, part] = dot(hidden[...], panel(1, 3 * chunk + block)[...], 0, 0).astype(BF16)
        return carry

    for chunk in range(4):
        expand_back(chunk, 0)
    pack()
    feed_move.start()
    sums = [jnp.zeros((1, 768), F32) for _ in range(3)]
    for block in range(3):
        rows = rows_of(block)
        grad = acc[rows, :]
        unit = normed[rows, :]
        back = norm_back(grad, vector(vectors, VEC_GAIN1), unit, scales[rows, 0:1])
        acc[rows, :] = back
        branch_grad[rows, :] = back.astype(BF16)
        sums[0] = sums[0] + jnp.sum(grad * unit, axis=0, keepdims=True)
        sums[1] = sums[1] + jnp.sum(grad, axis=0, keepdims=True)
        sums[2] = sums[2] + jnp.sum(back, axis=0, keepdims=True)
    saves[3].start()
    saves[4].start()
    put(VEC_GAIN1, sums[0])
    put(VEC_SHIFT1, sums[1])
    put(VEC_OUTPUT, sums[2])
    hidden[...] = dot(ctx_t[...], branch_grad[...]).astype(BF16)
    move = pltpu.make_async_copy(hidden, output_out, local.at[31])
    move.start()
    feed_move.wait()
    move.wait()


def forward_call(lengths, skip, frames, upstream, *shards):
    square = shape(768, 768)
    return pl.pallas_call(
        forward_kernel,
        out_shape=(
            shape(1, VECTORS * 768, kind=F32), square, shape(768, 768, kind=F32), square, square,
            shape(96, 768, kind=F32), shape(3, 768, 768), square, square, square, square, square, shape(12, 768, 768),
            shape(PARTS * 128 * ROWS_F, LANES),
        ),
        in_specs=[SCALARS] * 2 + [ANYWHERE] * 2 + [WHOLE] * 20,
        out_specs=[WHOLE] + [ANYWHERE] * 13,
        scratch_shapes=[
            pltpu.VMEM((PARTS * 128 * ROWS_A, LANES), BF16),
            pltpu.VMEM((PARTS * 128 * ROWS_F, LANES), BF16),
            pltpu.VMEM((ROWS_ALL, 768), F32),
            pltpu.VMEM((128, 128), F32),
            pltpu.VMEM((3, 768, 768), BF16),
            pltpu.VMEM((768, 768), BF16),
            pltpu.VMEM((768, 3072), BF16),
            pltpu.VMEM((3072, 768), BF16),
            pltpu.VMEM((1, VECTORS * 768), F32),
        ]
        + [pltpu.VMEM((768, 768), kind) for kind in (BF16, BF16, F32, BF16, BF16)]
        + [pltpu.VMEM((96, 768), F32), pltpu.VMEM((2, 256, 768), BF16), pltpu.VMEM((768, 128), BF16)]
        + [pltpu.SemaphoreType.DMA((PARTS, 22))] * 4
        + [pltpu.SemaphoreType.DMA((39,))],
        compiler_params=pltpu.CompilerParams(collective_id=0, has_side_effects=True, vmem_limit_bytes=62 * 2**20),
        name="forward",
    )(
        lengths, skip, frames, upstream, *shards,
        jnp.asarray(attention_rows(), BF16), jnp.asarray(expand_rows(), BF16), jnp.asarray(shrink_rows(), BF16),
        jnp.asarray(expand_rows().T, BF16), jnp.asarray(shrink_rows().T, BF16),
    )


class Scatter:
    def __init__(self, place, own, outgoing, other, far, near, second, first, rows, send, recv):
        self.place, self.own, self.outgoing, self.other = place, own, outgoing, other
        self.rows, self.send, self.recv = rows, send, recv
        self.buffers = (far, near, second, first)

    def mine(self, part):
        return tuple(self.place.along(part, stage) for stage in (2, 1, 0))

    def rows_of(self, ref, start, count):
        return rows_at(ref, start * self.rows, count * self.rows)

    def view(self, part, third, second=0, first=0, count=1, ref=None):
        return self.rows_of(self.own if ref is None else ref, ((part * 4 + third) * 4 + second) * 4 + first, count)

    def across(self, part, third, second=0, count=16):
        return self.view(part, third, second, 0, count, self.other)

    def landing(self, kind, part, slot):
        slots, count = ((2, 8), (2, 16), (3, 4), (3, 1))[kind]
        return self.rows_of(self.buffers[kind], (part * slots + slot) * count, count)

    def start(self, part, number, source, target, device):
        remote(source, target, self.send.at[part, number], self.recv.at[part, number], device).start()

    def arrived(self, part, number, view):
        remote(view, view, self.send.at[part, number], self.recv.at[part, number], self.place.sibling()).wait_recv()

    def accumulate(self, target, sources, count):
        group = min(count, 8)
        size = group * self.rows

        def body(number, carry):
            rows = pl.ds(pl.multiple_of(number * size, size), size)
            total = target[rows, :].astype(F32)
            for source in sources:
                total = total + source[rows, :].astype(F32)
            target[rows, :] = total.astype(BF16)
            return carry

        lax.fori_loop(0, count // group, body, 0)

    def exchange(self):
        for slot, step in enumerate((2, 1, 3, 0)):
            for part in range(PARTS):
                third = self.place.along(part, 2, step)
                source = self.view(part, third, count=16, ref=self.outgoing)
                self.start(part, slot, source, self.across(part, third), self.place.sibling())

    def far_out(self):
        for part in range(PARTS):
            third = self.place.along(part, 2, 2)
            self.arrived(part, 0, self.across(part, third))
            self.accumulate(self.view(part, third, count=16), [self.across(part, third)], 16)
            for half, step in ((0, 1), (1, 3)):
                source = self.view(part, third, 2 * half, count=8)
                self.start(part, 4 + half, source, self.landing(0, part, half), self.place.peer(part, 2, step))

    def near_out(self):
        for part in range(PARTS):
            for half, step in ((0, 1), (1, 3)):
                third = self.place.along(part, 2, step)
                self.arrived(part, 1 + half, self.across(part, third))
                self.arrived(part, 4 + half, self.landing(0, part, half))
                for side in (0, 1):
                    sources = [self.across(part, third, 2 * side, 8)]
                    if side == half:
                        sources.append(self.landing(0, part, half))
                    self.accumulate(self.view(part, third, 2 * side, count=8), sources, 8)
                source = self.view(part, third, count=16)
                self.start(part, 6 + half, source, self.landing(1, part, half), self.place.peer(part, 2, step))

    def second_out(self):
        for part in range(PARTS):
            third, second, first = self.mine(part)
            self.arrived(part, 3, self.across(part, third))
            for half in (0, 1):
                self.arrived(part, 6 + half, self.landing(1, part, half))
            sources = [self.across(part, third), self.landing(1, part, 0), self.landing(1, part, 1)]
            self.accumulate(self.view(part, third, count=16), sources, 16)
            for step in (1, 3, 2):
                source = self.view(part, third, self.place.along(part, 1, step), count=4)
                target = self.landing(2, part, step - 1)
                self.start(part, 7 + step, source, target, self.place.peer(part, 1, step))

    def first_out(self):
        for part in range(PARTS):
            third, second, first = self.mine(part)
            for step in (1, 3, 2):
                self.arrived(part, 7 + step, self.landing(2, part, step - 1))
            sources = [self.landing(2, part, slot) for slot in range(3)]
            self.accumulate(self.view(part, third, second, count=4), sources, 4)
            for step in (1, 3, 2):
                source = self.view(part, third, second, self.place.along(part, 0, step))
                target = self.landing(3, part, step - 1)
                self.start(part, 10 + step, source, target, self.place.peer(part, 0, step))

    def total(self, out, place):
        for part in range(PARTS):
            third, second, first = self.mine(part)
            for step in (1, 3, 2):
                self.arrived(part, 10 + step, self.landing(3, part, step - 1))
            value = self.view(part, third, second, first)[...].astype(F32)
            for slot in range(3):
                value = value + self.landing(3, part, slot)[...].astype(F32)
            out[place : place + self.rows, LANES * part : LANES * (part + 1)] = value

    def sent(self):
        for part in range(PARTS):
            for number in range(14):
                count = 16 if number < 4 else 8 if number < 6 else 16 if number < 8 else 4 if number < 11 else 1
                view = self.view(part, 0, count=count)
                remote(view, view, self.send.at[part, number], self.recv.at[part, number], self.place.sibling()).wait_send()


def pack_attention(early, grads, spread, back_a_ref, core, ref):
    for number in range(8):
        dp = number * 2 + core
        rows = pl.ds(pl.multiple_of(dp * 48, 16), 48)
        for part in range(PARTS):
            columns = slice(LANES * part, LANES * (part + 1))
            pieces = [grad[rows, columns] for grad in grads]
            if part == 0:
                tail = spread[pl.ds(pl.multiple_of(dp * 8, 8), 8), :]
                tail = jnp.concatenate([tail, jnp.zeros((8, 128), F32)], axis=0)
                tail = jnp.concatenate([tail, jnp.zeros((16, 128), F32)], axis=1)
            else:
                tail = jnp.zeros((16, LANES), F32)
            blocks = dot(back_a_ref[...], jnp.concatenate(pieces + [tail.astype(BF16)], axis=0)).astype(BF16)
            for device, index in enumerate(chunk_blocks(part, number // 4, number % 4, 0)):
                target = early.view(part, *index[2:], ref=ref)
                target[...] = blocks[ROWS_A * device : ROWS_A * (device + 1)]


def pack_vectors(vectors, numbers):
    packed = jnp.zeros((128, 128), F32)
    for number in numbers:
        wide = 6 if number < 8 else 24
        mask = owner_mask(0 if number < 8 else 768 * (number - 8), wide)
        whole = jnp.where(mask, vectors[number], 0.0).astype(BF16)
        packed = packed + dot(whole, vector_lanes(number), 1, 1)
    return packed


def backward_kernel(
    lengths_ref, skip_ref, inverse, vector_in, back_a_ref,
    frames_in, upstream_in, q_in, k_in, v_in, ctx_in, probs_in, branch_in, residual_in, attend_in, output_in, output_grad_in,
    feed_in,
    summed, frames_grad,
    own_f, own_a, outgoing_a, other_a, other_f, far_f, near_f, second_f, first_f, far_a, near_a, second_a, first_a,
    attend, output_weight, q_n, k_t, v_n, ctx_t, frames, branch, scaled_t, dk_n, dq_t, dv_t, score_grad, probs,
    ctx_grad, right, ones_mask, spread,
    send_a, recv_a, send_f, recv_f, local,
):
    place = Place()
    core = place.at[3]
    greet(place)
    pairs = (
        (output_in, output_weight), (branch_in, branch), (v_in, v_n), (ctx_in, ctx_t), (k_in, k_t), (q_in, q_n),
        (feed_in.at[pl.ds(pl.multiple_of(core * HALF_F, 16), HALF_F), :], own_f), (frames_in, frames), (attend_in, attend),
    )
    loads = [pltpu.make_async_copy(source, target, local.at[i]) for i, (source, target) in enumerate(pairs)]
    later = [
        pltpu.make_async_copy(output_grad_in, output_weight, local.at[9]),
        pltpu.make_async_copy(upstream_in, branch, local.at[10]),
        pltpu.make_async_copy(residual_in, ctx_grad, local.at[11]),
        pltpu.make_async_copy(scaled_t, frames_grad, local.at[12]),
    ]

    def prob_load(head, slot):
        return pltpu.make_async_copy(probs_in.at[head], probs.at[slot], local.at[13 + slot])

    for item in loads[:4]:
        item.start()
    prob_load(0, 0).start()
    for item in loads[4:6]:
        item.start()
    prob_load(1, 1).start()
    prob_load(2, 2).start()
    for item in loads[6:]:
        item.start()
    outgoing = feed_in.at[pl.ds(pl.multiple_of((1 - core) * HALF_F, 16), HALF_F), :]
    late = Scatter(place, own_f, outgoing, other_f, far_f, near_f, second_f, first_f, ROWS_F, send_f, recv_f)
    early = Scatter(
        place, own_a, outgoing_a, other_a,
        far_a, near_a, second_a, first_a, ROWS_A, send_a, recv_a,
    )
    lane = lax.broadcasted_iota(jnp.int32, (768, 128), 1)
    ones_mask[...] = jnp.where(lane < 2, 1.0, 0.0).astype(BF16)
    for side in range(2):
        right[side] = jnp.zeros((256, 768), BF16)
    meet()
    late.exchange()
    spread[...] = pack_vectors([vector(vector_in, i) for i in range(VECTORS)], range(2, VECTORS))
    loads[0].wait()
    loads[1].wait()
    ctx_grad[...] = dot(output_weight[...], branch[...], 1, 1)
    later[0].start()
    later[1].start()
    for item in loads[2:4]:
        item.wait()
    prob_load(0, 0).wait()

    def score_stage(pair, side):
        head = pair * 2 + side
        rows = head_rows(head)
        factor = inverse[pl.ds(pl.multiple_of(head * 8, 8), 8), :][0:1]
        scaled = (ctx_grad[rows, :] * factor).astype(BF16)
        scaled_t[rows, :] = scaled
        right[side, 64 * side : 64 * side + 64] = scaled
        inner = jnp.sum(scaled.astype(F32) * ctx_t[rows, :].astype(F32), axis=0, keepdims=True)
        high = inner.astype(BF16).astype(F32)
        row = lax.broadcasted_iota(jnp.int32, (16, 768), 0)
        right[side, 128:144] = jnp.where(row == 0, -high, jnp.where(row == 1, high - inner, 0.0)).astype(BF16)
        left = jnp.concatenate([v_n[:, pair_lanes(pair)], ones_mask[...]], axis=1)
        score_grad[side] = (dot(left, right[side]) * probs[lax.rem(head, 3)].astype(F32)).astype(BF16)

    def use_stage(pair, side):
        head = pair * 2 + side
        rows = head_rows(head)
        lanes = pair_lanes(pair)
        dv_t[rows, :] = dot(scaled_t[rows, :], probs[lax.rem(head, 3)], 1, 1).astype(BF16)
        dq_t[rows, :] = (dot(k_t[rows, :], score_grad[side]) * SCALE).astype(BF16)
        keys = dot(score_grad[side], q_n[:, lanes]).astype(BF16)
        if side == 1:
            keys = jnp.where(lax.broadcasted_iota(jnp.int32, (768, 128), 1) < 64, dk_n[:, lanes], keys)
        dk_n[:, lanes] = keys

    def refill(head):
        @pl.when(head + 3 < 12)
        def _():
            prob_load(head + 3, lax.rem(head, 3)).start()

        @pl.when(head + 2 < 12)
        def _():
            prob_load(head + 2, lax.rem(head + 2, 3)).wait()

    score_stage(0, 0)
    for item in loads[4:6]:
        item.wait()
    prob_load(1, 1).wait()
    loads[6].wait()
    steps = (None, late.far_out, late.near_out, None, None, late.second_out)

    def body(pair, carry):
        for number, step in enumerate(steps):
            if step is not None:
                pl.when(pair == number)(step)
        score_stage(pair, 1)
        use_stage(pair, 0)
        refill(pair * 2)
        score_stage(jnp.minimum(pair + 1, 5), 0)
        use_stage(pair, 1)
        refill(pair * 2 + 1)
        return carry

    lax.fori_loop(0, 6, body, 0)
    later[2].start()
    loads[7].wait()
    loads[8].wait()
    x = frames[...]
    queries, values = score_grad.at[0], score_grad.at[1]
    queries[...] = dq_t[...].T
    values[...] = dv_t[...].T
    grads = (k_t, q_n, v_n, output_weight)
    k_t[...] = dot(x, queries[...], 0, 0).astype(BF16)
    q_n[...] = dot(x, dk_n[...], 0, 0).astype(BF16)
    v_n[...] = dot(x, values[...], 0, 0).astype(BF16)
    sums = [jnp.sum(ref[...].astype(F32), axis=0, keepdims=True) for ref in (queries, values)]
    spread[...] = spread[...] + pack_vectors(sums, range(2))
    later[0].wait()
    late.first_out()
    pack_attention(early, grads, spread, back_a_ref, 1 - core, outgoing_a)
    early.exchange()
    pack_attention(early, grads, spread, back_a_ref, core, own_a)
    later[1].wait()
    later[2].wait()

    def finish_rows(block):
        rows = slice(256 * block, 256 * (block + 1))
        live = live_mask(lengths_ref, skip_ref, (256, 1), 256 * block)
        total = ctx_grad[rows, :] + dot(queries[rows, :], attend[0], 1, 1) + dot(dk_n[rows, :], attend[1], 1, 1)
        total = total + dot(values[rows, :], attend[2], 1, 1)
        scaled_t[rows, :] = jnp.where(live, total, branch[rows, :].astype(F32)).astype(BF16)

    early.far_out()
    finish_rows(0)
    early.near_out()
    finish_rows(1)
    finish_rows(2)
    later[3].start()
    late.total(summed, ROWS_A)
    late.sent()
    early.second_out()
    early.first_out()
    early.total(summed, 0)
    later[3].wait()
    early.sent()


def backward_call(*args):
    square = pltpu.VMEM((768, 768), BF16)

    def blocks(count, rows):
        return pltpu.VMEM((PARTS * count * rows, LANES), BF16)

    return pl.pallas_call(
        backward_kernel,
        out_shape=(shape(ROWS_ALL, 768, kind=F32), shape(768, 768)),
        in_specs=[SCALARS] * 2 + [WHOLE] * 3 + [ANYWHERE] * 13,
        out_specs=[WHOLE, ANYWHERE],
        scratch_shapes=[blocks(64, ROWS_F)] + [blocks(64, ROWS_A)] * 3 + [blocks(64, ROWS_F)]
        + [blocks(count, ROWS_F) for count in (16, 32, 12, 3)]
        + [blocks(count, ROWS_A) for count in (16, 32, 12, 3)]
        + [pltpu.VMEM((3, 768, 768), BF16)]
        + [square] * 11
        + [
            pltpu.VMEM((2, 768, 768), BF16), pltpu.VMEM((3, 768, 768), BF16), pltpu.VMEM((768, 768), F32),
            pltpu.VMEM((2, 256, 768), BF16), pltpu.VMEM((768, 128), BF16), pltpu.VMEM((128, 128), F32),
        ]
        + [pltpu.SemaphoreType.DMA((PARTS, 14))] * 4
        + [pltpu.SemaphoreType.DMA((16,))],
        compiler_params=pltpu.CompilerParams(collective_id=1, has_side_effects=True, vmem_limit_bytes=62 * 2**20),
        name="backward",
    )(*args)


def deliver_kernel(summed, encoded_in, frames_in, encoded_out, frames_out, *rest):
    query_out, key_out, value_out, output_out, expand_out, shrink_out, *vectors = rest
    encoded_out[...] = encoded_in[...]
    frames_out[...] = frames_in[...]
    for number, target in enumerate((query_out, key_out, value_out, output_out)):
        target[...] = summed[6 * number : 6 * number + 6, :]
    for number in range(4):
        expand_out[:, 768 * number : 768 * (number + 1)] = summed[32 + 6 * number : 38 + 6 * number, :]
    shrink_out[...] = summed[56:80, :]
    for at, target in zip(PLACES, vectors, strict=True):
        target[...] = summed[24, at : at + target.shape[0]]


def deliver(summed, encoded, frames_grad):
    sizes = ((6, 768),) * 4 + ((6, 3072), (24, 768)) + ((6,),) * 8 + ((24,),)
    return pl.pallas_call(
        deliver_kernel,
        out_shape=(shape(768, 768), shape(768, 768)) + tuple(shape(*s, kind=F32) for s in sizes),
        in_specs=[WHOLE] * 3,
        out_specs=[WHOLE] * 17,
        name="deliver",
    )(summed, encoded, frames_grad)


PLACES = (0, 6, 12, 18, 24, 30, 36, 42, 48)


def local(
    frames,
    upstream,
    clip_lengths,
    clip_skip,
    query_weight,
    key_weight,
    value_weight,
    output_weight,
    query_bias,
    value_bias,
    output_bias,
    first_gain,
    first_shift,
    expand_weight,
    shrink_weight,
    expand_bias,
    shrink_bias,
    second_gain,
    second_shift,
):
    vectors = (
        query_bias, value_bias, output_bias, first_gain, first_shift, shrink_bias, second_gain, second_shift, expand_bias,
    )
    (
        vector_grad, encoded, residual_grad, branch_grad, ctx_t, inverse,
        attend, output, output_grad, q_n, k_t, v_n, probs, feed_grad,
    ) = forward_call(
        clip_lengths, clip_skip, frames, upstream,
        query_weight, key_weight, value_weight, output_weight, expand_weight, shrink_weight, *vectors,
    )
    summed, frames_grad = backward_call(
        clip_lengths, clip_skip, inverse, vector_grad,
        jnp.asarray(attention_rows().T, BF16),
        frames, upstream, q_n, k_t, v_n, ctx_t, probs, branch_grad, residual_grad, attend, output, output_grad, feed_grad,
    )
    encoded, frames_grad, query_sum, key_sum, value_sum, output_sum, expand_sum, shrink_sum, *sums = deliver(
        summed, encoded, frames_grad
    )
    return (
        encoded, frames_grad, query_sum, key_sum, value_sum, output_sum, sums[0], sums[1], sums[2], sums[3], sums[4],
        expand_sum, shrink_sum, sums[8], sums[5], sums[6], sums[7],
    )


def solution(mesh):
    return jax.shard_map(
        local,
        mesh=mesh,
        in_specs=(
            P(("dp", "fsdp"), None),
            P(("dp", "fsdp"), None),
            P(("dp", "fsdp"), None),
            P(("dp", "fsdp"), None),
            P(("dp", "fsdp"), None),
            P(("dp", "fsdp"), None),
            P(("dp", "fsdp"), None),
            P(("dp", "fsdp"), None),
            P(("dp", "fsdp")),
            P(("dp", "fsdp")),
            P(("dp", "fsdp")),
            P(("dp", "fsdp")),
            P(("dp", "fsdp")),
            P(("dp", "fsdp"), None),
            P(("dp", "fsdp"), None),
            P(("dp", "fsdp")),
            P(("dp", "fsdp")),
            P(("dp", "fsdp")),
            P(("dp", "fsdp")),
        ),
        out_specs=(
            P(("dp", "fsdp"), None),
            P(("dp", "fsdp"), None),
            P(("dp", "fsdp"), None),
            P(("dp", "fsdp"), None),
            P(("dp", "fsdp"), None),
            P(("dp", "fsdp"), None),
            P(("dp", "fsdp")),
            P(("dp", "fsdp")),
            P(("dp", "fsdp")),
            P(("dp", "fsdp")),
            P(("dp", "fsdp")),
            P(("dp", "fsdp"), None),
            P(("dp", "fsdp"), None),
            P(("dp", "fsdp")),
            P(("dp", "fsdp")),
            P(("dp", "fsdp")),
            P(("dp", "fsdp")),
        ),
        check_vma=False,
    )
```

```python
import functools
import math

import jax
import jax.numpy as jnp
import numpy as np
from jax import lax
from jax.experimental import pallas as pl
from jax.experimental.pallas import tpu as pltpu
from jax.sharding import PartitionSpec as P

epsilon = 1e-05

SCALE = 0.125
LN2 = math.log(2.0)
EXCLUDED = -1e30
F32 = jnp.float32
BF16 = jnp.bfloat16
WHOLE = pl.BlockSpec(memory_space=pltpu.VMEM)
SCALARS = pl.BlockSpec(memory_space=pltpu.SMEM)
ANYWHERE = pl.BlockSpec(memory_space=pl.ANY)
VEC_QUERY, VEC_VALUE, VEC_OUTPUT, VEC_GAIN1, VEC_SHIFT1, VEC_SHRINK, VEC_GAIN2, VEC_SHIFT2, VEC_EXPAND = range(9)


def dot(left, right, a=1, b=0):
    return lax.dot_general(left, right, (((a,), (b,)), ((), ())), preferred_element_type=F32)


def shape(*sizes, kind=jnp.bfloat16):
    return jax.ShapeDtypeStruct(sizes, kind)


def segments(lengths_ref, axis, extent, first=0):
    place = lax.broadcasted_iota(jnp.int32, extent, axis) + first
    first_end = lengths_ref[0, 0]
    second_end = first_end + lengths_ref[0, 1]
    return jnp.where(place < first_end, 0, jnp.where(place < second_end, 1, 2))


def live_mask(lengths_ref, skip_ref, extent, first):
    segment = segments(lengths_ref, 0, extent, first)
    dropped = jnp.where(segment == 0, skip_ref[0, 0], jnp.where(segment == 1, skip_ref[0, 1], 1))
    return dropped == 0


def vector(ref, number):
    return ref[0:1, 768 * number : 768 * (number + 1)]


def head_rows(head):
    return pl.ds(pl.multiple_of(head * 64, 64), 64)


def pair_lanes(pair):
    return pl.ds(pl.multiple_of(pair * 128, 128), 128)


def project(frames, attend, vectors, q_n, k_n, v_n, q_t, k_t, v_t):
    x = frames[...]
    q_n[...] = ((dot(x, attend[0]) + vector(vectors, VEC_QUERY)) * (SCALE / LN2)).astype(BF16)
    q_t[...] = q_n[...].T
    k_n[...] = dot(x, attend[1]).astype(BF16)
    k_t[...] = k_n[...].T
    v_n[...] = (dot(x, attend[2]) + vector(vectors, VEC_VALUE)).astype(BF16)
    v_t[...] = v_n[...].T


def mask_operands(lengths_ref, right, k_mask):
    lane = lax.broadcasted_iota(jnp.int32, (768, 128), 1)
    k_mask[...] = jnp.where(lane == segments(lengths_ref, 0, (768, 128)), 1.0, 0.0).astype(BF16)
    row = lax.broadcasted_iota(jnp.int32, (128, 768), 0)
    other = (row < 3) & (row != segments(lengths_ref, 1, (128, 768)))
    other = jnp.where(other, EXCLUDED, 0.0).astype(BF16)
    for side in range(2):
        right[side, 128:256] = other
        right[side, 64 * (1 - side) : 64 * (1 - side) + 64] = jnp.zeros((64, 768), BF16)


def score_stage(pair, side, q_t, k_n, k_mask, right, scores, tops):
    left = jnp.concatenate([k_n[:, pair_lanes(pair)], k_mask[...]], axis=1)
    right[side, 64 * side : 64 * side + 64] = q_t[head_rows(pair * 2 + side), :]
    values = dot(left, right[side])
    scores[side] = values
    tops[side] = jnp.broadcast_to(jnp.max(values, axis=0, keepdims=True), (8, 768))


def prob_stage(pair, side, v_t, scores, tops, probs, inverse, ctx_t):
    head = pair * 2 + side
    rows = head_rows(head)
    left = jnp.concatenate([v_t[rows, :], jnp.ones((16, 768), BF16)], axis=0)
    raised = jnp.exp2(scores[side] - tops[side, 0:1]).astype(BF16)
    probs[side][...] = raised
    total = dot(left, raised)
    factor = 1.0 / total[64:65]
    inverse[pl.ds(pl.multiple_of(head * 8, 8), 8), :] = jnp.broadcast_to(factor, (8, 768))
    ctx_t[rows, :] = (total[:64] * factor).astype(BF16)


def gelu_pair(v):
    base = 1.0 + (0.3275911 / math.sqrt(2.0)) * jnp.abs(v)
    t = pl.reciprocal(base, approx=True)
    t = t * (2.0 - base * t)
    e = jnp.exp2((v * v) * (-0.5 / math.log(2.0)))
    poly = t * (0.127414796 + t * (-0.142248368 + t * (0.7107068705 + t * (-0.7265760135 + t * 0.5307027145))))
    tail = poly * e
    phi = jnp.where(v >= 0, 1.0 - tail, tail)
    return v * phi, phi + v * e * (1.0 / math.sqrt(2.0 * math.pi))


def normalise(values):
    centered = values - jnp.mean(values, axis=-1, keepdims=True)
    scale = lax.rsqrt(jnp.mean(centered * centered, axis=-1, keepdims=True) + epsilon)
    return centered * scale, scale


def norm_back(cotangent, gain, normed, scale):
    c = cotangent * gain
    return scale * (
        c - jnp.mean(c, axis=-1, keepdims=True) - normed * jnp.mean(c * normed, axis=-1, keepdims=True)
    )


MESH = pl.DeviceIdType.MESH
ROWS_A = 32
ROWS_F = 48
ROWS_ALL = ROWS_A + ROWS_F
LANES = 256
PARTS = 3
HALF_F = PARTS * 64 * ROWS_F
VECTORS = 12
BIAS_OUT = 208


def attention_rows():
    table = np.zeros((BIAS_OUT, 8 * ROWS_A), np.float32)
    for row in range(192):
        matrix, inner = divmod(row, 48)
        device, lane = divmod(inner, 6)
        table[row, device * ROWS_A + 6 * matrix + lane] = 1
    for device in range(8):
        table[192 + device, device * ROWS_A + 24] = 1
    return table


def expand_rows():
    table = np.zeros((192, 256), np.float32)
    for row in range(192):
        matrix, inner = divmod(row, 48)
        device, lane = divmod(inner, 6)
        table[row, 32 * device + 6 * matrix + lane] = 1
    return table


def shrink_rows():
    table = np.zeros((192, 256), np.float32)
    for row in range(192):
        device, lane = divmod(row, 24)
        table[row, 32 * device + 8 + lane] = 1
    return table


def vector_lanes(number):
    lane = lax.broadcasted_iota(jnp.int32, (128, 768), 0)
    column = lax.broadcasted_iota(jnp.int32, (128, 768), 1)
    if number < 8:
        wanted = column - 6 * ((column * 10923) >> 16) + 6 * number
    else:
        wanted = column - 24 * ((column * 2731) >> 16) + 48
    return jnp.where(lane == wanted, 1.0, 0.0).astype(BF16)


def owner_mask(first, wide):
    device = lax.broadcasted_iota(jnp.int32, (128, 768), 0)
    column = lax.broadcasted_iota(jnp.int32, (128, 768), 1) + first
    low = device * wide
    return (column >= low) & (column < low + wide)


def position():
    dp = lax.axis_index("dp")
    fsdp = lax.axis_index("fsdp")
    core = lax.rem(dp, 2)
    y = lax.rem(lax.div(dp, 2), 4)
    z = lax.div(dp, 8) * 2 + lax.div(fsdp, 4)
    x = lax.rem(fsdp, 4)
    return x, y, z, core


def device_of(x, y, z, core):
    return ((lax.div(z, 2) * 4 + y) * 2 + core, lax.rem(z, 2) * 4 + x)


AXES = ((0, 1, 2), (1, 2, 0), (2, 0, 1))


class Place:
    def __init__(self):
        self.at = position()
        x, y, z, core = self.at
        self.turns = [[at] + [lax.rem(at + step, 4) for step in (1, 2, 3)] for at in (x, y, z)]
        self.twin = device_of(x, y, z, 1 - core)
        self.devices = {}
        for axis in range(3):
            for step in (1, 2, 3):
                where = list(self.at)
                where[axis] = self.turns[axis][step]
                self.devices[axis, step] = device_of(*where)

    def along(self, part, stage, step=0):
        return self.turns[AXES[part][stage]][step]

    def peer(self, part, stage, step):
        return self.devices[AXES[part][stage], step]

    def sibling(self):
        return self.twin


def greet(place):
    for target in (place.twin, *place.devices.values()):
        pl.semaphore_signal(pltpu.get_barrier_semaphore(), inc=1, device_id=target, device_id_type=MESH)


def meet():
    pl.semaphore_wait(pltpu.get_barrier_semaphore(), 10)


def remote(source, target, send, receive, device):
    return pltpu.make_async_remote_copy(
        src_ref=source,
        dst_ref=target,
        send_sem=send,
        recv_sem=receive,
        device_id=device,
        device_id_type=MESH,
    )


def chunk_blocks(part, high, y, core):
    blocks = []
    for low in range(2):
        for x in range(4):
            where = (x, y, high * 2 + low)
            first, second, third = (where[a] for a in AXES[part])
            blocks.append((part, core, third, second, first))
    return blocks


def rows_at(ref, start, count):
    if isinstance(start, int):
        return ref.at[start : start + count, :]
    return ref.at[pl.ds(pl.multiple_of(start, 16), count), :]


class Gather:
    def __init__(self, place, held, rows, send, recv):
        self.place, self.held, self.rows, self.send, self.recv = place, held, rows, send, recv
        self.core = place.at[3]

    def view(self, part, core, third, second=0, first=0, count=1):
        start = (((core * PARTS + part) * 4 + third) * 4 + second) * 4 + first
        return rows_at(self.held, start * self.rows, count * self.rows)

    def mine(self, part):
        return tuple(self.place.along(part, stage) for stage in (2, 1, 0))

    def copy(self, part, number, view, device):
        return remote(view, view, self.send.at[part, number], self.recv.at[part, number], device)

    def start(self, part, number, view, device):
        self.copy(part, number, view, device).start()

    def arrived(self, part, number, view):
        self.copy(part, number, view, self.place.sibling()).wait_recv()

    def block(self, part, third, second, first):
        return self.view(part, self.core, third, second, first)

    def two(self, part, third, second, half):
        return self.view(part, self.core, third, second, 2 * half, 2)

    def eight(self, part, core, third, half):
        return self.view(part, core, third, 2 * half, 0, 8)

    def first(self):
        for part in range(PARTS):
            view = self.block(part, *self.mine(part))
            for step in (1, 3, 2):
                self.start(part, step - 1, view, self.place.peer(part, 0, step))

    def second(self):
        for part in range(PARTS):
            third, second, first = self.mine(part)
            for step in (1, 3, 2):
                self.arrived(part, step - 1, self.block(part, third, second, self.place.along(part, 0, 4 - step)))
            ahead, behind = self.place.peer(part, 1, 1), self.place.peer(part, 1, 3)
            for half in (0, 1):
                self.start(part, 3 + half, self.two(part, third, second, half), ahead)
                self.start(part, 6 - half, self.two(part, third, second, 1 - half), behind)

    def second_on(self):
        for part in range(PARTS):
            third, second, first = self.mine(part)
            ahead, behind = self.place.peer(part, 1, 1), self.place.peer(part, 1, 3)
            view = self.two(part, third, self.place.along(part, 1, 3), 0)
            self.arrived(part, 3, view)
            self.start(part, 7, view, ahead)
            view = self.two(part, third, self.place.along(part, 1, 1), 1)
            self.arrived(part, 6, view)
            self.start(part, 8, view, behind)

    def third(self):
        for part in range(PARTS):
            third, second, first = self.mine(part)
            self.arrived(part, 4, self.two(part, third, self.place.along(part, 1, 3), 1))
            self.arrived(part, 5, self.two(part, third, self.place.along(part, 1, 1), 0))
            for half in (0, 1):
                self.arrived(part, 7 + half, self.two(part, third, self.place.along(part, 1, 2), half))
            ahead, behind = self.place.peer(part, 2, 1), self.place.peer(part, 2, 3)
            for half in (0, 1):
                self.start(part, 9 + half, self.eight(part, self.core, third, half), ahead)
                self.start(part, 12 - half, self.eight(part, self.core, third, 1 - half), behind)
            self.start(part, 15, self.view(part, self.core, third, count=16), self.place.sibling())

    def third_on(self):
        for part in range(PARTS):
            third, second, first = self.mine(part)
            ahead, behind = self.place.peer(part, 2, 1), self.place.peer(part, 2, 3)
            view = self.eight(part, self.core, self.place.along(part, 2, 3), 0)
            self.arrived(part, 9, view)
            self.start(part, 13, view, ahead)
            self.start(part, 16, view, self.place.sibling())
            view = self.eight(part, self.core, self.place.along(part, 2, 1), 1)
            self.arrived(part, 12, view)
            self.start(part, 14, view, behind)
            self.start(part, 17, view, self.place.sibling())

    def near_over(self):
        for part in range(PARTS):
            third, second, first = self.mine(part)
            view = self.eight(part, self.core, self.place.along(part, 2, 3), 1)
            self.arrived(part, 10, view)
            self.start(part, 18, view, self.place.sibling())
            view = self.eight(part, self.core, self.place.along(part, 2, 1), 0)
            self.arrived(part, 11, view)
            self.start(part, 19, view, self.place.sibling())

    def far_over(self):
        for part in range(PARTS):
            third, second, first = self.mine(part)
            for half in (0, 1):
                view = self.eight(part, self.core, self.place.along(part, 2, 2), half)
                self.arrived(part, 13 + half, view)
                self.start(part, 20 + half, view, self.place.sibling())

    def finish(self):
        other = 1 - self.core
        for part in range(PARTS):
            third, second, first = self.mine(part)
            self.arrived(part, 15, self.view(part, other, third, count=16))
            self.arrived(part, 16, self.eight(part, other, self.place.along(part, 2, 3), 0))
            self.arrived(part, 17, self.eight(part, other, self.place.along(part, 2, 1), 1))
            self.arrived(part, 18, self.eight(part, other, self.place.along(part, 2, 3), 1))
            self.arrived(part, 19, self.eight(part, other, self.place.along(part, 2, 1), 0))
            for half in (0, 1):
                self.arrived(part, 20 + half, self.eight(part, other, self.place.along(part, 2, 2), half))

    def sent(self):
        for part in range(PARTS):
            for number in range(22):
                if number < 3:
                    view = self.block(part, 0, 0, 0)
                elif number < 9:
                    view = self.two(part, 0, 0, 0)
                elif number == 15:
                    view = self.view(part, self.core, 0, count=16)
                else:
                    view = self.eight(part, self.core, 0, 0)
                self.copy(part, number, view, self.place.sibling()).wait_send()


def unpack_attention(held, rows_a_ref, attend, output, vectors, spread):
    def body(y, carry):
        for high, core in ((0, 0), (0, 1), (1, 0), (1, 1)):
            start = 8 * high + core
            rows = pl.ds(pl.multiple_of(48 * start + 96 * y, 16), 48)
            for part in range(PARTS):
                columns = slice(LANES * part, LANES * (part + 1))
                blocks = jnp.concatenate([held.view(*index)[...] for index in chunk_blocks(part, high, y, core)], axis=0)
                blocks = dot(rows_a_ref[...], blocks)
                if part == 0:
                    spread[pl.ds(pl.multiple_of(8 * start + 16 * y, 8), 8), :] = blocks[192:200, :128]
                blocks = blocks.astype(BF16)
                for matrix in range(3):
                    attend[matrix, rows, columns] = blocks[48 * matrix : 48 * (matrix + 1)]
                output[rows, columns] = blocks[144:192]
        return carry

    lax.fori_loop(0, 4, body, 0)

    packed = spread[...].astype(BF16)
    for number in range(VECTORS):
        wide = 6 if number < 8 else 24
        mask = owner_mask(0 if number < 8 else 768 * (number - 8), wide)
        columns = slice(768 * number, 768 * (number + 1))
        whole = dot(packed, vector_lanes(number))
        vectors[:, columns] = jnp.sum(jnp.where(mask, whole, 0.0), axis=0, keepdims=True)


def unpack_feed(held, rows_e_ref, rows_s_ref, expand, shrink, beside):
    def body(y, carry):
        beside(y)
        for high, core in ((0, 0), (0, 1), (1, 0), (1, 1)):
            start = 8 * high + core
            rows = pl.ds(pl.multiple_of(48 * start + 96 * y, 16), 48)
            for part in range(PARTS):
                columns = slice(LANES * part, LANES * (part + 1))
                blocks = [held.view(*index)[...] for index in chunk_blocks(part, high, y, core)]
                first = dot(rows_e_ref[...], jnp.concatenate([b[:32] for b in blocks], axis=0)).astype(BF16)
                second = dot(rows_s_ref[...], jnp.concatenate([b[16:] for b in blocks], axis=0)).astype(BF16)
                for matrix in range(4):
                    expand[rows, 768 * matrix + LANES * part : 768 * matrix + LANES * (part + 1)] = first[
                        48 * matrix : 48 * (matrix + 1)
                    ]
                shrink[pl.ds(pl.multiple_of(192 * start + 384 * y, 16), 192), columns] = second
        return carry

    lax.fori_loop(0, 4, body, 0)


def pack_feed(held, back_e_ref, back_s_ref, expand, shrink):
    def body(y, carry):
        for high, core in ((0, 0), (0, 1), (1, 0), (1, 1)):
            start = 8 * high + core
            rows = pl.ds(pl.multiple_of(48 * start + 96 * y, 16), 48)
            for part in range(PARTS):
                pieces = [
                    expand[rows, 768 * matrix + LANES * part : 768 * matrix + LANES * (part + 1)] for matrix in range(4)
                ]
                first = dot(back_e_ref[...], jnp.concatenate(pieces, axis=0))
                values = shrink[pl.ds(pl.multiple_of(192 * start + 384 * y, 16), 192), LANES * part : LANES * (part + 1)]
                second = dot(back_s_ref[...], values)
                for device, index in enumerate(chunk_blocks(part, high, y, core)):
                    at = 32 * device
                    block = held.view(*index)
                    block[0:16, :] = first[at : at + 16].astype(BF16)
                    block[16:32, :] = (first[at + 16 : at + 32] + second[at : at + 16]).astype(BF16)
                    block[32:48, :] = second[at + 16 : at + 32].astype(BF16)
        return carry

    lax.fori_loop(0, 4, body, 0)


def forward_kernel(
    lengths_ref, skip_ref, frames_in, upstream_in,
    query_in, key_in, value_in, output_in, expand_in, shrink_in,
    *rest,
):
    forward_body(
        lengths_ref, skip_ref, frames_in, upstream_in, query_in, key_in, value_in, output_in, expand_in, shrink_in,
        rest[:9], *rest[9:],
    )


def forward_body(
    lengths_ref, skip_ref, frames_in, upstream_in, query_in, key_in, value_in, output_in, expand_in, shrink_in,
    vectors_in, rows_a_ref, rows_e_ref, rows_s_ref, back_e_ref, back_s_ref,
    vector_out, encoded_out, residual_out, branch_out, ctx_out, inverse_out,
    attend_out, weight_out, output_out, q_out, k_out, v_out, probs_out, feed_out,
    held_a, held_f, block_ref, spread, attend, output_weight, expand, shrink, vectors,
    frames, upstream, residual_grad, branch_grad, ctx_t, inverse, right, k_mask,
    send_a, recv_a, send_f, recv_f, local,
):
    place = Place()
    core = place.at[3]
    greet(place)
    frames_load = pltpu.make_async_copy(frames_in, frames, local.at[32])
    upstream_load = pltpu.make_async_copy(upstream_in, upstream, local.at[33])
    frames_load.start()
    upstream_load.start()
    for number, source in enumerate((query_in, key_in, value_in, output_in)):
        block_ref[6 * number : 6 * number + 6, :] = source[...].astype(F32)
    block_ref[24:32, :] = jnp.zeros((8, 768), F32)
    for at, ref in zip(PLACES, vectors_in, strict=True):
        size = ref.shape[0]
        block_ref[24:25, at : at + size] = ref[...].astype(F32).reshape(1, size)
    for number in range(4):
        block_ref[32 + 6 * number : 38 + 6 * number, :] = expand_in[:, 768 * number : 768 * (number + 1)].astype(F32)
    block_ref[56:80, :] = shrink_in[...].astype(F32)
    early = Gather(place, held_a, ROWS_A, send_a, recv_a)
    late = Gather(place, held_f, ROWS_F, send_f, recv_f)
    for part in range(PARTS):
        third, second, first = early.mine(part)
        values = block_ref[:, LANES * part : LANES * (part + 1)].astype(BF16)
        early.block(part, third, second, first)[...] = values[:ROWS_A]
        late.block(part, third, second, first)[...] = values[ROWS_A:]
    mask_operands(lengths_ref, right, k_mask)
    meet()
    early.first()
    late.first()
    early.second()
    early.second_on()
    early.third()
    late.second()
    early.third_on()
    late.second_on()
    early.near_over()
    early.far_over()
    late.third()
    early.finish()
    unpack_attention(early, rows_a_ref, attend, output_weight, vectors, spread)
    keep = [
        pltpu.make_async_copy(attend, attend_out, local.at[0]),
        pltpu.make_async_copy(output_weight, weight_out, local.at[1]),
    ]
    for item in keep:
        item.start()
    late.third_on()

    def attention(scores, tops):
        q_n, k_n, v_n, q_t = (expand.at[:, 768 * i : 768 * (i + 1)] for i in range(4))
        k_t, v_t, *probs = (shrink.at[768 * i : 768 * (i + 1), :] for i in range(4))
        frames_load.wait()
        project(frames, attend, vectors, q_n, k_n, v_n, q_t, k_t, v_t)
        hold = [
            pltpu.make_async_copy(q_n, q_out, local.at[2]),
            pltpu.make_async_copy(k_t, k_out, local.at[3]),
            pltpu.make_async_copy(v_n, v_out, local.at[4]),
        ]
        for item in hold:
            item.start()
        score_stage(0, 0, q_t, k_n, k_mask, right, scores, tops)

        def away(head, side):
            return pltpu.make_async_copy(probs[side], probs_out.at[head], local.at[5 + side])

        def body(pair, carry):
            @pl.when(pair > 0)
            def _():
                away(0, 0).wait()

            @pl.when(pair == 1)
            def _():
                late.near_over()

            @pl.when(pair == 3)
            def _():
                late.far_over()

            score_stage(pair, 1, q_t, k_n, k_mask, right, scores, tops)
            prob_stage(pair, 0, v_t, scores, tops, probs, inverse, ctx_t)
            away(pair * 2, 0).start()

            @pl.when(pair > 0)
            def _():
                away(0, 1).wait()

            score_stage(jnp.minimum(pair + 1, 5), 0, q_t, k_n, k_mask, right, scores, tops)
            prob_stage(pair, 1, v_t, scores, tops, probs, inverse, ctx_t)
            away(pair * 2 + 1, 1).start()
            return carry

        lax.fori_loop(0, 6, body, 0)
        for side in range(2):
            away(0, side).wait()
        for item in hold:
            item.wait()

    square = pltpu.VMEM((768, 768), BF16)
    pl.run_scoped(
        attention, pltpu.VMEM((2, 768, 768), F32), pltpu.VMEM((2, 8, 768), F32),
    )
    saves = [
        pltpu.make_async_copy(ctx_t, ctx_out, local.at[34]),
        pltpu.make_async_copy(inverse, inverse_out, local.at[35]),
        pltpu.make_async_copy(frames, encoded_out, local.at[36]),
        pltpu.make_async_copy(residual_grad, residual_out, local.at[37]),
        pltpu.make_async_copy(branch_grad, branch_out, local.at[38]),
    ]
    saves[0].start()
    saves[1].start()
    late.finish()
    late.sent()
    upstream_load.wait()

    def feed(normed, scales, hidden, raw):
        feed_forward(
            lengths_ref, skip_ref, frames, upstream, ctx_t, output_weight, expand, shrink, vectors,
            residual_grad, branch_grad, output_out, vector_out,
            normed, scales, hidden, held_f, raw, branch_grad, local, saves,
            lambda beside: unpack_feed(late, rows_e_ref, rows_s_ref, expand, shrink, beside),
            lambda: pack_feed(late, back_e_ref, back_s_ref, expand, shrink),
            pltpu.make_async_copy(held_f, feed_out, local.at[7]),
        )

    pl.run_scoped(
        feed, pltpu.VMEM((768, 768), F32), pltpu.VMEM((768, 128), F32), square,
        pltpu.VMEM((2, 768, 512), F32),
    )
    for item in keep + saves:
        item.wait()
    early.sent()


def feed_forward(
    lengths_ref, skip_ref, frames, upstream, ctx_t, output_weight, expand, shrink, vectors,
    acc, branch_grad, output_out, vector_out,
    normed, scales, hidden, panels, raw, summed_grad, local, saves, unpack, pack, feed_move,
):
    def rows_of(block):
        return slice(256 * block, 256 * (block + 1))

    def wide_columns(chunk):
        return pl.ds(pl.multiple_of(768 * chunk, 768), 768)

    hidden[...] = ctx_t[...].T

    def first_norm(y):
        rows = pl.ds(pl.multiple_of(192 * y, 64), 192)
        values = dot(hidden[rows, :], output_weight[...]) + frames[rows, :].astype(F32) + vector(vectors, VEC_OUTPUT)
        unit, scale = normalise(values)
        normed[rows, :] = unit
        scales[rows, :] = jnp.broadcast_to(scale, (192, 128))
        hidden[rows, :] = (unit * vector(vectors, VEC_GAIN1) + vector(vectors, VEC_SHIFT1)).astype(BF16)

    unpack(first_norm)

    def panel(kind, number, block=None):
        start = (kind * 12 + number) * 768
        if block is None:
            return panels.at[pl.ds(pl.multiple_of(start, 256), 768), :]
        return panels.at[pl.ds(pl.multiple_of(start + 256 * block, 256), 256), :]

    def load(kind, first, count, block=None):
        return jnp.concatenate([panel(kind, first + i, block)[...] for i in range(count)], axis=1)

    def save(kind, first, count, block, values):
        for i in range(count):
            panel(kind, first + i, block)[...] = values[:, 256 * i : 256 * (i + 1)].astype(BF16)

    def narrow_columns(chunk):
        return pl.ds(pl.multiple_of(512 * chunk, 512), 512)

    def expand_stage(chunk, slot):
        raw[slot] = dot(hidden[...], expand[:, narrow_columns(chunk)])

    def gelu_stage(chunk, slot):
        bias = vectors[0:1, pl.ds(pl.multiple_of(768 * VEC_EXPAND + 512 * chunk, 512), 512)]
        for block in range(3):
            rows = rows_of(block)
            value, derivative = gelu_pair(raw[slot, rows] + bias)
            save(0, 2 * chunk, 2, block, value)
            save(1, 2 * chunk, 2, block, derivative)

    def shrink_stage(chunk, first=False):
        columns = narrow_columns(chunk)
        for block in range(3):
            rows = rows_of(block)
            product = dot(load(0, 2 * chunk, 2, block), shrink[columns, :])
            acc[rows, :] = product if first else acc[rows, :] + product

    expand_stage(0, 0)
    expand_stage(1, 1)
    gelu_stage(0, 0)

    def chunks(number, carry):
        for inner in (1, 2):
            chunk = 2 * number + inner
            expand_stage(chunk + 1, 1 - inner % 2)
            gelu_stage(chunk, inner % 2)
            shrink_stage(chunk - 1, chunk == 1)
        return carry

    for number in range(2):
        chunks(number, 0)
    gelu_stage(5, 1)
    shrink_stage(4)
    shrink_stage(5)

    sums = [jnp.zeros((1, 768), F32) for _ in range(3)]
    for block in range(3):
        rows = rows_of(block)
        first = normed[rows, :] * vector(vectors, VEC_GAIN1) + vector(vectors, VEC_SHIFT1)
        unit, scale = normalise(first + acc[rows, :] + vector(vectors, VEC_SHRINK))
        result = unit * vector(vectors, VEC_GAIN2) + vector(vectors, VEC_SHIFT2)
        live = live_mask(lengths_ref, skip_ref, (256, 1), 256 * block)
        frames[rows, :] = jnp.where(live, result, frames[rows, :].astype(F32)).astype(BF16)
        cotangent = jnp.where(live, upstream[rows, :].astype(F32), 0.0)
        grad = norm_back(cotangent, vector(vectors, VEC_GAIN2), unit, scale)
        acc[rows, :] = grad
        summed_grad[rows, :] = grad.astype(BF16)
        sums[0] = sums[0] + jnp.sum(cotangent * unit, axis=0, keepdims=True)
        sums[1] = sums[1] + jnp.sum(cotangent, axis=0, keepdims=True)
        sums[2] = sums[2] + jnp.sum(grad, axis=0, keepdims=True)

    saves[2].start()

    def put(number, value):
        vector_out[0:1, 768 * number : 768 * (number + 1)] = value

    put(VEC_QUERY, jnp.zeros((1, 768), F32))
    put(VEC_VALUE, jnp.zeros((1, 768), F32))
    put(VEC_GAIN2, sums[0])
    put(VEC_SHIFT2, sums[1])
    put(VEC_SHRINK, sums[2])

    def shrink_back(chunk, carry):
        columns = wide_columns(chunk)
        total = jnp.zeros((1, 768), F32)
        for block in range(3):
            rows = rows_of(block)
            grad = dot(summed_grad[rows, :], shrink[columns, :], 1, 1) * load(1, 3 * chunk, 3, block).astype(F32)
            total = total + jnp.sum(grad, axis=0, keepdims=True)
            save(1, 3 * chunk, 3, block, grad)
        vector_out[0:1, pl.ds(pl.multiple_of(768 * (VEC_EXPAND + chunk), 768), 768)] = total
        for block in range(3):
            part = pl.ds(pl.multiple_of(768 * chunk + 256 * block, 256), 256)
            shrink[part, :] = dot(panel(0, 3 * chunk + block)[...], summed_grad[...], 0, 0).astype(BF16)
        return carry

    for chunk in range(4):
        shrink_back(chunk, 0)

    def expand_back(chunk, carry):
        columns = wide_columns(chunk)
        for block in range(3):
            rows = rows_of(block)
            acc[rows, :] = acc[rows, :] + dot(load(1, 3 * chunk, 3, block), expand[:, columns], 1, 1)
        for block in range(3):
            part = pl.ds(pl.multiple_of(768 * chunk + 256 * block, 256), 256)
            expand[:, part] = dot(hidden[...], panel(1, 3 * chunk + block)[...], 0, 0).astype(BF16)
        return carry

    for chunk in range(4):
        expand_back(chunk, 0)
    pack()
    feed_move.start()
    sums = [jnp.zeros((1, 768), F32) for _ in range(3)]
    for block in range(3):
        rows = rows_of(block)
        grad = acc[rows, :]
        unit = normed[rows, :]
        back = norm_back(grad, vector(vectors, VEC_GAIN1), unit, scales[rows, 0:1])
        acc[rows, :] = back
        branch_grad[rows, :] = back.astype(BF16)
        sums[0] = sums[0] + jnp.sum(grad * unit, axis=0, keepdims=True)
        sums[1] = sums[1] + jnp.sum(grad, axis=0, keepdims=True)
        sums[2] = sums[2] + jnp.sum(back, axis=0, keepdims=True)
    saves[3].start()
    saves[4].start()
    put(VEC_GAIN1, sums[0])
    put(VEC_SHIFT1, sums[1])
    put(VEC_OUTPUT, sums[2])
    hidden[...] = dot(ctx_t[...], branch_grad[...]).astype(BF16)
    move = pltpu.make_async_copy(hidden, output_out, local.at[31])
    move.start()
    feed_move.wait()
    move.wait()


def forward_call(lengths, skip, frames, upstream, *shards):
    square = shape(768, 768)
    return pl.pallas_call(
        forward_kernel,
        out_shape=(
            shape(1, VECTORS * 768, kind=F32), square, shape(768, 768, kind=F32), square, square,
            shape(96, 768, kind=F32), shape(3, 768, 768), square, square, square, square, square, shape(12, 768, 768),
            shape(PARTS * 128 * ROWS_F, LANES),
        ),
        in_specs=[SCALARS] * 2 + [ANYWHERE] * 2 + [WHOLE] * 20,
        out_specs=[WHOLE] + [ANYWHERE] * 13,
        scratch_shapes=[
            pltpu.VMEM((PARTS * 128 * ROWS_A, LANES), BF16),
            pltpu.VMEM((PARTS * 128 * ROWS_F, LANES), BF16),
            pltpu.VMEM((ROWS_ALL, 768), F32),
            pltpu.VMEM((128, 128), F32),
            pltpu.VMEM((3, 768, 768), BF16),
            pltpu.VMEM((768, 768), BF16),
            pltpu.VMEM((768, 3072), BF16),
            pltpu.VMEM((3072, 768), BF16),
            pltpu.VMEM((1, VECTORS * 768), F32),
        ]
        + [pltpu.VMEM((768, 768), kind) for kind in (BF16, BF16, F32, BF16, BF16)]
        + [pltpu.VMEM((96, 768), F32), pltpu.VMEM((2, 256, 768), BF16), pltpu.VMEM((768, 128), BF16)]
        + [pltpu.SemaphoreType.DMA((PARTS, 22))] * 4
        + [pltpu.SemaphoreType.DMA((39,))],
        compiler_params=pltpu.CompilerParams(collective_id=0, has_side_effects=True, vmem_limit_bytes=62 * 2**20),
        name="forward",
    )(
        lengths, skip, frames, upstream, *shards,
        jnp.asarray(attention_rows(), BF16), jnp.asarray(expand_rows(), BF16), jnp.asarray(shrink_rows(), BF16),
        jnp.asarray(expand_rows().T, BF16), jnp.asarray(shrink_rows().T, BF16),
    )


class Scatter:
    def __init__(self, place, own, outgoing, other, far, near, second, first, rows, send, recv):
        self.place, self.own, self.outgoing, self.other = place, own, outgoing, other
        self.rows, self.send, self.recv = rows, send, recv
        self.buffers = (far, near, second, first)

    def mine(self, part):
        return tuple(self.place.along(part, stage) for stage in (2, 1, 0))

    def rows_of(self, ref, start, count):
        return rows_at(ref, start * self.rows, count * self.rows)

    def view(self, part, third, second=0, first=0, count=1, ref=None):
        return self.rows_of(self.own if ref is None else ref, ((part * 4 + third) * 4 + second) * 4 + first, count)

    def across(self, part, third, second=0, count=16):
        return self.view(part, third, second, 0, count, self.other)

    def landing(self, kind, part, slot):
        slots, count = ((2, 8), (2, 16), (3, 4), (3, 1))[kind]
        return self.rows_of(self.buffers[kind], (part * slots + slot) * count, count)

    def start(self, part, number, source, target, device):
        remote(source, target, self.send.at[part, number], self.recv.at[part, number], device).start()

    def arrived(self, part, number, view):
        remote(view, view, self.send.at[part, number], self.recv.at[part, number], self.place.sibling()).wait_recv()

    def accumulate(self, target, sources, count):
        group = min(count, 8)
        size = group * self.rows

        def body(number, carry):
            rows = pl.ds(pl.multiple_of(number * size, size), size)
            total = target[rows, :].astype(F32)
            for source in sources:
                total = total + source[rows, :].astype(F32)
            target[rows, :] = total.astype(BF16)
            return carry

        lax.fori_loop(0, count // group, body, 0)

    def exchange(self):
        for slot, step in enumerate((2, 1, 3, 0)):
            for part in range(PARTS):
                third = self.place.along(part, 2, step)
                source = self.view(part, third, count=16, ref=self.outgoing)
                self.start(part, slot, source, self.across(part, third), self.place.sibling())

    def far_out(self):
        for part in range(PARTS):
            third = self.place.along(part, 2, 2)
            self.arrived(part, 0, self.across(part, third))
            self.accumulate(self.view(part, third, count=16), [self.across(part, third)], 16)
            for half, step in ((0, 1), (1, 3)):
                source = self.view(part, third, 2 * half, count=8)
                self.start(part, 4 + half, source, self.landing(0, part, half), self.place.peer(part, 2, step))

    def near_out(self):
        for part in range(PARTS):
            for half, step in ((0, 1), (1, 3)):
                third = self.place.along(part, 2, step)
                self.arrived(part, 1 + half, self.across(part, third))
                self.arrived(part, 4 + half, self.landing(0, part, half))
                for side in (0, 1):
                    sources = [self.across(part, third, 2 * side, 8)]
                    if side == half:
                        sources.append(self.landing(0, part, half))
                    self.accumulate(self.view(part, third, 2 * side, count=8), sources, 8)
                source = self.view(part, third, count=16)
                self.start(part, 6 + half, source, self.landing(1, part, half), self.place.peer(part, 2, step))

    def second_out(self):
        for part in range(PARTS):
            third, second, first = self.mine(part)
            self.arrived(part, 3, self.across(part, third))
            for half in (0, 1):
                self.arrived(part, 6 + half, self.landing(1, part, half))
            sources = [self.across(part, third), self.landing(1, part, 0), self.landing(1, part, 1)]
            self.accumulate(self.view(part, third, count=16), sources, 16)
            for step in (1, 3, 2):
                source = self.view(part, third, self.place.along(part, 1, step), count=4)
                target = self.landing(2, part, step - 1)
                self.start(part, 7 + step, source, target, self.place.peer(part, 1, step))

    def first_out(self):
        for part in range(PARTS):
            third, second, first = self.mine(part)
            for step in (1, 3, 2):
                self.arrived(part, 7 + step, self.landing(2, part, step - 1))
            sources = [self.landing(2, part, slot) for slot in range(3)]
            self.accumulate(self.view(part, third, second, count=4), sources, 4)
            for step in (1, 3, 2):
                source = self.view(part, third, second, self.place.along(part, 0, step))
                target = self.landing(3, part, step - 1)
                self.start(part, 10 + step, source, target, self.place.peer(part, 0, step))

    def total(self, out, place):
        for part in range(PARTS):
            third, second, first = self.mine(part)
            for step in (1, 3, 2):
                self.arrived(part, 10 + step, self.landing(3, part, step - 1))
            value = self.view(part, third, second, first)[...].astype(F32)
            for slot in range(3):
                value = value + self.landing(3, part, slot)[...].astype(F32)
            out[place : place + self.rows, LANES * part : LANES * (part + 1)] = value

    def sent(self):
        for part in range(PARTS):
            for number in range(14):
                count = 16 if number < 4 else 8 if number < 6 else 16 if number < 8 else 4 if number < 11 else 1
                view = self.view(part, 0, count=count)
                remote(view, view, self.send.at[part, number], self.recv.at[part, number], self.place.sibling()).wait_send()


def pack_attention(early, grads, spread, back_a_ref, core, ref):
    for number in range(8):
        dp = number * 2 + core
        rows = pl.ds(pl.multiple_of(dp * 48, 16), 48)
        for part in range(PARTS):
            columns = slice(LANES * part, LANES * (part + 1))
            pieces = [grad[rows, columns] for grad in grads]
            if part == 0:
                tail = spread[pl.ds(pl.multiple_of(dp * 8, 8), 8), :]
                tail = jnp.concatenate([tail, jnp.zeros((8, 128), F32)], axis=0)
                tail = jnp.concatenate([tail, jnp.zeros((16, 128), F32)], axis=1)
            else:
                tail = jnp.zeros((16, LANES), F32)
            blocks = dot(back_a_ref[...], jnp.concatenate(pieces + [tail.astype(BF16)], axis=0)).astype(BF16)
            for device, index in enumerate(chunk_blocks(part, number // 4, number % 4, 0)):
                target = early.view(part, *index[2:], ref=ref)
                target[...] = blocks[ROWS_A * device : ROWS_A * (device + 1)]


def pack_vectors(vectors, numbers):
    packed = jnp.zeros((128, 128), F32)
    for number in numbers:
        wide = 6 if number < 8 else 24
        mask = owner_mask(0 if number < 8 else 768 * (number - 8), wide)
        whole = jnp.where(mask, vectors[number], 0.0).astype(BF16)
        packed = packed + dot(whole, vector_lanes(number), 1, 1)
    return packed


def backward_kernel(
    lengths_ref, skip_ref, inverse, vector_in, back_a_ref,
    frames_in, upstream_in, q_in, k_in, v_in, ctx_in, probs_in, branch_in, residual_in, attend_in, output_in, output_grad_in,
    feed_in,
    summed, frames_grad,
    own_f, own_a, outgoing_a, other_a, other_f, far_f, near_f, second_f, first_f, far_a, near_a, second_a, first_a,
    attend, output_weight, q_n, k_t, v_n, ctx_t, frames, branch, scaled_t, dk_n, dq_t, dv_t, score_grad, probs,
    ctx_grad, right, ones_mask, spread,
    send_a, recv_a, send_f, recv_f, local,
):
    place = Place()
    core = place.at[3]
    greet(place)
    pairs = (
        (output_in, output_weight), (branch_in, branch), (v_in, v_n), (ctx_in, ctx_t), (k_in, k_t), (q_in, q_n),
        (feed_in.at[pl.ds(pl.multiple_of(core * HALF_F, 16), HALF_F), :], own_f), (frames_in, frames), (attend_in, attend),
    )
    loads = [pltpu.make_async_copy(source, target, local.at[i]) for i, (source, target) in enumerate(pairs)]
    later = [
        pltpu.make_async_copy(output_grad_in, output_weight, local.at[9]),
        pltpu.make_async_copy(upstream_in, branch, local.at[10]),
        pltpu.make_async_copy(residual_in, ctx_grad, local.at[11]),
        pltpu.make_async_copy(scaled_t, frames_grad, local.at[12]),
    ]

    def prob_load(head, slot):
        return pltpu.make_async_copy(probs_in.at[head], probs.at[slot], local.at[13 + slot])

    for item in loads[:4]:
        item.start()
    prob_load(0, 0).start()
    for item in loads[4:6]:
        item.start()
    prob_load(1, 1).start()
    prob_load(2, 2).start()
    for item in loads[6:]:
        item.start()
    outgoing = feed_in.at[pl.ds(pl.multiple_of((1 - core) * HALF_F, 16), HALF_F), :]
    late = Scatter(place, own_f, outgoing, other_f, far_f, near_f, second_f, first_f, ROWS_F, send_f, recv_f)
    early = Scatter(
        place, own_a, outgoing_a, other_a,
        far_a, near_a, second_a, first_a, ROWS_A, send_a, recv_a,
    )
    lane = lax.broadcasted_iota(jnp.int32, (768, 128), 1)
    ones_mask[...] = jnp.where(lane < 2, 1.0, 0.0).astype(BF16)
    for side in range(2):
        right[side] = jnp.zeros((256, 768), BF16)
    meet()
    late.exchange()
    spread[...] = pack_vectors([vector(vector_in, i) for i in range(VECTORS)], range(2, VECTORS))
    loads[0].wait()
    loads[1].wait()
    ctx_grad[...] = dot(output_weight[...], branch[...], 1, 1)
    later[0].start()
    later[1].start()
    for item in loads[2:4]:
        item.wait()
    prob_load(0, 0).wait()

    def score_stage(pair, side):
        head = pair * 2 + side
        rows = head_rows(head)
        factor = inverse[pl.ds(pl.multiple_of(head * 8, 8), 8), :][0:1]
        scaled = (ctx_grad[rows, :] * factor).astype(BF16)
        scaled_t[rows, :] = scaled
        right[side, 64 * side : 64 * side + 64] = scaled
        inner = jnp.sum(scaled.astype(F32) * ctx_t[rows, :].astype(F32), axis=0, keepdims=True)
        high = inner.astype(BF16).astype(F32)
        row = lax.broadcasted_iota(jnp.int32, (16, 768), 0)
        right[side, 128:144] = jnp.where(row == 0, -high, jnp.where(row == 1, high - inner, 0.0)).astype(BF16)
        left = jnp.concatenate([v_n[:, pair_lanes(pair)], ones_mask[...]], axis=1)
        score_grad[side] = (dot(left, right[side]) * probs[lax.rem(head, 3)].astype(F32)).astype(BF16)

    def use_stage(pair, side):
        head = pair * 2 + side
        rows = head_rows(head)
        lanes = pair_lanes(pair)
        dv_t[rows, :] = dot(scaled_t[rows, :], probs[lax.rem(head, 3)], 1, 1).astype(BF16)
        dq_t[rows, :] = (dot(k_t[rows, :], score_grad[side]) * SCALE).astype(BF16)
        keys = (dot(score_grad[side], q_n[:, lanes]) * LN2).astype(BF16)
        if side == 1:
            keys = jnp.where(lax.broadcasted_iota(jnp.int32, (768, 128), 1) < 64, dk_n[:, lanes], keys)
        dk_n[:, lanes] = keys

    def refill(head):
        @pl.when(head + 3 < 12)
        def _():
            prob_load(head + 3, lax.rem(head, 3)).start()

        @pl.when(head + 2 < 12)
        def _():
            prob_load(head + 2, lax.rem(head + 2, 3)).wait()

    score_stage(0, 0)
    for item in loads[4:6]:
        item.wait()
    prob_load(1, 1).wait()
    loads[6].wait()
    steps = (None, late.far_out, late.near_out, None, None, late.second_out)

    def body(pair, carry):
        for number, step in enumerate(steps):
            if step is not None:
                pl.when(pair == number)(step)
        score_stage(pair, 1)
        use_stage(pair, 0)
        refill(pair * 2)
        score_stage(jnp.minimum(pair + 1, 5), 0)
        use_stage(pair, 1)
        refill(pair * 2 + 1)
        return carry

    lax.fori_loop(0, 6, body, 0)
    later[2].start()
    loads[7].wait()
    loads[8].wait()
    x = frames[...]
    queries, values = score_grad.at[0], score_grad.at[1]
    queries[...] = dq_t[...].T
    values[...] = dv_t[...].T
    grads = (k_t, q_n, v_n, output_weight)
    k_t[...] = dot(x, queries[...], 0, 0).astype(BF16)
    q_n[...] = dot(x, dk_n[...], 0, 0).astype(BF16)
    v_n[...] = dot(x, values[...], 0, 0).astype(BF16)
    sums = [jnp.sum(ref[...].astype(F32), axis=0, keepdims=True) for ref in (queries, values)]
    spread[...] = spread[...] + pack_vectors(sums, range(2))
    later[0].wait()
    late.first_out()
    pack_attention(early, grads, spread, back_a_ref, 1 - core, outgoing_a)
    early.exchange()
    pack_attention(early, grads, spread, back_a_ref, core, own_a)
    later[1].wait()
    later[2].wait()

    def finish_rows(block):
        rows = slice(256 * block, 256 * (block + 1))
        live = live_mask(lengths_ref, skip_ref, (256, 1), 256 * block)
        total = ctx_grad[rows, :] + dot(queries[rows, :], attend[0], 1, 1) + dot(dk_n[rows, :], attend[1], 1, 1)
        total = total + dot(values[rows, :], attend[2], 1, 1)
        scaled_t[rows, :] = jnp.where(live, total, branch[rows, :].astype(F32)).astype(BF16)

    early.far_out()
    finish_rows(0)
    early.near_out()
    finish_rows(1)
    finish_rows(2)
    later[3].start()
    late.total(summed, ROWS_A)
    late.sent()
    early.second_out()
    early.first_out()
    early.total(summed, 0)
    later[3].wait()
    early.sent()


def backward_call(*args):
    square = pltpu.VMEM((768, 768), BF16)

    def blocks(count, rows):
        return pltpu.VMEM((PARTS * count * rows, LANES), BF16)

    return pl.pallas_call(
        backward_kernel,
        out_shape=(shape(ROWS_ALL, 768, kind=F32), shape(768, 768)),
        in_specs=[SCALARS] * 2 + [WHOLE] * 3 + [ANYWHERE] * 13,
        out_specs=[WHOLE, ANYWHERE],
        scratch_shapes=[blocks(64, ROWS_F)] + [blocks(64, ROWS_A)] * 3 + [blocks(64, ROWS_F)]
        + [blocks(count, ROWS_F) for count in (16, 32, 12, 3)]
        + [blocks(count, ROWS_A) for count in (16, 32, 12, 3)]
        + [pltpu.VMEM((3, 768, 768), BF16)]
        + [square] * 11
        + [
            pltpu.VMEM((2, 768, 768), BF16), pltpu.VMEM((3, 768, 768), BF16), pltpu.VMEM((768, 768), F32),
            pltpu.VMEM((2, 256, 768), BF16), pltpu.VMEM((768, 128), BF16), pltpu.VMEM((128, 128), F32),
        ]
        + [pltpu.SemaphoreType.DMA((PARTS, 14))] * 4
        + [pltpu.SemaphoreType.DMA((16,))],
        compiler_params=pltpu.CompilerParams(collective_id=1, has_side_effects=True, vmem_limit_bytes=62 * 2**20),
        name="backward",
    )(*args)


def deliver_kernel(summed, encoded_in, frames_in, encoded_out, frames_out, *rest):
    query_out, key_out, value_out, output_out, expand_out, shrink_out, *vectors = rest
    encoded_out[...] = encoded_in[...]
    frames_out[...] = frames_in[...]
    for number, target in enumerate((query_out, key_out, value_out, output_out)):
        target[...] = summed[6 * number : 6 * number + 6, :]
    for number in range(4):
        expand_out[:, 768 * number : 768 * (number + 1)] = summed[32 + 6 * number : 38 + 6 * number, :]
    shrink_out[...] = summed[56:80, :]
    for at, target in zip(PLACES, vectors, strict=True):
        target[...] = summed[24, at : at + target.shape[0]]


def deliver(summed, encoded, frames_grad):
    sizes = ((6, 768),) * 4 + ((6, 3072), (24, 768)) + ((6,),) * 8 + ((24,),)
    return pl.pallas_call(
        deliver_kernel,
        out_shape=(shape(768, 768), shape(768, 768)) + tuple(shape(*s, kind=F32) for s in sizes),
        in_specs=[WHOLE] * 3,
        out_specs=[WHOLE] * 17,
        name="deliver",
    )(summed, encoded, frames_grad)


PLACES = (0, 6, 12, 18, 24, 30, 36, 42, 48)


def local(
    frames,
    upstream,
    clip_lengths,
    clip_skip,
    query_weight,
    key_weight,
    value_weight,
    output_weight,
    query_bias,
    value_bias,
    output_bias,
    first_gain,
    first_shift,
    expand_weight,
    shrink_weight,
    expand_bias,
    shrink_bias,
    second_gain,
    second_shift,
):
    vectors = (
        query_bias, value_bias, output_bias, first_gain, first_shift, shrink_bias, second_gain, second_shift, expand_bias,
    )
    (
        vector_grad, encoded, residual_grad, branch_grad, ctx_t, inverse,
        attend, output, output_grad, q_n, k_t, v_n, probs, feed_grad,
    ) = forward_call(
        clip_lengths, clip_skip, frames, upstream,
        query_weight, key_weight, value_weight, output_weight, expand_weight, shrink_weight, *vectors,
    )
    summed, frames_grad = backward_call(
        clip_lengths, clip_skip, inverse, vector_grad,
        jnp.asarray(attention_rows().T, BF16),
        frames, upstream, q_n, k_t, v_n, ctx_t, probs, branch_grad, residual_grad, attend, output, output_grad, feed_grad,
    )
    encoded, frames_grad, query_sum, key_sum, value_sum, output_sum, expand_sum, shrink_sum, *sums = deliver(
        summed, encoded, frames_grad
    )
    return (
        encoded, frames_grad, query_sum, key_sum, value_sum, output_sum, sums[0], sums[1], sums[2], sums[3], sums[4],
        expand_sum, shrink_sum, sums[8], sums[5], sums[6], sums[7],
    )


def solution(mesh):
    return jax.shard_map(
        local,
        mesh=mesh,
        in_specs=(
            P(("dp", "fsdp"), None),
            P(("dp", "fsdp"), None),
            P(("dp", "fsdp"), None),
            P(("dp", "fsdp"), None),
            P(("dp", "fsdp"), None),
            P(("dp", "fsdp"), None),
            P(("dp", "fsdp"), None),
            P(("dp", "fsdp"), None),
            P(("dp", "fsdp")),
            P(("dp", "fsdp")),
            P(("dp", "fsdp")),
            P(("dp", "fsdp")),
            P(("dp", "fsdp")),
            P(("dp", "fsdp"), None),
            P(("dp", "fsdp"), None),
            P(("dp", "fsdp")),
            P(("dp", "fsdp")),
            P(("dp", "fsdp")),
            P(("dp", "fsdp")),
        ),
        out_specs=(
            P(("dp", "fsdp"), None),
            P(("dp", "fsdp"), None),
            P(("dp", "fsdp"), None),
            P(("dp", "fsdp"), None),
            P(("dp", "fsdp"), None),
            P(("dp", "fsdp"), None),
            P(("dp", "fsdp")),
            P(("dp", "fsdp")),
            P(("dp", "fsdp")),
            P(("dp", "fsdp")),
            P(("dp", "fsdp")),
            P(("dp", "fsdp"), None),
            P(("dp", "fsdp"), None),
            P(("dp", "fsdp")),
            P(("dp", "fsdp")),
            P(("dp", "fsdp")),
            P(("dp", "fsdp")),
        ),
        check_vma=False,
    )
```
